128 devices in a mesh: pipe: 8 (over y, z_hi), dp: 16 (over x, z_lo, core).
Axes of the slice: x: 4, y: 4, z: 4 (z_hi: 2, z_lo: 2; z = z_hi * 2 + z_lo), core: 2. Of those that a mesh axis runs over, the one named last changes fastest.
Arguments:
- inputs_x: bfloat16 [4096, 5120], P('dp'), may hold values from -6 to 6
- cotangent: bfloat16 [4096, 5120], P('dp'), may hold values from -6 to 6
- master_in: float32 [8, 5120, 512], P('pipe', 'dp'), may hold values from -0.078125 to 0.078125
- master_out: float32 [8, 512, 5120], P('pipe', 'dp'), may hold values from -0.25 to 0.25
- moment_in: float32 [8, 5120, 512], P('pipe', 'dp'), may hold values from -60 to 60
- moment_out: float32 [8, 512, 5120], P('pipe', 'dp'), may hold values from -60 to 60
- second_in: float32 [8, 5120, 512], P('pipe', 'dp'), may hold values from 1 to 16
- second_out: float32 [8, 512, 5120], P('pipe', 'dp'), may hold values from 1 to 16
Outputs:
- input_grads: bfloat16 [8, 4096, 5120], P('pipe', 'dp')
- new_master_in: float32 [8, 5120, 512], P('pipe', 'dp')
- new_moment_in: float32 [8, 5120, 512], P('pipe', 'dp')
- new_second_in: float32 [8, 5120, 512], P('pipe', 'dp')
- new_master_out: float32 [8, 512, 5120], P('pipe', 'dp')
- new_moment_out: float32 [8, 512, 5120], P('pipe', 'dp')
- new_second_out: float32 [8, 512, 5120], P('pipe', 'dp')
- rollout_in: bfloat16 [8, 512, 5120], P('pipe', 'dp')
- rollout_out: bfloat16 [8, 5120, 512], P('pipe', 'dp')
The draws below stay inside these ranges and needn't reach their ends.
All inputs are finite; a program needn't handle non-finite values.
Results may differ from the reference program's by a relative error of at most 0.035.
Values may be sent and summed in bfloat16 or wider, within the bound.
No kernel may reach another device: no remote copies, remote signals or barrier semaphores. Data moves between devices by JAX's collectives and lax.ppermute only.
A program may use at most 128 MiB of HBM per device.

```python
import math
import jax
import jax.numpy as jnp
from jax import lax

D = 5120
R = 512
TOK_DEV = 256
TOKENS = 4096
SECTIONS = 8
N_DP = 16


def strengthened(drawn, rng, source, target, parts, factor):
    def block_of(dim):
        return (jnp.arange(drawn.shape[dim]) // (drawn.shape[dim] // parts)).reshape((-1,) + (1,) * (drawn.ndim - 1 - dim))

    first = jax.random.permutation(rng, parts)[block_of(target)]
    second = (block_of(target) + parts // 2) % parts
    return jnp.where((block_of(source) == first) | (block_of(source) == second), factor * drawn, drawn)


def block_scale(rng, shape, split, low, largest):
    loudness = 1.0
    for axis_at, parts in split:
        heights = jax.random.uniform(jax.random.fold_in(jax.random.fold_in(rng, 6), axis_at), (parts,), jnp.float32, low / len(split), largest / len(split))
        loudness = loudness * jnp.repeat(jnp.exp(heights), shape[axis_at] // parts).reshape((-1,) + (1,) * (len(shape) - 1 - axis_at))
    return loudness


def scatter_about(own_key, extent, scale, reach, cuts=(), kind=jnp.bfloat16):
    drawn = jax.random.normal(own_key, extent, jnp.float32) * scale
    if len(cuts) > 0:
        drawn = block_scale(own_key, extent, cuts, -0.22, 0.18) * drawn
    return jnp.clip(drawn, min=-reach, max=reach).astype(kind)


def noise_with(stream_key, extent, deviation, reach, shards, heavy, dtype=jnp.bfloat16):
    entries = deviation * jax.random.normal(stream_key, extent, jnp.float32)
    if shards:
        entries = entries * block_scale(stream_key, extent, shards, -0.22, 0.18)
    return jnp.clip(strengthened(entries, jax.random.fold_in(stream_key, 3), *heavy), -reach, reach).astype(dtype)


def setup_inputs(seed: int = 0) -> dict:
    splits = jax.random.split(jax.random.key(seed), 9)
    return {
        "inputs_x": noise_with(splits[0], (TOKENS, D), 1.0, 6.0, ((0, 16),), (0, 1, 16, 2.0)),
        "cotangent": scatter_about(splits[1], (TOKENS, D), 1.0, 6.0, ((0, 16),)),
        "master_in": scatter_about(splits[2], (SECTIONS, D, R), D ** -0.5, 0.078125, ((0, 8), (1, 16)), jnp.float32),
        "master_out": scatter_about(splits[3], (SECTIONS, R, D), R ** -0.5, 0.25, ((0, 8), (1, 16)), jnp.float32),
        "moment_in": scatter_about(splits[4], (SECTIONS, D, R), 10.0, 60.0, ((0, 8), (1, 16)), jnp.float32),
        "moment_out": scatter_about(splits[5], (SECTIONS, R, D), 10.0, 60.0, ((0, 8), (1, 16)), jnp.float32),
        "second_in": jnp.clip(jnp.exp(math.log(16.0) - 2.7725887 * jax.random.uniform(splits[6], (SECTIONS, D, R), jnp.float32) ** block_scale(splits[6], (SECTIONS, D, R), ((0, 8), (1, 16)), -0.2, 0.2)), 1.0, 16.0),
        "second_out": jnp.clip(jnp.exp(math.log(16.0) - 2.7725887 * jax.random.uniform(splits[7], (SECTIONS, R, D), jnp.float32) ** block_scale(splits[7], (SECTIONS, R, D), ((0, 8), (1, 16)), -0.2, 0.2)), 1.0, 16.0),
    }


norm_eps = 1e-06
beta_one = 0.9
beta_two = 0.999
learn_rate = 0.02
decay_rate = 0.1
adam_eps = 1e-08
adam_step = 100

def normalize(values):
    return values * lax.rsqrt(lax.optimization_barrier(jnp.mean(values * values, axis=-1, keepdims=True)) + norm_eps)

def section_forward(rows_in, weight_in, weight_out):
    widened = rows_in.astype(jnp.float32)
    normed = normalize(widened).astype(jnp.bfloat16)
    hidden = jnp.dot(normed, weight_in, preferred_element_type=jnp.float32)
    activated = jax.nn.silu(hidden).astype(jnp.bfloat16)
    return (widened + jnp.dot(activated, weight_out, preferred_element_type=jnp.float32)).astype(jnp.bfloat16)

def section_backward(rows_in, upstream, weight_in, weight_out):
    widened = rows_in.astype(jnp.float32)
    scale_inv = lax.rsqrt(lax.optimization_barrier(jnp.mean(widened * widened, axis=-1, keepdims=True)) + norm_eps)
    normed_full = widened * scale_inv
    normed = normed_full.astype(jnp.bfloat16)
    hidden = jnp.dot(normed, weight_in, preferred_element_type=jnp.float32)
    activated = jax.nn.silu(hidden).astype(jnp.bfloat16)
    grad_act = jnp.dot(upstream, weight_out.T, preferred_element_type=jnp.float32)
    sigmoid_h = jax.nn.sigmoid(hidden)
    grad_hidden = (grad_act * sigmoid_h * (1.0 + hidden * (1.0 - sigmoid_h))).astype(jnp.bfloat16)
    grad_normed = jnp.dot(grad_hidden, weight_in.T, preferred_element_type=jnp.float32)
    inner = lax.optimization_barrier(jnp.mean(grad_normed * normed_full, axis=-1, keepdims=True))
    grad_rows = upstream.astype(jnp.float32) + scale_inv * (grad_normed - normed_full * inner)
    return (grad_rows.astype(jnp.bfloat16), normed, grad_hidden, activated)

def block_total(left, right):
    left_blocks = left.reshape(N_DP, TOK_DEV, left.shape[1])
    right_blocks = right.reshape(N_DP, TOK_DEV, right.shape[1])

    def add_block(total, pair):
        part = jnp.dot(pair[0].T, pair[1], preferred_element_type=jnp.float32)
        part = lax.optimization_barrier(part.astype(jnp.bfloat16)).astype(jnp.float32)
        return (total + part, None)
    start = jnp.zeros((left.shape[1], right.shape[1]), jnp.float32)
    total, unused = lax.scan(add_block, start, (left_blocks, right_blocks))
    return total

def adam_update(master, moment, second, grad):
    moment_new = beta_one * moment + (1.0 - beta_one) * grad
    second_new = beta_two * second + (1.0 - beta_two) * grad * grad
    moment_hat = moment_new / (1.0 - beta_one ** adam_step)
    second_hat = second_new / (1.0 - beta_two ** adam_step)
    master_new = master - learn_rate * (moment_hat / (jnp.sqrt(second_hat) + adam_eps) + decay_rate * master)
    return (master_new, moment_new, second_new)

def reference(inputs_x, cotangent, master_in, master_out, moment_in, moment_out, second_in, second_out):
    weight_in = master_in.astype(jnp.bfloat16)
    weight_out = master_out.astype(jnp.bfloat16)
    section_inputs = [inputs_x]
    for section_number in range(SECTIONS - 1):
        section_inputs.append(section_forward(section_inputs[-1], weight_in[section_number], weight_out[section_number]))
    upstream = cotangent
    grad_list = [None] * SECTIONS
    sums_in = [None] * SECTIONS
    sums_out = [None] * SECTIONS
    for section_number in reversed(range(SECTIONS)):
        grad_rows, normed, grad_hidden, activated = section_backward(section_inputs[section_number], upstream, weight_in[section_number], weight_out[section_number])
        sums_in[section_number] = block_total(normed, grad_hidden)
        sums_out[section_number] = block_total(activated, upstream)
        grad_list[section_number] = grad_rows
        upstream = grad_rows
    grad_in = jnp.stack(sums_in)
    grad_out = jnp.stack(sums_out)
    new_in, new_moment_in, new_second_in = adam_update(master_in, moment_in, second_in, grad_in)
    new_out, new_moment_out, new_second_out = adam_update(master_out, moment_out, second_out, grad_out)
    rollout_in = jnp.swapaxes(new_in.astype(jnp.bfloat16), 1, 2)
    rollout_out = jnp.swapaxes(new_out.astype(jnp.bfloat16), 1, 2)
    return (jnp.stack(grad_list), new_in, new_moment_in, new_second_in, new_out, new_moment_out, new_second_out, rollout_in, rollout_out)
```

```python
import jax
import jax.numpy as jnp
from jax import lax
from jax.sharding import PartitionSpec as P

norm_eps = 1e-06
beta_one = 0.9
beta_two = 0.999
learn_rate = 0.02
decay_rate = 0.1
adam_eps = 1e-08
adam_step = 100

BLOCKS = ((0, 4), (4, 8))


def dot(left, right, dims):
    return lax.dot_general(left, right, (dims, ((), ())), preferred_element_type=jnp.float32)


ROWS = ((1,), (0,))
LAST = ((1,), (1,))
FIRST = ((0,), (0,))


def swap(x, axis):
    return lax.all_to_all(x, axis, 0, 0, tiled=True)


def split_scalars(scalars):
    columns = []
    for value in scalars:
        high = value.astype(jnp.bfloat16)
        columns += [high, (value - high.astype(jnp.float32)).astype(jnp.bfloat16)]
    columns.append(jnp.zeros((scalars[0].shape[0], 128 - len(columns)), jnp.bfloat16))
    return columns


def joined_scalar(packed, at):
    return packed[:, at : at + 1].astype(jnp.float32) + packed[:, at + 1 : at + 2].astype(
        jnp.float32
    )


def sum_to_owner(columns, count):
    packed = jnp.concatenate([c.astype(jnp.bfloat16) for c in columns], axis=1)
    arrived = swap(packed, "pipe").reshape(count, packed.shape[0] // count, packed.shape[1])
    return jnp.sum(arrived.astype(jnp.float32), axis=0)


def gather_rows(columns, count):
    packed = jnp.concatenate(columns, axis=1)
    return swap(jnp.tile(packed, (count, 1)), "pipe")


def adam_update(master, moment, second, grad):
    moment_new = beta_one * moment + (1.0 - beta_one) * grad
    second_new = beta_two * second + (1.0 - beta_two) * grad * grad
    moment_hat = moment_new / (1.0 - beta_one**adam_step)
    second_hat = second_new / (1.0 - beta_two**adam_step)
    master_new = master - learn_rate * (
        moment_hat / (jnp.sqrt(second_hat) + adam_eps) + decay_rate * master
    )
    return (master_new, moment_new, second_new)


def reduce_grads(parts_in, parts_out, n_dp):
    group = len(parts_in)
    chunk, inner = parts_in[0].shape
    rows = group * chunk // n_dp
    share = inner // n_dp
    stacked_in = jnp.concatenate(parts_in, axis=0).reshape(n_dp, rows, inner)
    stacked_out = jnp.stack(parts_out, axis=1).reshape(n_dp, share, group, chunk)
    stacked_out = stacked_out.reshape(n_dp, rows, inner)
    both = jnp.concatenate([stacked_in, stacked_out], axis=1).reshape(n_dp * 2 * rows, inner)
    summed = lax.psum_scatter(both, "dp", scatter_dimension=0, tiled=True)
    return summed[:rows], summed[rows:].reshape(share, group, chunk)


def move_in(summed, first, group, n_pipe, n_dp):
    per = n_pipe // group
    moved = []
    for q in range(per):
        pairs = []
        for i in range(n_pipe):
            for j in range(q, n_dp, per):
                section = j * group // n_dp
                half = j // per % 2
                pairs.append((i * n_dp + j, (first + section) * n_dp + 2 * i + half))
        moved.append(lax.ppermute(summed, ("pipe", "dp"), pairs))
    return jnp.concatenate(moved, axis=0)


def gram_units(first, last):
    units = []
    for j in range(first, last - 1):
        units += [(j, k, False) for k in range(j, last - 1)]
        units += [(j, s, True) for s in range(j + 1, last)]
    return units


def on_device(
    inputs_x, cotangent, master_in, master_out, moment_in, moment_out, second_in, second_out
):
    n_pipe = lax.axis_size("pipe")
    n_dp = lax.axis_size("dp")
    me = lax.axis_index("pipe")
    tok_rows, width = inputs_x.shape
    chunk = width // n_pipe
    inner = master_in.shape[2]
    share_in = master_in.shape[1]
    share_out = master_out.shape[1]

    own_in = master_in[0].astype(jnp.bfloat16)
    own_out = master_out[0].astype(jnp.bfloat16)
    pairs = [
        (s * n_dp + 2 * i + h, i * n_dp + 2 * s + h)
        for s in range(n_pipe)
        for i in range(n_pipe)
        for h in range(2)
    ]
    piece_in = lax.ppermute(own_in, ("pipe", "dp"), pairs)
    piece_out = swap(own_out.reshape(share_out, n_pipe, chunk).transpose(1, 0, 2), "pipe")
    flat_out = piece_out.transpose(1, 0, 2).reshape(share_out, width)
    all_in = lax.all_gather(piece_in, "dp", axis=0, tiled=True)
    all_out = lax.all_gather(flat_out, "dp", axis=0, tiled=True)
    weight_in = [all_in[s * chunk : (s + 1) * chunk] for s in range(n_pipe)]
    weight_out = [all_out[:, s * chunk : (s + 1) * chunk] for s in range(n_pipe)]

    units = [unit for first, last in BLOCKS for unit in gram_units(first, last)]
    padded = -(-len(units) // n_pipe) * n_pipe
    partial = []
    for j, other, down in units:
        if down:
            partial.append(dot(piece_out[j], weight_in[other], ROWS))
        else:
            partial.append(dot(piece_out[j], weight_out[other], LAST))
    partial += [jnp.zeros_like(partial[0])] * (padded - len(units))
    arrived = swap(jnp.stack(partial).astype(jnp.bfloat16), "pipe")
    arrived = arrived.reshape(n_pipe, padded // n_pipe, share_out, inner)
    mine = jnp.sum(arrived.astype(jnp.float32), axis=0).astype(jnp.bfloat16)
    rows_of = swap(jnp.tile(mine, (n_pipe, 1, 1)), "pipe")
    rows_of = rows_of.transpose(1, 0, 2).reshape(share_out, padded * inner)
    gram_all = lax.all_gather(rows_of, "dp", axis=0, tiled=True)
    gram = {
        unit: gram_all[:, at * inner : (at + 1) * inner] for at, unit in enumerate(units)
    }

    rows = lax.dynamic_slice_in_dim(inputs_x, me * chunk, chunk, 1)
    exact = rows.astype(jnp.float32)
    seed = lax.dynamic_slice_in_dim(cotangent, me * chunk, chunk, 1)

    def grad_start(upstream, first, last):
        sums = sum_to_owner(
            [dot(upstream, weight_out[s], LAST) for s in range(first, last)], n_pipe
        )
        return {
            s: sums[:, (s - first) * inner : (s - first + 1) * inner] for s in range(first, last)
        }

    grad_act = grad_start(seed, *BLOCKS[-1])
    saved_rows, saved_act, state = {}, {}, {}

    def forward_block(first, last):
        count = last - first
        columns = [dot(rows, weight_in[s], ROWS) for s in range(first, last)]
        columns += [dot(rows, weight_out[s], LAST) for s in range(first, last - 1)]
        columns += split_scalars([jnp.sum(exact * exact, axis=1, keepdims=True)])
        sums = sum_to_owner(columns, n_pipe)
        raw = {s: sums[:, (s - first) * inner : (s - first + 1) * inner] for s in range(first, last)}
        cross = {
            s: sums[:, (count + s - first) * inner : (count + s - first + 1) * inner]
            for s in range(first, last - 1)
        }
        at = (2 * count - 1) * inner
        square = sums[:, at : at + 1] + sums[:, at + 1 : at + 2]
        for s in range(first, last):
            scale = lax.rsqrt(jnp.maximum(square, 0.0) / width + norm_eps)
            hidden = raw[s] * scale
            gate = jax.nn.sigmoid(hidden)
            act = (hidden * gate).astype(jnp.bfloat16)
            seen = {}
            if s < last - 1:
                added = {}
                for k in range(first, last - 1):
                    if k >= s:
                        added[k] = dot(act, gram[(s, k, False)], ROWS)
                    else:
                        added[k] = dot(act, gram[(k, s, False)], LAST)
                wide = act.astype(jnp.float32)
                square = square + jnp.sum(
                    wide * (2.0 * cross[s] + added[s]), axis=1, keepdims=True
                )
                for k in range(first, last - 1):
                    cross[k] = cross[k] + added[k]
                for t in range(s + 1, last):
                    raw[t] = raw[t] + dot(act, gram[(s, t, True)], ROWS)
                seen = dict(cross)
            state[s] = (hidden, gate, scale, act)
            inputs_cross[s + 1] = seen

    inputs_cross = {}

    def backward_block(first, last):
        packs, pulls = {}, {}
        for s in reversed(range(first, last)):
            hidden, gate, scale, act = state[s]
            grad_hidden = grad_act[s] * gate * (1.0 + hidden * (1.0 - gate))
            mean = jnp.sum(grad_hidden * hidden, axis=1, keepdims=True) / width
            packs[s] = (grad_hidden * scale).astype(jnp.bfloat16)
            pulls[s] = mean * scale * scale
            for t in range(first, s):
                grad_act[t] = (
                    grad_act[t]
                    + dot(packs[s], gram[(t, s, True)], LAST)
                    - pulls[s] * inputs_cross[s][t]
                )
        return packs, pulls

    upstream = seed
    upstream_exact = seed.astype(jnp.float32)
    grads = [None] * n_pipe
    reduced = {}

    def take_rows(act_all, first, last, more):
        nonlocal rows, exact
        for s in range(first, last):
            saved_rows[s] = rows
            saved_act[s] = act_all[:, (s - first) * inner : (s - first + 1) * inner]
            if s < last - 1 or more:
                exact = exact + dot(saved_act[s], weight_out[s], ROWS)
                rows = exact.astype(jnp.bfloat16)

    for first, last in BLOCKS[:-1]:
        forward_block(first, last)
        gathered = gather_rows([state[s][3] for s in range(first, last)], n_pipe)
        take_rows(gathered, first, last, True)

    for number in reversed(range(len(BLOCKS))):
        first, last = BLOCKS[number]
        count = last - first
        is_last = number == len(BLOCKS) - 1
        if is_last:
            forward_block(first, last)
        else:
            grad_act.update(grad_start(upstream, first, last))
        packs, pulls = backward_block(first, last)
        columns = [packs[s] for s in range(first, last)]
        if is_last:
            columns += [state[s][3] for s in range(first, last)]
        columns += split_scalars([pulls[s] for s in range(first, last)])
        gathered = gather_rows(columns, n_pipe)
        if is_last:
            take_rows(gathered[:, count * inner :], first, last, False)
        scalar_at = gathered.shape[1] - 128
        parts_in, parts_out = {}, {}
        for s in reversed(range(first, last)):
            pack = gathered[:, (s - first) * inner : (s - first + 1) * inner]
            pull = joined_scalar(gathered, scalar_at + 2 * (s - first))
            parts_in[s] = dot(saved_rows[s], pack, FIRST).astype(jnp.bfloat16)
            parts_out[s] = dot(saved_act[s], upstream, FIRST).astype(jnp.bfloat16)
            upstream_exact = (
                upstream_exact
                + dot(pack, weight_in[s], LAST)
                - pull * saved_rows[s].astype(jnp.float32)
            )
            upstream = upstream_exact.astype(jnp.bfloat16)
            grads[s] = upstream
        reduced[first] = reduce_grads(
            [parts_in[s] for s in range(first, last)],
            [parts_out[s] for s in range(first, last)],
            n_dp,
        )

    input_grads = swap(jnp.stack(grads), "pipe")
    input_grads = input_grads.transpose(1, 0, 2).reshape(1, tok_rows, width)

    grad_in = jnp.zeros((share_in, inner), jnp.bfloat16)
    outs = []
    for first, last in BLOCKS:
        sum_in, sum_out = reduced[first]
        moved = move_in(sum_in, first, last - first, n_pipe, n_dp)
        grad_in = jnp.where((me >= first) & (me < last), moved, grad_in)
        outs.append(sum_out.transpose(1, 0, 2))
    grad_out = swap(jnp.concatenate(outs, axis=0), "pipe")
    grad_out = grad_out.transpose(1, 0, 2).reshape(share_out, width)

    new_in, new_moment_in, new_second_in = adam_update(
        master_in[0], moment_in[0], second_in[0], grad_in.astype(jnp.float32)
    )
    new_out, new_moment_out, new_second_out = adam_update(
        master_out[0], moment_out[0], second_out[0], grad_out.astype(jnp.float32)
    )
    cast_in = new_in.astype(jnp.bfloat16).T.reshape(n_dp, share_out, share_in)
    cast_out = new_out.astype(jnp.bfloat16).reshape(share_out, n_dp, share_in).transpose(1, 0, 2)
    swapped = swap(jnp.stack([cast_in, cast_out], axis=1), "dp")
    roll_in = swapped[:, 0].transpose(1, 0, 2).reshape(share_out, width)
    roll_out = swapped[:, 1].reshape(inner, share_in).T
    return (
        input_grads,
        new_in[None],
        new_moment_in[None],
        new_second_in[None],
        new_out[None],
        new_moment_out[None],
        new_second_out[None],
        roll_in[None],
        roll_out[None],
    )


def solution(mesh):
    in_specs = (P("dp", None), P("dp", None)) + (P("pipe", "dp", None),) * 6
    out_specs = (P("pipe", "dp", None),) * 9
    return jax.shard_map(
        on_device, mesh=mesh, in_specs=in_specs, out_specs=out_specs, check_vma=False
    )
```

```python
import jax
import jax.numpy as jnp
from jax import lax
from jax.sharding import PartitionSpec as P

norm_eps = 1e-06
beta_one = 0.9
beta_two = 0.999
learn_rate = 0.02
decay_rate = 0.1
adam_eps = 1e-08
adam_step = 100

BLOCKS = ((0, 4), (4, 8))
LANES = 128


def dot(left, right, dims):
    return lax.dot_general(left, right, (dims, ((), ())), preferred_element_type=jnp.float32)


ROWS = ((1,), (0,))
LAST = ((1,), (1,))
FIRST = ((0,), (0,))


def swap(x, axis):
    return lax.all_to_all(x, axis, 0, 0, tiled=True)


def split_scalars(scalars):
    columns = []
    for value in scalars:
        high = value.astype(jnp.bfloat16)
        columns += [high, (value - high.astype(jnp.float32)).astype(jnp.bfloat16)]
    columns.append(jnp.zeros((scalars[0].shape[0], 128 - len(columns)), jnp.bfloat16))
    return columns


def joined_scalar(packed, at):
    return packed[:, at : at + 1].astype(jnp.float32) + packed[:, at + 1 : at + 2].astype(
        jnp.float32
    )


def sum_to_owner(columns, count):
    packed = jnp.concatenate([c.astype(jnp.bfloat16) for c in columns], axis=1)
    arrived = swap(packed, "pipe").reshape(count, packed.shape[0] // count, packed.shape[1])
    return jnp.sum(arrived.astype(jnp.float32), axis=0)


def gather_rows(columns, count):
    packed = jnp.concatenate(columns, axis=1)
    return swap(jnp.tile(packed, (count, 1)), "pipe")


def adam_update(master, moment, second, grad):
    moment_new = beta_one * moment + (1.0 - beta_one) * grad
    second_new = beta_two * second + (1.0 - beta_two) * grad * grad
    moment_hat = moment_new / (1.0 - beta_one**adam_step)
    second_hat = second_new / (1.0 - beta_two**adam_step)
    master_new = master - learn_rate * (
        moment_hat / (jnp.sqrt(second_hat) + adam_eps) + decay_rate * master
    )
    return (master_new, moment_new, second_new)


def reduce_grads(parts_in, parts_out, n_dp):
    chunk, inner = parts_in[0].shape
    group = len(parts_in)
    share = inner // n_dp
    stacked_in = jnp.concatenate(parts_in, axis=0).reshape(n_dp, -1, inner // LANES, LANES)
    stacked_out = jnp.concatenate(parts_out, axis=1).reshape(n_dp, share, -1, LANES)
    both = jnp.concatenate(
        [
            stacked_in.transpose(0, 2, 1, 3).reshape(n_dp, -1, LANES),
            stacked_out.transpose(0, 2, 1, 3).reshape(n_dp, -1, LANES),
        ],
        axis=1,
    )
    half = both.shape[1] // 2
    summed = lax.psum_scatter(both.reshape(-1, LANES), "dp", scatter_dimension=0, tiled=True)

    def finish(summed):
        sum_in = summed[:half].reshape(inner // LANES, -1, LANES).transpose(1, 0, 2)
        sum_out = summed[half:].reshape(group, chunk // LANES, share, LANES)
        return sum_in.reshape(-1, inner), sum_out.transpose(0, 2, 1, 3).reshape(group, share, chunk)

    return summed, finish


def move_in(summed, first, group, n_pipe, n_dp):
    per = n_pipe // group
    moved = []
    for q in range(per):
        pairs = []
        for i in range(n_pipe):
            for j in range(q, n_dp, per):
                section = j * group // n_dp
                half = j // per % 2
                pairs.append((i * n_dp + j, (first + section) * n_dp + 2 * i + half))
        moved.append(lax.ppermute(summed, ("pipe", "dp"), pairs))
    return jnp.concatenate(moved, axis=0)


def on_device(
    inputs_x, cotangent, master_in, master_out, moment_in, moment_out, second_in, second_out
):
    n_pipe = lax.axis_size("pipe")
    n_dp = lax.axis_size("dp")
    me = lax.axis_index("pipe")
    tok_rows, width = inputs_x.shape
    chunk = width // n_pipe
    inner = master_in.shape[2]
    share_in = master_in.shape[1]
    share_out = master_out.shape[1]

    own_in = master_in[0].astype(jnp.bfloat16)
    own_out = master_out[0].astype(jnp.bfloat16)
    pairs = [
        (s * n_dp + 2 * i + h, i * n_dp + 2 * s + h)
        for s in range(n_pipe)
        for i in range(n_pipe)
        for h in range(2)
    ]
    piece_in = lax.ppermute(own_in, ("pipe", "dp"), pairs)
    piece_out = swap(own_out.reshape(share_out, n_pipe, chunk).transpose(1, 0, 2), "pipe")
    flat_out = piece_out.transpose(1, 0, 2).reshape(share_out, width)
    all_in = lax.all_gather(piece_in, "dp", axis=0, tiled=True)
    all_out = lax.all_gather(flat_out, "dp", axis=0, tiled=True)
    weight_in = [all_in[s * chunk : (s + 1) * chunk] for s in range(n_pipe)]
    weight_out = [all_out[:, s * chunk : (s + 1) * chunk] for s in range(n_pipe)]

    gram = {}

    def products(first, last):
        units, partial = [], []
        for t in range(first + 1, last):
            left = piece_out[first:t].reshape(-1, chunk)
            partial.append(dot(left, weight_in[t], ROWS))
            units += [(k, t, True) for k in range(first, t)]
        for t in range(first, last - 1):
            left = piece_out[first : t + 1].reshape(-1, chunk)
            partial.append(dot(left, weight_out[t], LAST))
            units += [(k, t, False) for k in range(first, t + 1)]
        padded = -(-len(units) // n_pipe) * n_pipe
        partial = [p.astype(jnp.bfloat16) for p in partial]
        partial.append(jnp.zeros(((padded - len(units)) * share_out, inner), jnp.bfloat16))
        arrived = swap(jnp.concatenate(partial, axis=0), "pipe")
        arrived = arrived.reshape(n_pipe, -1, inner)
        mine = jnp.sum(arrived.astype(jnp.float32), axis=0).astype(jnp.bfloat16)
        every = swap(jnp.tile(mine, (n_pipe, 1)), "pipe").reshape(padded, share_out, inner)
        order = sorted(range(len(units)), key=lambda at: units[at])
        columns = jnp.concatenate([every[at] for at in order], axis=1)
        whole = lax.all_gather(columns, "dp", axis=0, tiled=True)
        return [units[at] for at in order], whole

    def unpack(units, whole):
        for at, unit in enumerate(units):
            gram[unit] = whole[:, at * inner : (at + 1) * inner]

    made = [products(first, last) for first, last in BLOCKS]

    rows = lax.dynamic_slice_in_dim(inputs_x, me * chunk, chunk, 1)
    exact = rows.astype(jnp.float32)
    seed = lax.dynamic_slice_in_dim(cotangent, me * chunk, chunk, 1)

    def grad_start(upstream, first, last, held=None):
        columns = [dot(upstream, weight_out[s], LAST) for s in range(first, last)]
        if held is not None:
            columns, held = lax.optimization_barrier((columns, held))
        sums = sum_to_owner(columns, n_pipe)
        return {
            s: sums[:, (s - first) * inner : (s - first + 1) * inner] for s in range(first, last)
        }, held

    grad_act, _ = grad_start(seed, *BLOCKS[-1])
    whole, grad_act = lax.optimization_barrier((made[0][1], grad_act))
    unpack(made[0][0], whole)
    for later, whole in made[1:]:
        unpack(later, whole)
    saved_rows, saved_act, state = {}, {}, {}

    def forward_block(first, last):
        count = last - first
        columns = [dot(rows, weight_in[s], ROWS) for s in range(first, last)]
        columns += [dot(rows, weight_out[s], LAST) for s in range(first, last - 1)]
        columns += split_scalars([jnp.sum(exact * exact, axis=1, keepdims=True)])
        sums = sum_to_owner(columns, n_pipe)
        raw = {s: sums[:, (s - first) * inner : (s - first + 1) * inner] for s in range(first, last)}
        cross = {
            s: sums[:, (count + s - first) * inner : (count + s - first + 1) * inner]
            for s in range(first, last - 1)
        }
        at = (2 * count - 1) * inner
        square = sums[:, at : at + 1] + sums[:, at + 1 : at + 2]
        for s in range(first, last):
            scale = lax.rsqrt(jnp.maximum(square, 0.0) / width + norm_eps)
            hidden = raw[s] * scale
            gate = jax.nn.sigmoid(hidden)
            act = (hidden * gate).astype(jnp.bfloat16)
            seen = {}
            if s < last - 1:
                added = {}
                for k in range(first, last - 1):
                    if k >= s:
                        added[k] = dot(act, gram[(s, k, False)], ROWS)
                    else:
                        added[k] = dot(act, gram[(k, s, False)], LAST)
                wide = act.astype(jnp.float32)
                square = square + jnp.sum(
                    wide * (2.0 * cross[s] + added[s]), axis=1, keepdims=True
                )
                for k in range(first, last - 1):
                    cross[k] = cross[k] + added[k]
                for t in range(s + 1, last):
                    raw[t] = raw[t] + dot(act, gram[(s, t, True)], ROWS)
                seen = dict(cross)
            state[s] = (hidden, gate, scale, act)
            inputs_cross[s + 1] = seen

    inputs_cross = {}

    def backward_block(first, last):
        packs, pulls = {}, {}
        for s in reversed(range(first, last)):
            hidden, gate, scale, act = state[s]
            grad_hidden = grad_act[s] * gate * (1.0 + hidden * (1.0 - gate))
            mean = jnp.sum(grad_hidden * hidden, axis=1, keepdims=True) / width
            packs[s] = (grad_hidden * scale).astype(jnp.bfloat16)
            pulls[s] = mean * scale * scale
            for t in range(first, s):
                grad_act[t] = (
                    grad_act[t]
                    + dot(packs[s], gram[(t, s, True)], LAST)
                    - pulls[s] * inputs_cross[s][t]
                )
        return packs, pulls

    upstream = seed
    upstream_exact = seed.astype(jnp.float32)
    grads = [None] * n_pipe
    reduced = {}

    def take_rows(act_all, first, last, more):
        nonlocal rows, exact
        for s in range(first, last):
            saved_rows[s] = rows
            saved_act[s] = act_all[:, (s - first) * inner : (s - first + 1) * inner]
            if s < last - 1 or more:
                exact = exact + dot(saved_act[s], weight_out[s], ROWS)
                rows = exact.astype(jnp.bfloat16)

    for first, last in BLOCKS[:-1]:
        forward_block(first, last)
        gathered = gather_rows([state[s][3] for s in range(first, last)], n_pipe)
        take_rows(gathered, first, last, True)

    for number in reversed(range(len(BLOCKS))):
        first, last = BLOCKS[number]
        count = last - first
        is_last = number == len(BLOCKS) - 1
        if is_last:
            forward_block(first, last)
            acts = gather_rows([state[s][3] for s in range(first, last)], n_pipe)
        packs, pulls = backward_block(first, last)
        columns = [packs[s] for s in range(first, last)]
        columns += split_scalars([pulls[s] for s in range(first, last)])
        gathered = gather_rows(columns, n_pipe)
        if is_last:
            take_rows(acts, first, last, False)
        scalar_at = count * inner
        parts_in, parts_out = {}, {}
        for s in reversed(range(first, last)):
            pack = gathered[:, (s - first) * inner : (s - first + 1) * inner]
            pull = joined_scalar(gathered, scalar_at + 2 * (s - first))
            parts_in[s] = dot(saved_rows[s], pack, FIRST).astype(jnp.bfloat16)
            parts_out[s] = dot(saved_act[s], upstream, FIRST).astype(jnp.bfloat16)
            upstream_exact = (
                upstream_exact
                + dot(pack, weight_in[s], LAST)
                - pull * saved_rows[s].astype(jnp.float32)
            )
            upstream = upstream_exact.astype(jnp.bfloat16)
            grads[s] = upstream
        pending = [parts_in[s] for s in range(first, last)], [
            parts_out[s] for s in range(first, last)
        ]
        if number > 0:
            following, pending = grad_start(upstream, *BLOCKS[number - 1], pending)
            grad_act.update(following)
        reduced[first] = reduce_grads(*pending, n_dp)

    input_grads = swap(jnp.stack(grads), "pipe")
    first = BLOCKS[0][0]
    input_grads, summed = lax.optimization_barrier((input_grads, reduced[first][0]))
    reduced[first] = (summed, reduced[first][1])
    input_grads = input_grads.transpose(1, 0, 2).reshape(1, tok_rows, width)

    grad_in = jnp.zeros((share_in, inner), jnp.bfloat16)
    outs = []
    for first, last in BLOCKS:
        summed, finish = reduced[first]
        sum_in, sum_out = finish(summed)
        moved = move_in(sum_in, first, last - first, n_pipe, n_dp)
        grad_in = jnp.where((me >= first) & (me < last), moved, grad_in)
        outs.append(sum_out)
    grad_out = swap(jnp.concatenate(outs, axis=0), "pipe")
    grad_out = grad_out.transpose(1, 0, 2).reshape(share_out, width)

    new_in, new_moment_in, new_second_in = adam_update(
        master_in[0], moment_in[0], second_in[0], grad_in.astype(jnp.float32)
    )
    new_out, new_moment_out, new_second_out = adam_update(
        master_out[0], moment_out[0], second_out[0], grad_out.astype(jnp.float32)
    )
    cast_in = new_in.astype(jnp.bfloat16).T.reshape(n_dp, share_out, share_in)
    cast_out = new_out.astype(jnp.bfloat16).reshape(share_out, n_dp, share_in).transpose(1, 0, 2)
    swapped = swap(jnp.stack([cast_in, cast_out], axis=1), "dp")
    roll_in = swapped[:, 0].transpose(1, 0, 2).reshape(share_out, width)
    roll_out = swapped[:, 1].reshape(inner, share_in).T
    return (
        input_grads,
        new_in[None],
        new_moment_in[None],
        new_second_in[None],
        new_out[None],
        new_moment_out[None],
        new_second_out[None],
        roll_in[None],
        roll_out[None],
    )


def solution(mesh):
    in_specs = (P("dp", None), P("dp", None)) + (P("pipe", "dp", None),) * 6
    out_specs = (P("pipe", "dp", None),) * 9
    return jax.shard_map(
        on_device, mesh=mesh, in_specs=in_specs, out_specs=out_specs, check_vma=False
    )
```

```python
import jax
import jax.numpy as jnp
from jax import lax
from jax.sharding import PartitionSpec as P

norm_eps = 1e-06
beta_one = 0.9
beta_two = 0.999
learn_rate = 0.02
decay_rate = 0.1
adam_eps = 1e-08
adam_step = 100

BLOCKS = ((0, 4), (4, 8))
LANES = 128


def dot(left, right, dims):
    return lax.dot_general(left, right, (dims, ((), ())), preferred_element_type=jnp.float32)


ROWS = ((1,), (0,))
LAST = ((1,), (1,))
FIRST = ((0,), (0,))


def swap(x, axis):
    return lax.all_to_all(x, axis, 0, 0, tiled=True)


def split_scalars(scalars):
    columns = []
    for value in scalars:
        high = value.astype(jnp.bfloat16)
        columns += [high, (value - high.astype(jnp.float32)).astype(jnp.bfloat16)]
    columns.append(jnp.zeros((scalars[0].shape[0], 128 - len(columns)), jnp.bfloat16))
    return columns


def joined_scalar(packed, at):
    return packed[:, at : at + 1].astype(jnp.float32) + packed[:, at + 1 : at + 2].astype(
        jnp.float32
    )


def sum_to_owner(columns, count):
    packed = jnp.concatenate([c.astype(jnp.bfloat16) for c in columns], axis=1)
    arrived = swap(packed, "pipe").reshape(count, packed.shape[0] // count, packed.shape[1])
    return jnp.sum(arrived.astype(jnp.float32), axis=0)


def gather_rows(columns, count):
    packed = jnp.concatenate(columns, axis=1)
    return swap(jnp.tile(packed, (count, 1)), "pipe")


def adam_update(master, moment, second, grad):
    moment_new = beta_one * moment + (1.0 - beta_one) * grad
    second_new = beta_two * second + (1.0 - beta_two) * grad * grad
    moment_hat = moment_new / (1.0 - beta_one**adam_step)
    second_hat = second_new / (1.0 - beta_two**adam_step)
    master_new = master - learn_rate * (
        moment_hat / (jnp.sqrt(second_hat) + adam_eps) + decay_rate * master
    )
    return (master_new, moment_new, second_new)


def pack_grads(parts_in, parts_out, n_dp):
    inner = parts_in[0].shape[1]
    stacked_in = jnp.concatenate(parts_in, axis=0)
    pieces = [lane_block(stacked_in, c) for c in range(inner // LANES)]
    pieces += [lane_block(p, c) for p in parts_out for c in range(p.shape[1] // LANES)]
    return jnp.concatenate([p.reshape(n_dp, -1, LANES) for p in pieces], axis=1)


def lane_block(x, at):
    return x[:, at * LANES : (at + 1) * LANES]


def unpack_grads(summed, inner, group, share):
    half = summed.shape[0] // 2
    rows = half * LANES // inner
    sum_in = [summed[c * rows : (c + 1) * rows] for c in range(inner // LANES)]
    return jnp.concatenate(sum_in, axis=1), summed[half:].reshape(group, -1, LANES)


def reduce_apart(packed):
    return lax.psum_scatter(
        packed.reshape(-1, LANES), "dp", scatter_dimension=0, tiled=True
    )


def reduce_now(packed, n_dp):
    core = lax.axis_index("dp") % 2
    paired = packed.reshape(n_dp // 2, 2, -1, LANES)
    mine = lax.dynamic_index_in_dim(paired, core, 1, keepdims=False)
    other = lax.dynamic_index_in_dim(paired, 1 - core, 1, keepdims=False)
    other = lax.ppermute(other, "dp", [(j, j + 1 - 2 * (j % 2)) for j in range(n_dp)])
    mine = (mine.astype(jnp.float32) + other.astype(jnp.float32)).astype(jnp.bfloat16)
    arrived = lax.all_to_all(
        mine,
        "dp",
        0,
        0,
        tiled=True,
        axis_index_groups=[list(range(c, n_dp, 2)) for c in range(2)],
    )
    return jnp.sum(arrived.astype(jnp.float32), axis=0).astype(jnp.bfloat16)


def move_in(summed, first, group, n_pipe, n_dp):
    per = n_pipe // group
    moved = []
    for q in range(per):
        pairs = []
        for i in range(n_pipe):
            for j in range(q, n_dp, per):
                section = j * group // n_dp
                half = j // per % 2
                pairs.append((i * n_dp + j, (first + section) * n_dp + 2 * i + half))
        moved.append(lax.ppermute(summed, ("pipe", "dp"), pairs))
    return jnp.concatenate(moved, axis=0)


def on_device(
    inputs_x, cotangent, master_in, master_out, moment_in, moment_out, second_in, second_out
):
    n_pipe = lax.axis_size("pipe")
    n_dp = lax.axis_size("dp")
    me = lax.axis_index("pipe")
    tok_rows, width = inputs_x.shape
    chunk = width // n_pipe
    inner = master_in.shape[2]
    share_in = master_in.shape[1]
    share_out = master_out.shape[1]

    own_in = master_in[0].astype(jnp.bfloat16)
    own_out = master_out[0].astype(jnp.bfloat16)
    pairs = [
        (s * n_dp + 2 * i + h, i * n_dp + 2 * s + h)
        for s in range(n_pipe)
        for i in range(n_pipe)
        for h in range(2)
    ]
    piece_in = lax.ppermute(own_in, ("pipe", "dp"), pairs)
    piece_out = swap(own_out.reshape(share_out, n_pipe, chunk).transpose(1, 0, 2), "pipe")
    flat_out = piece_out.transpose(1, 0, 2).reshape(share_out, width)
    all_in = lax.all_gather(piece_in, "dp", axis=0, tiled=True)
    all_out = lax.all_gather(flat_out, "dp", axis=0, tiled=True)
    weight_in = [all_in[s * chunk : (s + 1) * chunk] for s in range(n_pipe)]

    gram = {}

    def products(first, last):
        units, partial = [], []
        for t in range(first + 1, last):
            left = piece_out[first:t].reshape(-1, chunk)
            partial.append(dot(left, weight_in[t], ROWS))
            units += [(k, t, True) for k in range(first, t)]
        for t in range(first, last - 1):
            left = piece_out[first : t + 1].reshape(-1, chunk)
            partial.append(dot(left, weight_out[t], LAST))
            units += [(k, t, False) for k in range(first, t + 1)]
        padded = -(-len(units) // n_pipe) * n_pipe
        partial = [p.astype(jnp.bfloat16) for p in partial]
        partial.append(jnp.zeros(((padded - len(units)) * share_out, inner), jnp.bfloat16))
        arrived = swap(jnp.concatenate(partial, axis=0), "pipe")
        arrived = arrived.reshape(n_pipe, -1, inner)
        mine = jnp.sum(arrived.astype(jnp.float32), axis=0).astype(jnp.bfloat16)
        every = swap(jnp.tile(mine, (n_pipe, 1)), "pipe").reshape(padded, share_out, inner)
        order = sorted(range(len(units)), key=lambda at: units[at])
        columns = jnp.concatenate([every[at] for at in order], axis=1)
        return [units[at] for at in order], columns

    def unpack(units, whole):
        for at, unit in enumerate(units):
            gram[unit] = whole[:, at * inner : (at + 1) * inner]

    rows = lax.dynamic_slice_in_dim(inputs_x, me * chunk, chunk, 1)
    exact = rows.astype(jnp.float32)
    seed = lax.dynamic_slice_in_dim(cotangent, me * chunk, chunk, 1)

    def grad_start(upstream, first, last, held=None):
        columns = [dot(upstream, weight_out[s], LAST) for s in range(first, last)]
        if held is not None:
            columns, held = lax.optimization_barrier((columns, held))
        sums = sum_to_owner(columns, n_pipe)
        return {
            s: sums[:, (s - first) * inner : (s - first + 1) * inner] for s in range(first, last)
        }, held

    saved_rows, saved_act, state = {}, {}, {}

    def down_columns(first, last):
        columns = [dot(rows, weight_in[s], ROWS) for s in range(first, last)]
        return columns + split_scalars([jnp.sum(exact * exact, axis=1, keepdims=True)])

    def up_columns(first, last):
        return [dot(rows, weight_out[s], LAST) for s in range(first, last - 1)]

    def named_sums(first, last, down, up):
        at = (last - first) * inner
        raw = {s: down[:, (s - first) * inner : (s - first + 1) * inner] for s in range(first, last)}
        cross = {
            s: up[:, (s - first) * inner : (s - first + 1) * inner] for s in range(first, last - 1)
        }
        return raw, cross, down[:, at : at + 1] + down[:, at + 1 : at + 2]

    def forward_block(first, last, sums):
        raw, cross, square = sums
        for s in range(first, last):
            scale = lax.rsqrt(jnp.maximum(square, 0.0) / width + norm_eps)
            hidden = raw[s] * scale
            gate = jax.nn.sigmoid(hidden)
            act = (hidden * gate).astype(jnp.bfloat16)
            seen = {}
            if s < last - 1:
                added = {}
                for k in range(first, last - 1):
                    if k >= s:
                        added[k] = dot(act, gram[(s, k, False)], ROWS)
                    else:
                        added[k] = dot(act, gram[(k, s, False)], LAST)
                wide = act.astype(jnp.float32)
                square = square + jnp.sum(
                    wide * (2.0 * cross[s] + added[s]), axis=1, keepdims=True
                )
                for k in range(first, last - 1):
                    cross[k] = cross[k] + added[k]
                for t in range(s + 1, last):
                    raw[t] = raw[t] + dot(act, gram[(s, t, True)], ROWS)
                seen = dict(cross)
            state[s] = (hidden, gate, scale, act)
            inputs_cross[s + 1] = seen

    inputs_cross = {}

    def backward_block(first, last):
        packs, pulls = {}, {}
        for s in reversed(range(first, last)):
            hidden, gate, scale, act = state[s]
            grad_hidden = grad_act[s] * gate * (1.0 + hidden * (1.0 - gate))
            mean = jnp.sum(grad_hidden * hidden, axis=1, keepdims=True) / width
            packs[s] = (grad_hidden * scale).astype(jnp.bfloat16)
            pulls[s] = mean * scale * scale
            for t in range(first, s):
                grad_act[t] = (
                    grad_act[t]
                    + dot(packs[s], gram[(t, s, True)], LAST)
                    - pulls[s] * inputs_cross[s][t]
                )
        return packs, pulls

    upstream = seed
    upstream_exact = seed.astype(jnp.float32)
    grads = [None] * n_pipe
    reduced = {}

    def take_rows(act_all, first, last, more):
        nonlocal rows, exact
        for s in range(first, last):
            saved_rows[s] = rows
            saved_act[s] = act_all[:, (s - first) * inner : (s - first + 1) * inner]
            if s < last - 1 or more:
                exact = exact + dot(saved_act[s], weight_out[s], ROWS)
                rows = exact.astype(jnp.bfloat16)

    first, last = BLOCKS[0]
    down_sums = sum_to_owner(down_columns(first, last), n_pipe)
    all_out, down_sums = lax.optimization_barrier((all_out, down_sums))
    weight_out = [all_out[:, s * chunk : (s + 1) * chunk] for s in range(n_pipe)]
    units, columns = products(first, last)
    whole = lax.all_gather(columns, "dp", axis=0, tiled=True)
    up_sums = sum_to_owner(up_columns(first, last), n_pipe)
    made = [products(*block) for block in BLOCKS[1:]]
    whole, up_sums, made_columns = lax.optimization_barrier(
        (whole, up_sums, [columns for _, columns in made])
    )
    unpack(units, whole)
    for (units, _), columns in zip(made, made_columns):
        unpack(units, lax.all_gather(columns, "dp", axis=0, tiled=True))
    sums = named_sums(first, last, down_sums, up_sums)
    for first, last in BLOCKS[:-1]:
        forward_block(first, last, sums)
        gathered = gather_rows([state[s][3] for s in range(first, last)], n_pipe)
        take_rows(gathered, first, last, True)
        first, last = BLOCKS[BLOCKS.index((first, last)) + 1]
        both = sum_to_owner(down_columns(first, last) + up_columns(first, last), n_pipe)
        sums = named_sums(first, last, both, both[:, (last - first) * inner + LANES :])
    late, _ = lax.optimization_barrier((seed, state[BLOCKS[0][1] - 1][3]))
    grad_act, _ = grad_start(late, *BLOCKS[-1])

    for number in reversed(range(len(BLOCKS))):
        first, last = BLOCKS[number]
        count = last - first
        is_last = number == len(BLOCKS) - 1
        if is_last:
            forward_block(first, last, sums)
            acts = gather_rows([state[s][3] for s in range(first, last)], n_pipe)
        packs, pulls = backward_block(first, last)
        columns = [packs[s] for s in range(first, last)]
        columns += split_scalars([pulls[s] for s in range(first, last)])
        gathered = gather_rows(columns, n_pipe)
        if is_last:
            take_rows(acts, first, last, False)
        scalar_at = count * inner
        parts_in, parts_out = {}, {}
        for s in reversed(range(first, last)):
            pack = gathered[:, (s - first) * inner : (s - first + 1) * inner]
            pull = joined_scalar(gathered, scalar_at + 2 * (s - first))
            parts_in[s] = dot(saved_rows[s], pack, FIRST).astype(jnp.bfloat16)
            parts_out[s] = dot(saved_act[s], upstream, FIRST).astype(jnp.bfloat16)
            upstream_exact = (
                upstream_exact
                + dot(pack, weight_in[s], LAST)
                - pull * saved_rows[s].astype(jnp.float32)
            )
            upstream = upstream_exact.astype(jnp.bfloat16)
            grads[s] = upstream
        pending = [parts_in[s] for s in range(first, last)], [
            parts_out[s] for s in range(first, last)
        ]
        if number > 0:
            following, pending = grad_start(upstream, *BLOCKS[number - 1], pending)
            grad_act.update(following)
        packed = pack_grads(*pending, n_dp)
        reduced[first] = reduce_apart(packed) if number > 0 else reduce_now(packed, n_dp)

    input_grads = swap(jnp.stack(grads), "pipe")
    first = BLOCKS[0][0]
    input_grads, reduced[first] = lax.optimization_barrier((input_grads, reduced[first]))
    input_grads = input_grads.transpose(1, 0, 2).reshape(1, tok_rows, width)

    grad_in = jnp.zeros((share_in, inner), jnp.bfloat16)
    outs = []
    for first, last in BLOCKS:
        sum_in, sum_out = unpack_grads(reduced[first], inner, last - first, share_out)
        moved = move_in(sum_in, first, last - first, n_pipe, n_dp)
        grad_in = jnp.where((me >= first) & (me < last), moved, grad_in)
        outs.append(sum_out)
    grad_out = swap(jnp.concatenate(outs, axis=0), "pipe")
    grad_out = grad_out.reshape(-1, share_out, LANES)
    grad_out = jnp.concatenate([grad_out[at] for at in range(width // LANES)], axis=1)

    new_in, new_moment_in, new_second_in = adam_update(
        master_in[0], moment_in[0], second_in[0], grad_in.astype(jnp.float32)
    )
    new_out, new_moment_out, new_second_out = adam_update(
        master_out[0], moment_out[0], second_out[0], grad_out.astype(jnp.float32)
    )
    cast_in = new_in.astype(jnp.bfloat16).T.reshape(n_dp, share_out, share_in)
    cast_out = new_out.astype(jnp.bfloat16).reshape(share_out, n_dp, share_in).transpose(1, 0, 2)
    swapped = swap(jnp.stack([cast_in, cast_out], axis=1), "dp")
    roll_in = swapped[:, 0].transpose(1, 0, 2).reshape(share_out, width)
    roll_out = swapped[:, 1].reshape(inner, share_in).T
    return (
        input_grads,
        new_in[None],
        new_moment_in[None],
        new_second_in[None],
        new_out[None],
        new_moment_out[None],
        new_second_out[None],
        roll_in[None],
        roll_out[None],
    )


def solution(mesh):
    in_specs = (P("dp", None), P("dp", None)) + (P("pipe", "dp", None),) * 6
    out_specs = (P("pipe", "dp", None),) * 9
    return jax.shard_map(
        on_device, mesh=mesh, in_specs=in_specs, out_specs=out_specs, check_vma=False
    )
```

```python
import jax
import jax.numpy as jnp
from jax import lax
from jax.experimental import pallas as pl
from jax.experimental.pallas import tpu as pltpu
from jax.sharding import PartitionSpec as P

norm_eps = 1e-06
beta_one = 0.9
beta_two = 0.999
learn_rate = 0.02
decay_rate = 0.1
adam_eps = 1e-08
adam_step = 100

BLOCKS = ((0, 4), (4, 8))
LANES = 128
VMEM_BYTES = 48 * 1024 * 1024


def dot(left, right, dims):
    return lax.dot_general(left, right, (dims, ((), ())), preferred_element_type=jnp.float32)


ROWS = ((1,), (0,))
LAST = ((1,), (1,))
FIRST = ((0,), (0,))


def swap(x, axis):
    return lax.all_to_all(x, axis, 0, 0, tiled=True)


def split_scalars(scalars):
    columns = []
    for value in scalars:
        high = value.astype(jnp.bfloat16)
        columns += [high, (value - high.astype(jnp.float32)).astype(jnp.bfloat16)]
    columns.append(jnp.zeros((scalars[0].shape[0], 128 - len(columns)), jnp.bfloat16))
    return columns


def exchanged(columns, count):
    packed = columns
    if isinstance(columns, list):
        packed = jnp.concatenate([c.astype(jnp.bfloat16) for c in columns], axis=1)
    return swap(packed, "pipe").reshape(count, packed.shape[0] // count, packed.shape[1])


def adam_update(master, moment, second, grad):
    moment_new = beta_one * moment + (1.0 - beta_one) * grad
    second_new = beta_two * second + (1.0 - beta_two) * grad * grad
    moment_hat = moment_new / (1.0 - beta_one**adam_step)
    second_hat = second_new / (1.0 - beta_two**adam_step)
    master_new = master - learn_rate * (
        moment_hat / (jnp.sqrt(second_hat) + adam_eps) + decay_rate * master
    )
    return (master_new, moment_new, second_new)


def run(kernel, shapes, *operands):
    return pl.pallas_call(
        kernel,
        out_shape=[jax.ShapeDtypeStruct(shape, kind) for shape, kind in shapes],
        compiler_params=pltpu.CompilerParams(vmem_limit_bytes=VMEM_BYTES),
    )(*operands)


def part(ref, at, inner):
    return ref[:, at * inner : (at + 1) * inner]


def scalar_block(scalars):
    lane = lax.broadcasted_iota(jnp.int32, (scalars[0].shape[0], LANES), 1)
    packed = jnp.zeros(lane.shape, jnp.float32)
    for at, value in enumerate(scalars):
        high = value.astype(jnp.bfloat16).astype(jnp.float32)
        packed = jnp.where(lane == 2 * at, high, packed)
        packed = jnp.where(lane == 2 * at + 1, value - high, packed)
    return packed.astype(jnp.bfloat16)


def summed_part(ref, start, size):
    total = ref[0, :, start : start + size].astype(jnp.float32)
    for source in range(1, ref.shape[0]):
        total = total + ref[source, :, start : start + size].astype(jnp.float32)
    return total


def order_of(first, last):
    units = []
    for j in range(first, last - 1):
        units += [(j, t, False) for t in range(j, last - 1)]
        units += [(j, t, True) for t in range(j + 1, last)]
    return units


def forward_chain(first, last, width, inner, down_ref, up_ref, up_start, gram_ref):
    where = {unit: at for at, unit in enumerate(order_of(first, last))}
    count = last - first
    raw = {s: summed_part(down_ref, (s - first) * inner, inner) for s in range(first, last)}
    cross = {
        s: summed_part(up_ref, up_start + (s - first) * inner, inner)
        for s in range(first, last - 1)
    }
    square = summed_part(down_ref, count * inner, LANES)
    square = square[:, 0:1] + square[:, 1:2]
    state, crosses = {}, {}
    for s in range(first, last):
        scale = lax.rsqrt(jnp.maximum(square, 0.0) / width + norm_eps)
        hidden = raw[s] * scale
        gate = jax.nn.sigmoid(hidden)
        act = (hidden * gate).astype(jnp.bfloat16)
        state[s] = (hidden, scale, act)
        if s == last - 1:
            break
        added = {}
        for k in range(first, last - 1):
            if k >= s:
                added[k] = dot(act, part(gram_ref, where[(s, k, False)], inner), ROWS)
            else:
                added[k] = dot(act, part(gram_ref, where[(k, s, False)], inner), LAST)
        wide = act.astype(jnp.float32)
        square = square + jnp.sum(wide * (2.0 * cross[s] + added[s]), axis=1, keepdims=True)
        cross = {k: cross[k] + added[k] for k in cross}
        for t in range(s + 1, last):
            raw[t] = raw[t] + dot(act, part(gram_ref, where[(s, t, True)], inner), ROWS)
        crosses[s + 1] = cross
    return state, crosses


def backward_chain(first, last, width, inner, grad_ref, hidden_of, scale_of, cross_of, gram_ref):
    where = {unit: at for at, unit in enumerate(order_of(first, last))}
    grad_act = {s: summed_part(grad_ref, (s - first) * inner, inner) for s in range(first, last)}
    packs, pulls = {}, {}
    for s in reversed(range(first, last)):
        hidden, scale = hidden_of(s), scale_of(s)
        gate = jax.nn.sigmoid(hidden)
        grad_hidden = grad_act[s] * gate * (1.0 + hidden * (1.0 - gate))
        mean = jnp.sum(grad_hidden * hidden, axis=1, keepdims=True) / width
        packs[s] = (grad_hidden * scale).astype(jnp.bfloat16)
        pulls[s] = mean * scale * scale
        for t in range(first, s):
            grad_act[t] = (
                grad_act[t]
                + dot(packs[s], part(gram_ref, where[(t, s, True)], inner), LAST)
                - pulls[s] * cross_of(s, t)
            )
    return packs, pulls


def kept_crosses(first, last):
    return [(s, t) for s in range(first + 1, last) for t in range(first, s)]


def forward_kernel(first, last, width, inner, copies):
    def kernel(down_ref, up_ref, gram_ref, acts_ref, hidden_ref, scale_ref, cross_ref):
        state, crosses = forward_chain(
            first, last, width, inner, down_ref, up_ref, 0, gram_ref
        )
        rows = down_ref.shape[1]
        for s in range(first, last):
            hidden, scale, act = state[s]
            at = s - first
            for copy in range(copies):
                acts_ref[copy * rows : (copy + 1) * rows, at * inner : (at + 1) * inner] = act
            hidden_ref[at] = hidden
            scale_ref[at] = jnp.broadcast_to(scale, (rows, LANES))
        for at, (s, t) in enumerate(kept_crosses(first, last)):
            cross_ref[at] = crosses[s][t]

    return kernel


def store_packs(ref, packs, pulls, first, last, inner, rows, copies):
    scalars = scalar_block([pulls[s] for s in range(first, last)])
    for copy in range(copies):
        there = slice(copy * rows, (copy + 1) * rows)
        for s in range(first, last):
            ref[there, (s - first) * inner : (s - first + 1) * inner] = packs[s]
        at = (last - first) * inner
        ref[there, at : at + LANES] = scalars


def backward_kernel(first, last, width, inner, copies):
    kept = {pair: at for at, pair in enumerate(kept_crosses(first, last))}

    def kernel(grad_ref, hidden_ref, scale_ref, cross_ref, gram_ref, out_ref):
        packs, pulls = backward_chain(
            first,
            last,
            width,
            inner,
            grad_ref,
            lambda s: hidden_ref[s - first],
            lambda s: scale_ref[s - first][:, 0:1],
            lambda s, t: cross_ref[kept[(s, t)]],
            gram_ref,
        )
        store_packs(out_ref, packs, pulls, first, last, inner, grad_ref.shape[1], copies)

    return kernel


def turning_kernel(first, last, width, inner, copies):
    def kernel(sums_ref, grad_ref, gram_ref, out_ref):
        count = last - first
        state, crosses = forward_chain(
            first, last, width, inner, sums_ref, sums_ref, count * inner + LANES, gram_ref
        )
        packs, pulls = backward_chain(
            first,
            last,
            width,
            inner,
            grad_ref,
            lambda s: state[s][0],
            lambda s: state[s][1],
            lambda s, t: crosses[s][t],
            gram_ref,
        )
        rows = sums_ref.shape[1]
        store_packs(out_ref, packs, pulls, first, last, inner, rows, copies)
        for copy in range(copies):
            for s in range(first, last):
                at = count * inner + LANES + (s - first) * inner
                out_ref[copy * rows : (copy + 1) * rows, at : at + inner] = state[s][2]

    return kernel


def next_rows_kernel(first, last, then, inner, chunk):
    def kernel(rows_ref, acts_ref, in_ref, out_ref, exact_ref, columns_ref):
        exact = rows_ref[...].astype(jnp.float32)
        for s in range(first, last):
            exact = exact + dot(
                part(acts_ref, s - first, inner), part(out_ref, s, chunk), ROWS
            )
        exact_ref[...] = exact
        rows = exact.astype(jnp.bfloat16)
        at = 0
        for s in range(last, then):
            weight = in_ref[(s - last) * chunk : (s - last + 1) * chunk]
            columns_ref[:, at : at + inner] = dot(rows, weight, ROWS).astype(jnp.bfloat16)
            at += inner
        squares = jnp.sum(exact * exact, axis=1, keepdims=True)
        columns_ref[:, at : at + LANES] = scalar_block([squares])
        at += LANES
        for s in range(last, then - 1):
            columns = dot(rows, part(out_ref, s, chunk), LAST)
            columns_ref[:, at : at + inner] = columns.astype(jnp.bfloat16)
            at += inner

    return kernel


def grads_kernel(first, last, before, inner, chunk, n_dp, acts_start):
    group = last - first
    share_in = group * chunk // n_dp
    share_out = inner // n_dp
    lanes_in = inner // LANES
    lanes_out = chunk // LANES

    def kernel(*refs):
        exact_ref, packs_ref, acts_ref, up_ref, in_ref, out_ref = refs[:6]
        grads_ref, packed_ref, up_new_ref = refs[6:9]
        exact = exact_ref[...].astype(jnp.float32)
        rows = {first: exact.astype(jnp.bfloat16)}

        def act_of(s):
            at = acts_start + (s - first) * inner
            return acts_ref[:, at : at + inner]

        for s in range(first, last - 1):
            exact = exact + dot(act_of(s), part(out_ref, s, chunk), ROWS)
            rows[s + 1] = exact.astype(jnp.bfloat16)
        upstream = up_ref[...].astype(jnp.float32)
        narrow = upstream.astype(jnp.bfloat16)
        for s in reversed(range(first, last)):
            pack = part(packs_ref, s - first, inner)
            at = group * inner + 2 * (s - first)
            pull = packs_ref[:, group * inner : group * inner + LANES].astype(jnp.float32)
            at = 2 * (s - first)
            pull = pull[:, at : at + 1] + pull[:, at + 1 : at + 2]
            into = dot(rows[s], pack, FIRST).astype(jnp.bfloat16)
            for piece in range(chunk // share_in):
                device = (s - first) * (chunk // share_in) + piece
                for c in range(lanes_in):
                    packed_ref[device % 2, device // 2, c * share_in : (c + 1) * share_in] = into[
                        piece * share_in : (piece + 1) * share_in, c * LANES : (c + 1) * LANES
                    ]
            onto = dot(act_of(s), narrow, FIRST).astype(jnp.bfloat16)
            base = lanes_in * share_in + (s - first) * lanes_out * share_out
            for device in range(n_dp):
                for c in range(lanes_out):
                    row = base + c * share_out
                    packed_ref[device % 2, device // 2, row : row + share_out] = onto[
                        device * share_out : (device + 1) * share_out, c * LANES : (c + 1) * LANES
                    ]
            weight = in_ref[s * chunk : (s + 1) * chunk]
            upstream = (
                upstream + dot(pack, weight, LAST) - pull * rows[s].astype(jnp.float32)
            )
            narrow = upstream.astype(jnp.bfloat16)
            grads_ref[s - first] = narrow
        up_new_ref[...] = upstream
        if before < first:
            for s in range(before, first):
                columns = dot(narrow, part(out_ref, s, chunk), LAST).astype(jnp.bfloat16)
                refs[9][:, (s - before) * inner : (s - before + 1) * inner] = columns

    return kernel


def unpack_kernel(inner, share_in):
    def kernel(arrived_ref, in_ref, out_ref):
        lanes = inner // LANES
        for c in range(lanes):
            total = arrived_ref[0, c * share_in : (c + 1) * share_in].astype(jnp.float32)
            for source in range(1, arrived_ref.shape[0]):
                total = total + arrived_ref[source, c * share_in : (c + 1) * share_in].astype(
                    jnp.float32
                )
            in_ref[:, c * LANES : (c + 1) * LANES] = total.astype(jnp.bfloat16)
        start = lanes * share_in
        total = arrived_ref[0, start:].astype(jnp.float32)
        for source in range(1, arrived_ref.shape[0]):
            total = total + arrived_ref[source, start:].astype(jnp.float32)
        out_ref[...] = total.astype(jnp.bfloat16)

    return kernel


def adam_out_kernel(share, lanes):
    def kernel(grad_ref, master_ref, moment_ref, second_ref, master_new, moment_new, second_new):
        for device in range(grad_ref.shape[0]):
            for c in range(lanes):
                at = (device * lanes + c) * LANES
                grad = grad_ref[device, c * share : (c + 1) * share].astype(jnp.float32)
                results = adam_update(
                    master_ref[:, at : at + LANES],
                    moment_ref[:, at : at + LANES],
                    second_ref[:, at : at + LANES],
                    grad,
                )
                for ref, value in zip((master_new, moment_new, second_new), results):
                    ref[:, at : at + LANES] = value

    return kernel


def columns_kernel(order):
    def kernel(every_ref, out_ref):
        size = every_ref.shape[2]
        for at, unit in enumerate(order):
            out_ref[:, at * size : (at + 1) * size] = every_ref[unit]

    return kernel


def core_halves(packed, n_dp):
    core = lax.axis_index("dp") % 2
    mine = lax.dynamic_index_in_dim(packed, core, 0, keepdims=False)
    other = lax.dynamic_index_in_dim(packed, 1 - core, 0, keepdims=False)
    other = lax.ppermute(other, "dp", [(j, j + 1 - 2 * (j % 2)) for j in range(n_dp)])
    return (mine.astype(jnp.float32) + other.astype(jnp.float32)).astype(jnp.bfloat16)


def chips_of(n_dp):
    return [list(range(c, n_dp, 2)) for c in range(2)]


def reduce_apart(packed, n_dp):
    mine = core_halves(packed, n_dp)
    rows = mine.shape[1]
    summed = lax.psum_scatter(
        mine.reshape(-1, LANES),
        "dp",
        scatter_dimension=0,
        tiled=True,
        axis_index_groups=chips_of(n_dp),
    )
    return summed.reshape(1, rows, LANES)


def reduce_now(packed, n_dp):
    return lax.all_to_all(
        core_halves(packed, n_dp), "dp", 0, 0, tiled=True, axis_index_groups=chips_of(n_dp)
    )


def move_in(summed, first, group, n_pipe, n_dp):
    per = n_pipe // group
    moved = []
    for q in range(per):
        pairs = []
        for i in range(n_pipe):
            for j in range(q, n_dp, per):
                section = j * group // n_dp
                half = j // per % 2
                pairs.append((i * n_dp + j, (first + section) * n_dp + 2 * i + half))
        moved.append(lax.ppermute(summed, ("pipe", "dp"), pairs))
    return jnp.concatenate(moved, axis=0)


def on_device(
    inputs_x, cotangent, master_in, master_out, moment_in, moment_out, second_in, second_out
):
    n_pipe = lax.axis_size("pipe")
    n_dp = lax.axis_size("dp")
    me = lax.axis_index("pipe")
    tok_rows, width = inputs_x.shape
    chunk = width // n_pipe
    inner = master_in.shape[2]
    share_in = master_in.shape[1]
    share_out = master_out.shape[1]
    block = tok_rows // n_pipe

    own_in = master_in[0].astype(jnp.bfloat16)
    own_out = master_out[0].astype(jnp.bfloat16)
    pairs = [
        (s * n_dp + 2 * i + h, i * n_dp + 2 * s + h)
        for s in range(n_pipe)
        for i in range(n_pipe)
        for h in range(2)
    ]
    piece_in = lax.ppermute(own_in, ("pipe", "dp"), pairs)
    piece_out = swap(own_out.reshape(share_out, n_pipe, chunk).transpose(1, 0, 2), "pipe")
    flat_out = piece_out.transpose(1, 0, 2).reshape(share_out, width)
    all_in = lax.all_gather(piece_in, "dp", axis=0, tiled=True)
    all_out = lax.all_gather(flat_out, "dp", axis=0, tiled=True)
    weight_in = [all_in[s * chunk : (s + 1) * chunk] for s in range(n_pipe)]

    def products(first, last):
        units, partial = [], []
        for t in range(first + 1, last):
            left = piece_out[first:t].reshape(-1, chunk)
            partial.append(dot(left, weight_in[t], ROWS))
            units += [(k, t, True) for k in range(first, t)]
        for t in range(first, last - 1):
            left = piece_out[first : t + 1].reshape(-1, chunk)
            partial.append(dot(left, weight_out[t], LAST))
            units += [(k, t, False) for k in range(first, t + 1)]
        padded = -(-len(units) // n_pipe) * n_pipe
        partial = [p.astype(jnp.bfloat16) for p in partial]
        partial.append(jnp.zeros(((padded - len(units)) * share_out, inner), jnp.bfloat16))
        arrived = swap(jnp.concatenate(partial, axis=0), "pipe")
        arrived = arrived.reshape(n_pipe, -1, inner)
        mine = jnp.sum(arrived.astype(jnp.float32), axis=0).astype(jnp.bfloat16)
        every = swap(jnp.tile(mine, (n_pipe, 1)), "pipe").reshape(padded, share_out, inner)
        order = [units.index(unit) for unit in order_of(first, last)]
        shape = (share_out, len(units) * inner)
        return run(columns_kernel(order), [(shape, jnp.bfloat16)], every)[0]

    rows = lax.dynamic_slice_in_dim(inputs_x, me * chunk, chunk, 1)
    seed = lax.dynamic_slice_in_dim(cotangent, me * chunk, chunk, 1)

    (first, middle), (_, last) = BLOCKS
    count = middle - first
    wide = rows.astype(jnp.float32)
    down = [dot(rows, weight_in[s], ROWS) for s in range(first, middle)]
    down += split_scalars([jnp.sum(wide * wide, axis=1, keepdims=True)])
    down = exchanged(down, n_pipe)
    all_out, down = lax.optimization_barrier((all_out, down))
    weight_out = [all_out[:, s * chunk : (s + 1) * chunk] for s in range(n_pipe)]
    gram_low = lax.all_gather(products(first, middle), "dp", axis=0, tiled=True)
    up = exchanged([dot(rows, weight_out[s], LAST) for s in range(first, middle - 1)], n_pipe)
    columns = products(middle, last)
    gram_low, up, columns = lax.optimization_barrier((gram_low, up, columns))
    gram_high = lax.all_gather(columns, "dp", axis=0, tiled=True)

    kept = len(kept_crosses(first, middle))
    acts, hidden, scale, cross = run(
        forward_kernel(first, middle, width, inner, n_pipe),
        [
            ((tok_rows, count * inner), jnp.bfloat16),
            ((count, block, inner), jnp.float32),
            ((count, block, LANES), jnp.float32),
            ((kept, block, inner), jnp.float32),
        ],
        down,
        up,
        gram_low,
    )
    acts = swap(acts, "pipe")
    late, acts = lax.optimization_barrier((seed, acts))
    exact, columns = run(
        next_rows_kernel(first, middle, last, inner, chunk),
        [
            ((tok_rows, chunk), jnp.float32),
            ((tok_rows, (2 * (last - middle) - 1) * inner + LANES), jnp.bfloat16),
        ],
        rows,
        acts,
        all_in[middle * chunk : last * chunk],
        all_out,
    )
    sums = exchanged(columns, n_pipe)
    grad_high = exchanged([dot(late, weight_out[s], LAST) for s in range(middle, last)], n_pipe)

    turned = run(
        turning_kernel(middle, last, width, inner, n_pipe),
        [((tok_rows, 2 * (last - middle) * inner + LANES), jnp.bfloat16)],
        sums,
        grad_high,
        gram_high,
    )[0]
    turned = swap(turned, "pipe")

    def packed_shape(group):
        rows_packed = 2 * group * chunk * inner // (n_dp * LANES)
        return (2, n_dp // 2, rows_packed, LANES)

    grads_high, packed_high, upstream, columns = run(
        grads_kernel(middle, last, first, inner, chunk, n_dp, (last - middle) * inner + LANES),
        [
            ((last - middle, tok_rows, chunk), jnp.bfloat16),
            (packed_shape(last - middle), jnp.bfloat16),
            ((tok_rows, chunk), jnp.float32),
            ((tok_rows, count * inner), jnp.bfloat16),
        ],
        exact,
        turned,
        turned,
        seed,
        all_in,
        all_out,
    )
    grad_low = exchanged(columns, n_pipe)
    summed_high = reduce_apart(packed_high, n_dp)

    packs = run(
        backward_kernel(first, middle, width, inner, n_pipe),
        [((tok_rows, count * inner + LANES), jnp.bfloat16)],
        grad_low,
        hidden,
        scale,
        cross,
        gram_low,
    )[0]
    packs = swap(packs, "pipe")
    grads_low, packed_low, _ = run(
        grads_kernel(first, middle, first, inner, chunk, n_dp, 0),
        [
            ((count, tok_rows, chunk), jnp.bfloat16),
            (packed_shape(count), jnp.bfloat16),
            ((tok_rows, chunk), jnp.float32),
        ],
        rows,
        packs,
        acts,
        upstream,
        all_in,
        all_out,
    )
    arrived_low = reduce_now(packed_low, n_dp)

    input_grads = swap(jnp.concatenate([grads_low, grads_high], axis=0), "pipe")
    input_grads, arrived_low = lax.optimization_barrier((input_grads, arrived_low))
    input_grads = input_grads.transpose(1, 0, 2).reshape(1, tok_rows, width)

    grad_in = jnp.zeros((share_in, inner), jnp.bfloat16)
    outs = []
    for (low, high), arrived in zip(BLOCKS, (arrived_low, summed_high)):
        group = high - low
        share = group * chunk // n_dp
        sum_in, sum_out = run(
            unpack_kernel(inner, share),
            [
                ((share, inner), jnp.bfloat16),
                ((arrived.shape[1] - share * inner // LANES, LANES), jnp.bfloat16),
            ],
            arrived,
        )
        moved = move_in(sum_in, low, group, n_pipe, n_dp)
        grad_in = jnp.where((me >= low) & (me < high), moved, grad_in)
        outs.append(sum_out.reshape(group, -1, LANES))
    grad_out = swap(jnp.concatenate(outs, axis=0), "pipe")

    new_in, new_moment_in, new_second_in = adam_update(
        master_in[0], moment_in[0], second_in[0], grad_in.astype(jnp.float32)
    )
    shape_out = (share_out, width)
    new_out, new_moment_out, new_second_out = run(
        adam_out_kernel(share_out, chunk // LANES),
        [(shape_out, jnp.float32)] * 3,
        grad_out,
        master_out[0],
        moment_out[0],
        second_out[0],
    )
    cast_in = new_in.astype(jnp.bfloat16).T.reshape(n_dp, share_out, share_in)
    cast_out = new_out.astype(jnp.bfloat16).reshape(share_out, n_dp, share_in).transpose(1, 0, 2)
    swapped = swap(jnp.stack([cast_in, cast_out], axis=1), "dp")
    roll_in = swapped[:, 0].transpose(1, 0, 2).reshape(share_out, width)
    roll_out = swapped[:, 1].reshape(inner, share_in).T
    return (
        input_grads,
        new_in[None],
        new_moment_in[None],
        new_second_in[None],
        new_out[None],
        new_moment_out[None],
        new_second_out[None],
        roll_in[None],
        roll_out[None],
    )


def solution(mesh):
    in_specs = (P("dp", None), P("dp", None)) + (P("pipe", "dp", None),) * 6
    out_specs = (P("pipe", "dp", None),) * 9
    return jax.shard_map(
        on_device, mesh=mesh, in_specs=in_specs, out_specs=out_specs, check_vma=False
    )
```

```python
import jax
import jax.numpy as jnp
from jax import lax
from jax.experimental import pallas as pl
from jax.experimental.pallas import tpu as pltpu
from jax.sharding import PartitionSpec as P

norm_eps = 1e-06
beta_one = 0.9
beta_two = 0.999
learn_rate = 0.02
decay_rate = 0.1
adam_eps = 1e-08
adam_step = 100

BLOCKS = ((0, 4), (4, 8))
LANES = 128
VMEM_BYTES = 48 * 1024 * 1024


def dot(left, right, dims):
    return lax.dot_general(left, right, (dims, ((), ())), preferred_element_type=jnp.float32)


ROWS = ((1,), (0,))
LAST = ((1,), (1,))
FIRST = ((0,), (0,))


def swap(x, axis):
    return lax.all_to_all(x, axis, 0, 0, tiled=True)


def split_scalars(scalars):
    columns = []
    for value in scalars:
        high = value.astype(jnp.bfloat16)
        columns += [high, (value - high.astype(jnp.float32)).astype(jnp.bfloat16)]
    columns.append(jnp.zeros((scalars[0].shape[0], 128 - len(columns)), jnp.bfloat16))
    return columns


def exchanged(columns, count):
    packed = columns
    if isinstance(columns, list):
        packed = jnp.concatenate([c.astype(jnp.bfloat16) for c in columns], axis=1)
    return swap(packed, "pipe").reshape(count, packed.shape[0] // count, packed.shape[1])


def adam_update(master, moment, second, grad):
    moment_new = beta_one * moment + (1.0 - beta_one) * grad
    second_new = beta_two * second + (1.0 - beta_two) * grad * grad
    moment_hat = moment_new / (1.0 - beta_one**adam_step)
    second_hat = second_new / (1.0 - beta_two**adam_step)
    master_new = master - learn_rate * (
        moment_hat / (jnp.sqrt(second_hat) + adam_eps) + decay_rate * master
    )
    return (master_new, moment_new, second_new)


def run(kernel, shapes, *operands, specs=None):
    more = {}
    if specs is not None:
        whole = [pl.BlockSpec(x.shape, zeros_map(x.ndim)) for x in operands]
        outs = [pl.BlockSpec(shape, zeros_map(len(shape))) for shape, _ in shapes]
        given = [specs.get(at, spec) for at, spec in enumerate(whole)]
        more = {"grid": (1,), "in_specs": given, "out_specs": outs}
    return pl.pallas_call(
        kernel,
        out_shape=[jax.ShapeDtypeStruct(shape, kind) for shape, kind in shapes],
        compiler_params=pltpu.CompilerParams(vmem_limit_bytes=VMEM_BYTES),
        **more,
    )(*operands)


def zeros_map(ndim):
    return lambda step: (0,) * ndim


def part(ref, at, inner):
    return ref[:, at * inner : (at + 1) * inner]


def scalar_block(scalars):
    lane = lax.broadcasted_iota(jnp.int32, (scalars[0].shape[0], LANES), 1)
    packed = jnp.zeros(lane.shape, jnp.float32)
    for at, value in enumerate(scalars):
        high = value.astype(jnp.bfloat16).astype(jnp.float32)
        packed = jnp.where(lane == 2 * at, high, packed)
        packed = jnp.where(lane == 2 * at + 1, value - high, packed)
    return packed.astype(jnp.bfloat16)


def summed_part(ref, start, size):
    total = ref[0, :, start : start + size].astype(jnp.float32)
    for source in range(1, ref.shape[0]):
        total = total + ref[source, :, start : start + size].astype(jnp.float32)
    return total


def down_units(first, last):
    return [(j, t, True) for j in range(first, last) for t in range(j + 1, last)]


def up_units(first, last):
    return [(j, t, False) for j in range(first, last - 1) for t in range(j, last - 1)]


def finder(first, last, inner, down_ref, up_ref, up_start):
    places = {unit: (down_ref, at) for at, unit in enumerate(down_units(first, last))}
    if up_ref is not None:
        for at, unit in enumerate(up_units(first, last)):
            places[unit] = (up_ref, up_start + at)

    def find(unit):
        ref, at = places[unit]
        return part(ref, at, inner)

    return find


def forward_chain(first, last, width, inner, down_ref, up_ref, up_start, find):
    count = last - first
    raw = {s: summed_part(down_ref, (s - first) * inner, inner) for s in range(first, last)}
    cross = {
        s: summed_part(up_ref, up_start + (s - first) * inner, inner)
        for s in range(first, last - 1)
    }
    square = summed_part(down_ref, count * inner, LANES)
    square = square[:, 0:1] + square[:, 1:2]
    state, crosses = {}, {}
    for s in range(first, last):
        scale = lax.rsqrt(jnp.maximum(square, 0.0) / width + norm_eps)
        hidden = raw[s] * scale
        gate = jax.nn.sigmoid(hidden)
        act = (hidden * gate).astype(jnp.bfloat16)
        state[s] = (hidden, scale, act)
        if s == last - 1:
            break
        added = {}
        for k in range(first, last - 1):
            if k >= s:
                added[k] = dot(act, find((s, k, False)), ROWS)
            else:
                added[k] = dot(act, find((k, s, False)), LAST)
        wide = act.astype(jnp.float32)
        square = square + jnp.sum(wide * (2.0 * cross[s] + added[s]), axis=1, keepdims=True)
        cross = {k: cross[k] + added[k] for k in cross}
        for t in range(s + 1, last):
            raw[t] = raw[t] + dot(act, find((s, t, True)), ROWS)
        crosses[s + 1] = cross
    return state, crosses


def backward_chain(first, last, width, inner, grad_ref, hidden_of, scale_of, cross_of, find):
    grad_act = {s: summed_part(grad_ref, (s - first) * inner, inner) for s in range(first, last)}
    packs, pulls = {}, {}
    for s in reversed(range(first, last)):
        hidden, scale = hidden_of(s), scale_of(s)
        gate = jax.nn.sigmoid(hidden)
        grad_hidden = grad_act[s] * gate * (1.0 + hidden * (1.0 - gate))
        mean = jnp.sum(grad_hidden * hidden, axis=1, keepdims=True) / width
        packs[s] = (grad_hidden * scale).astype(jnp.bfloat16)
        pulls[s] = mean * scale * scale
        for t in range(first, s):
            grad_act[t] = (
                grad_act[t]
                + dot(packs[s], find((t, s, True)), LAST)
                - pulls[s] * cross_of(s, t)
            )
    return packs, pulls


def kept_crosses(first, last):
    return [(s, t) for s in range(first + 1, last) for t in range(first, s)]


def forward_kernel(first, last, width, inner, copies):
    def kernel(
        down_ref, up_ref, gram_in_ref, gram_out_ref, acts_ref, hidden_ref, scale_ref, cross_ref
    ):
        find = finder(first, last, inner, gram_in_ref, gram_out_ref, 0)
        state, crosses = forward_chain(first, last, width, inner, down_ref, up_ref, 0, find)
        rows = down_ref.shape[1]
        for s in range(first, last):
            hidden, scale, act = state[s]
            at = s - first
            for copy in range(copies):
                acts_ref[copy * rows : (copy + 1) * rows, at * inner : (at + 1) * inner] = act
            hidden_ref[at] = hidden
            scale_ref[at] = jnp.broadcast_to(scale, (rows, LANES))
        for at, (s, t) in enumerate(kept_crosses(first, last)):
            cross_ref[at] = crosses[s][t]

    return kernel


def store_packs(ref, packs, pulls, first, last, inner, rows, copies):
    scalars = scalar_block([pulls[s] for s in range(first, last)])
    for copy in range(copies):
        there = slice(copy * rows, (copy + 1) * rows)
        for s in range(first, last):
            ref[there, (s - first) * inner : (s - first + 1) * inner] = packs[s]
        at = (last - first) * inner
        ref[there, at : at + LANES] = scalars


def backward_kernel(first, last, width, inner, copies):
    kept = {pair: at for at, pair in enumerate(kept_crosses(first, last))}

    def kernel(grad_ref, hidden_ref, scale_ref, cross_ref, gram_ref, out_ref):
        packs, pulls = backward_chain(
            first,
            last,
            width,
            inner,
            grad_ref,
            lambda s: hidden_ref[s - first],
            lambda s: scale_ref[s - first][:, 0:1],
            lambda s, t: cross_ref[kept[(s, t)]],
            finder(first, last, inner, gram_ref, None, 0),
        )
        store_packs(out_ref, packs, pulls, first, last, inner, grad_ref.shape[1], copies)

    return kernel


def turning_kernel(first, last, width, inner, copies):
    def kernel(sums_ref, grad_ref, gram_ref, out_ref):
        count = last - first
        find = finder(first, last, inner, gram_ref, gram_ref, len(down_units(first, last)))
        state, crosses = forward_chain(
            first, last, width, inner, sums_ref, sums_ref, count * inner + LANES, find
        )
        packs, pulls = backward_chain(
            first,
            last,
            width,
            inner,
            grad_ref,
            lambda s: state[s][0],
            lambda s: state[s][1],
            lambda s, t: crosses[s][t],
            find,
        )
        rows = sums_ref.shape[1]
        store_packs(out_ref, packs, pulls, first, last, inner, rows, copies)
        for copy in range(copies):
            for s in range(first, last):
                at = count * inner + LANES + (s - first) * inner
                out_ref[copy * rows : (copy + 1) * rows, at : at + inner] = state[s][2]

    return kernel


def next_rows_kernel(first, last, then, inner, chunk):
    def kernel(rows_ref, acts_ref, in_ref, out_ref, exact_ref, columns_ref):
        exact = rows_ref[...].astype(jnp.float32)
        for s in range(first, last):
            exact = exact + dot(
                part(acts_ref, s - first, inner), part(out_ref, s, chunk), ROWS
            )
        exact_ref[...] = exact
        rows = exact.astype(jnp.bfloat16)
        at = 0
        for s in range(last, then):
            weight = in_ref[(s - last) * chunk : (s - last + 1) * chunk]
            columns_ref[:, at : at + inner] = dot(rows, weight, ROWS).astype(jnp.bfloat16)
            at += inner
        squares = jnp.sum(exact * exact, axis=1, keepdims=True)
        columns_ref[:, at : at + LANES] = scalar_block([squares])
        at += LANES
        for s in range(last, then - 1):
            columns = dot(rows, part(out_ref, s, chunk), LAST)
            columns_ref[:, at : at + inner] = columns.astype(jnp.bfloat16)
            at += inner

    return kernel


def grads_kernel(first, last, before, inner, chunk, n_dp, acts_start):
    group = last - first
    share_in = group * chunk // n_dp
    share_out = inner // n_dp
    lanes_in = inner // LANES
    lanes_out = chunk // LANES

    def kernel(*refs):
        core_ref, exact_ref, packs_ref, acts_ref, up_ref, in_ref, out_ref = refs[:7]
        grads_ref, mine_ref, other_ref, up_new_ref = refs[7:11]
        exact = exact_ref[...].astype(jnp.float32)
        rows = {first: exact.astype(jnp.bfloat16)}

        def act_of(s):
            at = acts_start + (s - first) * inner
            return acts_ref[:, at : at + inner]

        for s in range(first, last - 1):
            exact = exact + dot(act_of(s), part(out_ref, s, chunk), ROWS)
            rows[s + 1] = exact.astype(jnp.bfloat16)
        upstream = up_ref[...].astype(jnp.float32)
        narrow = upstream.astype(jnp.bfloat16)
        for s in reversed(range(first, last)):
            pack = part(packs_ref, s - first, inner)
            at = group * inner + 2 * (s - first)
            pull = packs_ref[:, group * inner : group * inner + LANES].astype(jnp.float32)
            at = 2 * (s - first)
            pull = pull[:, at : at + 1] + pull[:, at + 1 : at + 2]
            into = dot(rows[s], pack, FIRST).astype(jnp.bfloat16)
            onto = dot(act_of(s), narrow, FIRST).astype(jnp.bfloat16)
            base = lanes_in * share_in + (s - first) * lanes_out * share_out

            def store(refs_of, into=into, onto=onto, base=base, s=s):
                for piece in range(chunk // share_in):
                    device = (s - first) * (chunk // share_in) + piece
                    ref = refs_of[device % 2]
                    for c in range(lanes_in):
                        ref[device // 2, c * share_in : (c + 1) * share_in] = into[
                            piece * share_in : (piece + 1) * share_in,
                            c * LANES : (c + 1) * LANES,
                        ]
                for device in range(n_dp):
                    ref = refs_of[device % 2]
                    for c in range(lanes_out):
                        row = base + c * share_out
                        ref[device // 2, row : row + share_out] = onto[
                            device * share_out : (device + 1) * share_out,
                            c * LANES : (c + 1) * LANES,
                        ]

            @pl.when(core_ref[0] == 0)
            def _():
                store((mine_ref, other_ref))

            @pl.when(core_ref[0] == 1)
            def _():
                store((other_ref, mine_ref))

            weight = in_ref[s * chunk : (s + 1) * chunk]
            upstream = (
                upstream + dot(pack, weight, LAST) - pull * rows[s].astype(jnp.float32)
            )
            narrow = upstream.astype(jnp.bfloat16)
            grads_ref[s - first] = narrow
        up_new_ref[...] = upstream
        if before < first:
            for s in range(before, first):
                columns = dot(narrow, part(out_ref, s, chunk), LAST).astype(jnp.bfloat16)
                refs[11][:, (s - before) * inner : (s - before + 1) * inner] = columns

    return kernel


def unpack_kernel(inner, share_in):
    def kernel(arrived_ref, in_ref, out_ref):
        lanes = inner // LANES
        for c in range(lanes):
            total = arrived_ref[0, c * share_in : (c + 1) * share_in].astype(jnp.float32)
            for source in range(1, arrived_ref.shape[0]):
                total = total + arrived_ref[source, c * share_in : (c + 1) * share_in].astype(
                    jnp.float32
                )
            in_ref[:, c * LANES : (c + 1) * LANES] = total.astype(jnp.bfloat16)
        start = lanes * share_in
        total = arrived_ref[0, start:].astype(jnp.float32)
        for source in range(1, arrived_ref.shape[0]):
            total = total + arrived_ref[source, start:].astype(jnp.float32)
        out_ref[...] = total.astype(jnp.bfloat16)

    return kernel


def adam_kernel(share, lanes, share_in):
    def kernel(*refs):
        into_ref, onto_ref = refs[:2]
        state_in, state_out = refs[2:5], refs[5:8]
        new_in, new_out, pieces_ref = refs[8:11], refs[11:14], refs[14]
        per = LANES // share
        for c in range(into_ref.shape[1] // LANES):
            there = slice(c * LANES, (c + 1) * LANES)
            grad = into_ref[:, there].astype(jnp.float32)
            results = adam_update(*(ref[:, there] for ref in state_in), grad)
            for ref, value in zip(new_in, results):
                ref[:, there] = value
            turned = results[0].T.astype(jnp.bfloat16)
            for q in range(per):
                pieces_ref[c * per + q, 0] = turned[q * share : (q + 1) * share]
        for device in range(onto_ref.shape[0]):
            for c in range(lanes):
                at = (device * lanes + c) * LANES
                grad = onto_ref[device, c * share : (c + 1) * share].astype(jnp.float32)
                results = adam_update(*(ref[:, at : at + LANES] for ref in state_out), grad)
                for ref, value in zip(new_out, results):
                    ref[:, at : at + LANES] = value
        for device in range(pieces_ref.shape[0]):
            at = device * share_in
            start = at // LANES * LANES
            stop = -(-(at + share_in) // LANES) * LANES
            values = new_out[0][:, start:stop][:, at - start : at - start + share_in]
            pieces_ref[device, 1] = values.astype(jnp.bfloat16)

    return kernel


def rollout_kernel(share, share_in):
    def kernel(pieces_ref, in_ref, out_ref):
        per = LANES // share
        for pair in range(pieces_ref.shape[0] // 2):
            both = [pieces_ref[2 * pair + h, 0].astype(jnp.float32) for h in range(2)]
            at = 2 * pair * share_in
            in_ref[:, at : at + 2 * share_in] = jnp.concatenate(both, axis=1).astype(jnp.bfloat16)
        for c in range(pieces_ref.shape[0] // per):
            rows = [pieces_ref[c * per + q, 1].astype(jnp.float32) for q in range(per)]
            out_ref[:, c * LANES : (c + 1) * LANES] = jnp.concatenate(rows, axis=0).T.astype(
                jnp.bfloat16
            )

    return kernel


def columns_kernel(orders):
    def kernel(every_ref, *out_refs):
        size = every_ref.shape[2]
        for out_ref, order in zip(out_refs, orders):
            for at, unit in enumerate(order):
                out_ref[:, at * size : (at + 1) * size] = every_ref[unit]

    return kernel


def core_halves(mine, other, n_dp):
    other = lax.ppermute(other, "dp", [(j, j + 1 - 2 * (j % 2)) for j in range(n_dp)])
    return (mine.astype(jnp.float32) + other.astype(jnp.float32)).astype(jnp.bfloat16)


def chips_of(n_dp):
    return [list(range(c, n_dp, 2)) for c in range(2)]


def reduce_apart(mine, other, n_dp):
    mine = core_halves(mine, other, n_dp)
    rows = mine.shape[1]
    summed = lax.psum_scatter(
        mine.reshape(-1, LANES),
        "dp",
        scatter_dimension=0,
        tiled=True,
        axis_index_groups=chips_of(n_dp),
    )
    return summed.reshape(1, rows, LANES)


def reduce_now(mine, other, n_dp):
    return lax.all_to_all(
        core_halves(mine, other, n_dp), "dp", 0, 0, tiled=True, axis_index_groups=chips_of(n_dp)
    )


def move_in(summed, first, group, n_pipe, n_dp):
    per = n_pipe // group
    moved = []
    for q in range(per):
        pairs = []
        for i in range(n_pipe):
            for j in range(q, n_dp, per):
                section = j * group // n_dp
                half = j // per % 2
                pairs.append((i * n_dp + j, (first + section) * n_dp + 2 * i + half))
        moved.append(lax.ppermute(summed, ("pipe", "dp"), pairs))
    return jnp.concatenate(moved, axis=0)


def on_device(
    inputs_x, cotangent, master_in, master_out, moment_in, moment_out, second_in, second_out
):
    n_pipe = lax.axis_size("pipe")
    n_dp = lax.axis_size("dp")
    me = lax.axis_index("pipe")
    tok_rows, width = inputs_x.shape
    chunk = width // n_pipe
    inner = master_in.shape[2]
    share_in = master_in.shape[1]
    share_out = master_out.shape[1]
    block = tok_rows // n_pipe

    own_in = master_in[0].astype(jnp.bfloat16)
    own_out = master_out[0].astype(jnp.bfloat16)
    pairs = [
        (s * n_dp + 2 * i + h, i * n_dp + 2 * s + h)
        for s in range(n_pipe)
        for i in range(n_pipe)
        for h in range(2)
    ]
    piece_in = lax.ppermute(own_in, ("pipe", "dp"), pairs)
    piece_out = swap(own_out.reshape(share_out, n_pipe, chunk).transpose(1, 0, 2), "pipe")
    flat_out = piece_out.transpose(1, 0, 2).reshape(share_out, width)
    all_in = lax.all_gather(piece_in, "dp", axis=0, tiled=True)
    all_out = lax.all_gather(flat_out, "dp", axis=0, tiled=True)
    weight_in = [all_in[s * chunk : (s + 1) * chunk] for s in range(n_pipe)]

    def products(down, blocks):
        units, partial, orders = [], [], []
        for first, last in blocks:
            wanted = (down_units if down else up_units)(first, last)
            for t in sorted({t for _, t, _ in wanted}):
                ks = [k for k, other, _ in wanted if other == t]
                left = piece_out[ks[0] : ks[-1] + 1].reshape(-1, chunk)
                if down:
                    partial.append(dot(left, weight_in[t], ROWS))
                else:
                    partial.append(dot(left, weight_out[t], LAST))
                units += [(k, t, down) for k in ks]
        for first, last in blocks:
            wanted = (down_units if down else up_units)(first, last)
            orders.append([units.index(unit) for unit in wanted])
        padded = -(-len(units) // n_pipe) * n_pipe
        partial = [p.astype(jnp.bfloat16) for p in partial]
        if padded > len(units):
            partial.append(jnp.zeros(((padded - len(units)) * share_out, inner), jnp.bfloat16))
        arrived = swap(jnp.concatenate(partial, axis=0), "pipe")
        arrived = arrived.reshape(n_pipe, -1, inner)
        mine = jnp.sum(arrived.astype(jnp.float32), axis=0).astype(jnp.bfloat16)
        every = swap(jnp.tile(mine, (n_pipe, 1)), "pipe").reshape(padded, share_out, inner)
        shapes = [((share_out, len(order) * inner), jnp.bfloat16) for order in orders]
        return run(columns_kernel(orders), shapes, every)

    def over_dp(columns):
        return lax.all_gather(columns, "dp", axis=0, tiled=True)

    rows = lax.dynamic_slice_in_dim(inputs_x, me * chunk, chunk, 1)
    seed = lax.dynamic_slice_in_dim(cotangent, me * chunk, chunk, 1)

    (first, middle), (_, last) = BLOCKS
    count = middle - first
    wide = rows.astype(jnp.float32)
    down = [dot(rows, weight_in[s], ROWS) for s in range(first, middle)]
    down += split_scalars([jnp.sum(wide * wide, axis=1, keepdims=True)])
    down = exchanged(down, n_pipe)
    (down_low,) = products(True, BLOCKS[:1])
    all_out, down, down_low = lax.optimization_barrier((all_out, down, down_low))
    weight_out = [all_out[:, s * chunk : (s + 1) * chunk] for s in range(n_pipe)]
    gram_in_low = over_dp(down_low)
    up_low, up_high = products(False, BLOCKS)
    gram_out_low = over_dp(up_low)
    held_in, up_low = lax.optimization_barrier((all_in, up_low))
    weight_in = [held_in[s * chunk : (s + 1) * chunk] for s in range(n_pipe)]
    (down_high,) = products(True, BLOCKS[1:])
    up = exchanged([dot(rows, weight_out[s], LAST) for s in range(first, middle - 1)], n_pipe)
    gram_in_low, gram_out_low, up, columns = lax.optimization_barrier(
        (gram_in_low, gram_out_low, up, jnp.concatenate([down_high, up_high], axis=1))
    )
    gram_high = over_dp(columns)

    kept = len(kept_crosses(first, middle))
    acts, hidden, scale, cross = run(
        forward_kernel(first, middle, width, inner, n_pipe),
        [
            ((tok_rows, count * inner), jnp.bfloat16),
            ((count, block, inner), jnp.float32),
            ((count, block, LANES), jnp.float32),
            ((kept, block, inner), jnp.float32),
        ],
        down,
        up,
        gram_in_low,
        gram_out_low,
    )
    late, acts = lax.optimization_barrier((seed, acts))
    acts = swap(acts, "pipe")
    exact, columns = run(
        next_rows_kernel(first, middle, last, inner, chunk),
        [
            ((tok_rows, chunk), jnp.float32),
            ((tok_rows, (2 * (last - middle) - 1) * inner + LANES), jnp.bfloat16),
        ],
        rows,
        acts,
        all_in,
        all_out,
        specs={
            2: pl.BlockSpec(
                ((last - middle) * chunk, inner), lambda step: (middle // (last - middle), 0)
            )
        },
    )
    sums = exchanged(columns, n_pipe)
    grad_high = exchanged([dot(late, weight_out[s], LAST) for s in range(middle, last)], n_pipe)

    turned = run(
        turning_kernel(middle, last, width, inner, n_pipe),
        [((tok_rows, 2 * (last - middle) * inner + LANES), jnp.bfloat16)],
        sums,
        grad_high,
        gram_high,
    )[0]
    turned = swap(turned, "pipe")

    def packed_shape(group):
        rows_packed = 2 * group * chunk * inner // (n_dp * LANES)
        return (n_dp // 2, rows_packed, LANES)

    core = (lax.axis_index("dp") % 2).astype(jnp.int32).reshape(1)
    in_smem = {0: pl.BlockSpec(memory_space=pltpu.SMEM)}

    grads_high, mine, other, upstream, columns = run(
        grads_kernel(middle, last, first, inner, chunk, n_dp, (last - middle) * inner + LANES),
        [
            ((last - middle, tok_rows, chunk), jnp.bfloat16),
            (packed_shape(last - middle), jnp.bfloat16),
            (packed_shape(last - middle), jnp.bfloat16),
            ((tok_rows, chunk), jnp.float32),
            ((tok_rows, count * inner), jnp.bfloat16),
        ],
        core,
        exact,
        turned,
        turned,
        seed,
        all_in,
        all_out,
        specs=in_smem,
    )
    grad_low = exchanged(columns, n_pipe)
    summed_high = reduce_apart(mine, other, n_dp)

    packs = run(
        backward_kernel(first, middle, width, inner, n_pipe),
        [((tok_rows, count * inner + LANES), jnp.bfloat16)],
        grad_low,
        hidden,
        scale,
        cross,
        gram_in_low,
    )[0]
    packs = swap(packs, "pipe")
    grads_low, mine, other, _ = run(
        grads_kernel(first, middle, first, inner, chunk, n_dp, 0),
        [
            ((count, tok_rows, chunk), jnp.bfloat16),
            (packed_shape(count), jnp.bfloat16),
            (packed_shape(count), jnp.bfloat16),
            ((tok_rows, chunk), jnp.float32),
        ],
        core,
        rows,
        packs,
        acts,
        upstream,
        all_in,
        all_out,
        specs=in_smem,
    )
    arrived_low = reduce_now(mine, other, n_dp)

    input_grads = swap(jnp.concatenate([grads_low, grads_high], axis=0), "pipe")
    input_grads, arrived_low = lax.optimization_barrier((input_grads, arrived_low))
    input_grads = input_grads.transpose(1, 0, 2).reshape(1, tok_rows, width)

    grad_in = jnp.zeros((share_in, inner), jnp.bfloat16)
    outs = []
    for (low, high), arrived in zip(BLOCKS, (arrived_low, summed_high)):
        group = high - low
        share = group * chunk // n_dp
        sum_in, sum_out = run(
            unpack_kernel(inner, share),
            [
                ((share, inner), jnp.bfloat16),
                ((arrived.shape[1] - share * inner // LANES, LANES), jnp.bfloat16),
            ],
            arrived,
        )
        moved = move_in(sum_in, low, group, n_pipe, n_dp)
        grad_in = jnp.where((me >= low) & (me < high), moved, grad_in)
        outs.append(sum_out.reshape(group, -1, LANES))
    grad_out = swap(jnp.concatenate(outs, axis=0), "pipe")

    shape_in, shape_out = (share_in, inner), (share_out, width)
    *updated, pieces = run(
        adam_kernel(share_out, chunk // LANES, share_in),
        [(shape_in, jnp.float32)] * 3
        + [(shape_out, jnp.float32)] * 3
        + [((n_dp, 2, share_out, share_in), jnp.bfloat16)],
        grad_in,
        grad_out,
        master_in[0],
        moment_in[0],
        second_in[0],
        master_out[0],
        moment_out[0],
        second_out[0],
    )
    new_in, new_moment_in, new_second_in, new_out, new_moment_out, new_second_out = updated
    roll_in, roll_out = run(
        rollout_kernel(share_out, share_in),
        [(shape_out, jnp.bfloat16), (shape_in, jnp.bfloat16)],
        swap(pieces, "dp"),
    )
    return (
        input_grads,
        new_in[None],
        new_moment_in[None],
        new_second_in[None],
        new_out[None],
        new_moment_out[None],
        new_second_out[None],
        roll_in[None],
        roll_out[None],
    )


def solution(mesh):
    in_specs = (P("dp", None), P("dp", None)) + (P("pipe", "dp", None),) * 6
    out_specs = (P("pipe", "dp", None),) * 9
    return jax.shard_map(
        on_device, mesh=mesh, in_specs=in_specs, out_specs=out_specs, check_vma=False
    )
```

```python
import jax
import jax.numpy as jnp
from jax import lax
from jax.experimental import pallas as pl
from jax.experimental.pallas import tpu as pltpu
from jax.sharding import PartitionSpec as P

norm_eps = 1e-06
beta_one = 0.9
beta_two = 0.999
learn_rate = 0.02
decay_rate = 0.1
adam_eps = 1e-08
adam_step = 100

BLOCKS = ((0, 4), (4, 8))
LANES = 128
VMEM_BYTES = 48 * 1024 * 1024


def dot(left, right, dims):
    return lax.dot_general(left, right, (dims, ((), ())), preferred_element_type=jnp.float32)


ROWS = ((1,), (0,))
LAST = ((1,), (1,))
FIRST = ((0,), (0,))


def swap(x, axis):
    return lax.all_to_all(x, axis, 0, 0, tiled=True)


def split_scalars(scalars):
    columns = []
    for value in scalars:
        high = value.astype(jnp.bfloat16)
        columns += [high, (value - high.astype(jnp.float32)).astype(jnp.bfloat16)]
    columns.append(jnp.zeros((scalars[0].shape[0], 128 - len(columns)), jnp.bfloat16))
    return columns


def exchanged(columns, count):
    packed = columns
    if isinstance(columns, list):
        packed = jnp.concatenate([c.astype(jnp.bfloat16) for c in columns], axis=1)
    return swap(packed, "pipe").reshape(count, packed.shape[0] // count, packed.shape[1])


def adam_update(master, moment, second, grad):
    moment_new = beta_one * moment + (1.0 - beta_one) * grad
    second_new = beta_two * second + (1.0 - beta_two) * grad * grad
    moment_hat = moment_new / (1.0 - beta_one**adam_step)
    second_hat = second_new / (1.0 - beta_two**adam_step)
    master_new = master - learn_rate * (
        moment_hat / (jnp.sqrt(second_hat) + adam_eps) + decay_rate * master
    )
    return (master_new, moment_new, second_new)


def run(kernel, shapes, *operands, specs=None):
    more = {}
    if specs is not None:
        whole = [pl.BlockSpec(x.shape, zeros_map(x.ndim)) for x in operands]
        outs = [pl.BlockSpec(shape, zeros_map(len(shape))) for shape, _ in shapes]
        given = [specs.get(at, spec) for at, spec in enumerate(whole)]
        more = {"grid": (1,), "in_specs": given, "out_specs": outs}
    return pl.pallas_call(
        kernel,
        out_shape=[jax.ShapeDtypeStruct(shape, kind) for shape, kind in shapes],
        compiler_params=pltpu.CompilerParams(vmem_limit_bytes=VMEM_BYTES),
        **more,
    )(*operands)


def zeros_map(ndim):
    return lambda step: (0,) * ndim


def part(ref, at, inner):
    return ref[:, at * inner : (at + 1) * inner]


def scalar_block(scalars):
    lane = lax.broadcasted_iota(jnp.int32, (scalars[0].shape[0], LANES), 1)
    packed = jnp.zeros(lane.shape, jnp.float32)
    for at, value in enumerate(scalars):
        high = value.astype(jnp.bfloat16).astype(jnp.float32)
        packed = jnp.where(lane == 2 * at, high, packed)
        packed = jnp.where(lane == 2 * at + 1, value - high, packed)
    return packed.astype(jnp.bfloat16)


def summed_part(ref, start, size):
    total = ref[0, :, start : start + size].astype(jnp.float32)
    for source in range(1, ref.shape[0]):
        total = total + ref[source, :, start : start + size].astype(jnp.float32)
    return total


def down_units(first, last):
    return [(j, t, True) for j in range(first, last) for t in range(j + 1, last)]


def up_units(first, last):
    return [(j, t, False) for j in range(first, last - 1) for t in range(j, last - 1)]


def finder(first, last, inner, down_ref, up_ref, up_start):
    places = {unit: (down_ref, at) for at, unit in enumerate(down_units(first, last))}
    if up_ref is not None:
        for at, unit in enumerate(up_units(first, last)):
            places[unit] = (up_ref, up_start + at)

    def find(unit):
        ref, at = places[unit]
        return part(ref, at, inner)

    return find


def forward_chain(first, last, width, inner, down_ref, up_ref, up_start, find):
    count = last - first
    raw = {s: summed_part(down_ref, (s - first) * inner, inner) for s in range(first, last)}
    cross = {
        s: summed_part(up_ref, up_start + (s - first) * inner, inner)
        for s in range(first, last - 1)
    }
    square = summed_part(down_ref, count * inner, LANES)
    square = square[:, 0:1] + square[:, 1:2]
    state, crosses = {}, {}
    for s in range(first, last):
        scale = lax.rsqrt(jnp.maximum(square, 0.0) / width + norm_eps)
        hidden = raw[s] * scale
        gate = jax.nn.sigmoid(hidden)
        act = (hidden * gate).astype(jnp.bfloat16)
        state[s] = (hidden, scale, act)
        if s == last - 1:
            break
        added = {}
        for k in range(first, last - 1):
            if k >= s:
                added[k] = dot(act, find((s, k, False)), ROWS)
            else:
                added[k] = dot(act, find((k, s, False)), LAST)
        wide = act.astype(jnp.float32)
        square = square + jnp.sum(wide * (2.0 * cross[s] + added[s]), axis=1, keepdims=True)
        cross = {k: cross[k] + added[k] for k in cross}
        for t in range(s + 1, last):
            raw[t] = raw[t] + dot(act, find((s, t, True)), ROWS)
        crosses[s + 1] = cross
    return state, crosses


def backward_chain(first, last, width, inner, grad_ref, hidden_of, scale_of, cross_of, find):
    grad_act = {s: summed_part(grad_ref, (s - first) * inner, inner) for s in range(first, last)}
    packs, pulls = {}, {}
    for s in reversed(range(first, last)):
        hidden, scale = hidden_of(s), scale_of(s)
        gate = jax.nn.sigmoid(hidden)
        grad_hidden = grad_act[s] * gate * (1.0 + hidden * (1.0 - gate))
        mean = jnp.sum(grad_hidden * hidden, axis=1, keepdims=True) / width
        packs[s] = (grad_hidden * scale).astype(jnp.bfloat16)
        pulls[s] = mean * scale * scale
        for t in range(first, s):
            grad_act[t] = (
                grad_act[t]
                + dot(packs[s], find((t, s, True)), LAST)
                - pulls[s] * cross_of(s, t)
            )
    return packs, pulls


def kept_crosses(first, last):
    return [(s, t) for s in range(first + 1, last) for t in range(first, s)]


def forward_kernel(first, last, width, inner, copies):
    def kernel(
        down_ref, up_ref, gram_in_ref, gram_out_ref, acts_ref, hidden_ref, scale_ref, cross_ref
    ):
        find = finder(first, last, inner, gram_in_ref, gram_out_ref, 0)
        state, crosses = forward_chain(first, last, width, inner, down_ref, up_ref, 0, find)
        rows = down_ref.shape[1]
        for s in range(first, last):
            hidden, scale, act = state[s]
            at = s - first
            for copy in range(copies):
                acts_ref[copy * rows : (copy + 1) * rows, at * inner : (at + 1) * inner] = act
            hidden_ref[at] = hidden
            scale_ref[at] = jnp.broadcast_to(scale, (rows, LANES))
        for at, (s, t) in enumerate(kept_crosses(first, last)):
            cross_ref[at] = crosses[s][t]

    return kernel


def store_packs(ref, packs, pulls, first, last, inner, rows, copies):
    scalars = scalar_block([pulls[s] for s in range(first, last)])
    for copy in range(copies):
        there = slice(copy * rows, (copy + 1) * rows)
        for s in range(first, last):
            ref[there, (s - first) * inner : (s - first + 1) * inner] = packs[s]
        at = (last - first) * inner
        ref[there, at : at + LANES] = scalars


def backward_kernel(first, last, width, inner, copies):
    kept = {pair: at for at, pair in enumerate(kept_crosses(first, last))}

    def kernel(grad_ref, hidden_ref, scale_ref, cross_ref, gram_ref, out_ref):
        packs, pulls = backward_chain(
            first,
            last,
            width,
            inner,
            grad_ref,
            lambda s: hidden_ref[s - first],
            lambda s: scale_ref[s - first][:, 0:1],
            lambda s, t: cross_ref[kept[(s, t)]],
            finder(first, last, inner, gram_ref, None, 0),
        )
        store_packs(out_ref, packs, pulls, first, last, inner, grad_ref.shape[1], copies)

    return kernel


def turning_kernel(first, last, width, inner, copies):
    def kernel(sums_ref, grad_ref, gram_ref, out_ref):
        count = last - first
        find = finder(first, last, inner, gram_ref, gram_ref, len(down_units(first, last)))
        state, crosses = forward_chain(
            first, last, width, inner, sums_ref, sums_ref, count * inner + LANES, find
        )
        packs, pulls = backward_chain(
            first,
            last,
            width,
            inner,
            grad_ref,
            lambda s: state[s][0],
            lambda s: state[s][1],
            lambda s, t: crosses[s][t],
            find,
        )
        rows = sums_ref.shape[1]
        store_packs(out_ref, packs, pulls, first, last, inner, rows, copies)
        for copy in range(copies):
            for s in range(first, last):
                at = count * inner + LANES + (s - first) * inner
                out_ref[copy * rows : (copy + 1) * rows, at : at + inner] = state[s][2]

    return kernel


def next_rows_kernel(first, last, then, inner, chunk):
    def kernel(rows_ref, acts_ref, in_ref, out_ref, exact_ref, columns_ref):
        exact = rows_ref[...].astype(jnp.float32)
        for s in range(first, last):
            exact = exact + dot(
                part(acts_ref, s - first, inner), part(out_ref, s, chunk), ROWS
            )
        exact_ref[...] = exact
        rows = exact.astype(jnp.bfloat16)
        at = 0
        for s in range(last, then):
            weight = in_ref[(s - last) * chunk : (s - last + 1) * chunk]
            columns_ref[:, at : at + inner] = dot(rows, weight, ROWS).astype(jnp.bfloat16)
            at += inner
        squares = jnp.sum(exact * exact, axis=1, keepdims=True)
        columns_ref[:, at : at + LANES] = scalar_block([squares])
        at += LANES
        for s in range(last, then - 1):
            columns = dot(rows, part(out_ref, s, chunk), LAST)
            columns_ref[:, at : at + inner] = columns.astype(jnp.bfloat16)
            at += inner

    return kernel


def grads_kernel(first, last, before, inner, chunk, n_dp, acts_start):
    group = last - first
    share_in = group * chunk // n_dp
    share_out = inner // n_dp
    lanes_in = inner // LANES
    lanes_out = chunk // LANES

    def kernel(*refs):
        place_ref, exact_ref, packs_ref, acts_ref, up_ref, in_ref, out_ref = refs[:7]
        grads_ref, mine_ref, other_ref, up_new_ref = refs[7:11]
        exact = exact_ref[...].astype(jnp.float32)
        rows = {first: exact.astype(jnp.bfloat16)}

        def act_of(s):
            at = acts_start + (s - first) * inner
            return acts_ref[:, at : at + inner]

        for s in range(first, last - 1):
            exact = exact + dot(act_of(s), part(out_ref, s, chunk), ROWS)
            rows[s + 1] = exact.astype(jnp.bfloat16)
        upstream = up_ref[...].astype(jnp.float32)
        narrow = upstream.astype(jnp.bfloat16)
        for s in reversed(range(first, last)):
            pack = part(packs_ref, s - first, inner)
            at = group * inner + 2 * (s - first)
            pull = packs_ref[:, group * inner : group * inner + LANES].astype(jnp.float32)
            at = 2 * (s - first)
            pull = pull[:, at : at + 1] + pull[:, at + 1 : at + 2]
            into = dot(rows[s], pack, FIRST).astype(jnp.bfloat16)
            onto = dot(act_of(s), narrow, FIRST).astype(jnp.bfloat16)
            base = lanes_in * share_in + (s - first) * lanes_out * share_out

            def store(refs_of, into=into, onto=onto, base=base, s=s):
                for piece in range(chunk // share_in):
                    device = (s - first) * (chunk // share_in) + piece
                    ref = refs_of[device % 2]
                    for c in range(lanes_in):
                        ref[place_ref[device // 2], c * share_in : (c + 1) * share_in] = into[
                            piece * share_in : (piece + 1) * share_in,
                            c * LANES : (c + 1) * LANES,
                        ]
                for device in range(n_dp):
                    ref = refs_of[device % 2]
                    for c in range(lanes_out):
                        row = base + c * share_out
                        ref[place_ref[device // 2], row : row + share_out] = onto[
                            device * share_out : (device + 1) * share_out,
                            c * LANES : (c + 1) * LANES,
                        ]

            @pl.when(place_ref[n_dp // 2] == 0)
            def _():
                store((mine_ref, other_ref))

            @pl.when(place_ref[n_dp // 2] == 1)
            def _():
                store((other_ref, mine_ref))

            weight = in_ref[s * chunk : (s + 1) * chunk]
            upstream = (
                upstream + dot(pack, weight, LAST) - pull * rows[s].astype(jnp.float32)
            )
            narrow = upstream.astype(jnp.bfloat16)
            grads_ref[s - first] = narrow
        up_new_ref[...] = upstream
        if before < first:
            for s in range(before, first):
                columns = dot(narrow, part(out_ref, s, chunk), LAST).astype(jnp.bfloat16)
                refs[11][:, (s - before) * inner : (s - before + 1) * inner] = columns

    return kernel


def unpack_kernel(inner, share_in, sources):
    def kernel(*refs):
        in_ref, out_ref = refs[sources:]
        lanes = inner // LANES

        def total_of(start, stop):
            total = refs[0][start:stop].astype(jnp.float32)
            for ref in refs[1:sources]:
                total = total + ref[start:stop].astype(jnp.float32)
            return total.astype(jnp.bfloat16)

        for c in range(lanes):
            in_ref[:, c * LANES : (c + 1) * LANES] = total_of(c * share_in, (c + 1) * share_in)
        out_ref[...] = total_of(lanes * share_in, refs[0].shape[0])

    return kernel


def adam_kernel(share, lanes, share_in):
    def kernel(*refs):
        swapped_ref, one_ref, two_ref, onto_ref = refs[:4]
        state_in, state_out = refs[4:7], refs[7:10]
        new_in, new_out, pieces_ref = refs[10:13], refs[13:16], refs[16]
        per = LANES // share
        for c in range(one_ref.shape[1] // LANES):
            there = slice(c * LANES, (c + 1) * LANES)
            one = one_ref[:, there].astype(jnp.float32)
            two = two_ref[:, there].astype(jnp.float32)
            swapped = swapped_ref[0] == 1
            grad = jnp.concatenate(
                [jnp.where(swapped, two, one), jnp.where(swapped, one, two)], axis=0
            )
            results = adam_update(*(ref[:, there] for ref in state_in), grad)
            for ref, value in zip(new_in, results):
                ref[:, there] = value
            turned = results[0].T.astype(jnp.bfloat16)
            for q in range(per):
                pieces_ref[c * per + q, 0] = turned[q * share : (q + 1) * share]
        for device in range(onto_ref.shape[0]):
            for c in range(lanes):
                at = (device * lanes + c) * LANES
                grad = onto_ref[device, c * share : (c + 1) * share].astype(jnp.float32)
                results = adam_update(*(ref[:, at : at + LANES] for ref in state_out), grad)
                for ref, value in zip(new_out, results):
                    ref[:, at : at + LANES] = value
        for device in range(pieces_ref.shape[0]):
            at = device * share_in
            start = at // LANES * LANES
            stop = -(-(at + share_in) // LANES) * LANES
            values = new_out[0][:, start:stop][:, at - start : at - start + share_in]
            pieces_ref[device, 1] = values.astype(jnp.bfloat16)

    return kernel


def rollout_kernel(share, share_in):
    def kernel(pieces_ref, in_ref, out_ref):
        per = LANES // share
        for pair in range(pieces_ref.shape[0] // 2):
            both = [pieces_ref[2 * pair + h, 0].astype(jnp.float32) for h in range(2)]
            at = 2 * pair * share_in
            in_ref[:, at : at + 2 * share_in] = jnp.concatenate(both, axis=1).astype(jnp.bfloat16)
        for c in range(pieces_ref.shape[0] // per):
            rows = [pieces_ref[c * per + q, 1].astype(jnp.float32) for q in range(per)]
            out_ref[:, c * LANES : (c + 1) * LANES] = jnp.concatenate(rows, axis=0).T.astype(
                jnp.bfloat16
            )

    return kernel


def columns_kernel(orders):
    def kernel(every_ref, *out_refs):
        size = every_ref.shape[2]
        for out_ref, order in zip(out_refs, orders):
            for at, unit in enumerate(order):
                out_ref[:, at * size : (at + 1) * size] = every_ref[unit]

    return kernel


def other_core(x, n_dp):
    return lax.ppermute(x, "dp", [(j, j + 1 - 2 * (j % 2)) for j in range(n_dp)])


def add_kernel(mine_ref, other_ref, *out_refs):
    for at, out_ref in enumerate(out_refs):
        total = mine_ref[at].astype(jnp.float32) + other_ref[at].astype(jnp.float32)
        out_ref[...] = total.astype(jnp.bfloat16)


def chip_steps(n_dp):
    return [(dx, dz) for dx in range(n_dp // 4) for dz in range(2)]


def between_chips(blocks, n_dp):
    arrived = [blocks[0]]
    for (dx, dz), block in list(zip(chip_steps(n_dp), blocks))[1:]:
        pairs = []
        for j in range(n_dp):
            x, z, core = j // 4, j // 2 % 2, j % 2
            pairs.append((j, (x + dx) % (n_dp // 4) * 4 + (z ^ dz) * 2 + core))
        arrived.append(lax.ppermute(block, "dp", pairs))
    return arrived


def reduce_apart(mine, n_dp):
    summed = lax.psum_scatter(
        mine.reshape(-1, LANES),
        "dp",
        scatter_dimension=0,
        tiled=True,
        axis_index_groups=[list(range(c, n_dp, 2)) for c in range(2)],
    )
    return [summed]


def move_in(low, high, n_pipe, n_dp):
    odd = lax.axis_index("dp") % 2 == 1
    group = n_pipe // 2
    moved = []
    for q in range(2):
        pairs = []
        for i in range(n_pipe):
            for j in range(n_dp):
                section = j * group // n_dp + (0 if j % 2 == q else group)
                pairs.append((i * n_dp + j, section * n_dp + 2 * i + j // 2 % 2))
        payload = jnp.where(odd, low, high) if q == 1 else jnp.where(odd, high, low)
        moved.append(lax.ppermute(payload, ("pipe", "dp"), pairs))
    return moved


def on_device(
    inputs_x, cotangent, master_in, master_out, moment_in, moment_out, second_in, second_out
):
    n_pipe = lax.axis_size("pipe")
    n_dp = lax.axis_size("dp")
    me = lax.axis_index("pipe")
    tok_rows, width = inputs_x.shape
    chunk = width // n_pipe
    inner = master_in.shape[2]
    share_in = master_in.shape[1]
    share_out = master_out.shape[1]
    block = tok_rows // n_pipe

    own_in = master_in[0].astype(jnp.bfloat16)
    own_out = master_out[0].astype(jnp.bfloat16)
    pairs = [
        (s * n_dp + 2 * i + h, i * n_dp + 2 * s + h)
        for s in range(n_pipe)
        for i in range(n_pipe)
        for h in range(2)
    ]
    piece_in = lax.ppermute(own_in, ("pipe", "dp"), pairs)
    piece_out = swap(own_out.reshape(share_out, n_pipe, chunk).transpose(1, 0, 2), "pipe")
    flat_out = piece_out.transpose(1, 0, 2).reshape(share_out, width)
    all_in = lax.all_gather(piece_in, "dp", axis=0, tiled=True)
    all_out = lax.all_gather(flat_out, "dp", axis=0, tiled=True)
    weight_in = [all_in[s * chunk : (s + 1) * chunk] for s in range(n_pipe)]

    def products(down, blocks):
        units, partial, orders = [], [], []
        for first, last in blocks:
            wanted = (down_units if down else up_units)(first, last)
            for t in sorted({t for _, t, _ in wanted}):
                ks = [k for k, other, _ in wanted if other == t]
                left = piece_out[ks[0] : ks[-1] + 1].reshape(-1, chunk)
                if down:
                    partial.append(dot(left, weight_in[t], ROWS))
                else:
                    partial.append(dot(left, weight_out[t], LAST))
                units += [(k, t, down) for k in ks]
        for first, last in blocks:
            wanted = (down_units if down else up_units)(first, last)
            orders.append([units.index(unit) for unit in wanted])
        padded = -(-len(units) // n_pipe) * n_pipe
        partial = [p.astype(jnp.bfloat16) for p in partial]
        if padded > len(units):
            partial.append(jnp.zeros(((padded - len(units)) * share_out, inner), jnp.bfloat16))
        arrived = swap(jnp.concatenate(partial, axis=0), "pipe")
        arrived = arrived.reshape(n_pipe, -1, inner)
        mine = jnp.sum(arrived.astype(jnp.float32), axis=0).astype(jnp.bfloat16)
        every = swap(jnp.tile(mine, (n_pipe, 1)), "pipe").reshape(padded, share_out, inner)
        shapes = [((share_out, len(order) * inner), jnp.bfloat16) for order in orders]
        return run(columns_kernel(orders), shapes, every)

    def over_dp(columns):
        return lax.all_gather(columns, "dp", axis=0, tiled=True)

    rows = lax.dynamic_slice_in_dim(inputs_x, me * chunk, chunk, 1)
    seed = lax.dynamic_slice_in_dim(cotangent, me * chunk, chunk, 1)

    (first, middle), (_, last) = BLOCKS
    count = middle - first
    wide = rows.astype(jnp.float32)
    down = [dot(rows, weight_in[s], ROWS) for s in range(first, middle)]
    down += split_scalars([jnp.sum(wide * wide, axis=1, keepdims=True)])
    down = exchanged(down, n_pipe)
    (down_low,) = products(True, BLOCKS[:1])
    all_out, down, down_low = lax.optimization_barrier((all_out, down, down_low))
    weight_out = [all_out[:, s * chunk : (s + 1) * chunk] for s in range(n_pipe)]
    gram_in_low = over_dp(down_low)
    up_low, up_high = products(False, BLOCKS)
    gram_out_low = over_dp(up_low)
    held_in, up_low = lax.optimization_barrier((all_in, up_low))
    weight_in = [held_in[s * chunk : (s + 1) * chunk] for s in range(n_pipe)]
    (down_high,) = products(True, BLOCKS[1:])
    up = exchanged([dot(rows, weight_out[s], LAST) for s in range(first, middle - 1)], n_pipe)
    gram_in_low, gram_out_low, up, columns = lax.optimization_barrier(
        (gram_in_low, gram_out_low, up, jnp.concatenate([down_high, up_high], axis=1))
    )
    gram_high = over_dp(columns)

    kept = len(kept_crosses(first, middle))
    acts, hidden, scale, cross = run(
        forward_kernel(first, middle, width, inner, n_pipe),
        [
            ((tok_rows, count * inner), jnp.bfloat16),
            ((count, block, inner), jnp.float32),
            ((count, block, LANES), jnp.float32),
            ((kept, block, inner), jnp.float32),
        ],
        down,
        up,
        gram_in_low,
        gram_out_low,
    )
    late, acts = lax.optimization_barrier((seed, acts))
    acts = swap(acts, "pipe")
    exact, columns = run(
        next_rows_kernel(first, middle, last, inner, chunk),
        [
            ((tok_rows, chunk), jnp.float32),
            ((tok_rows, (2 * (last - middle) - 1) * inner + LANES), jnp.bfloat16),
        ],
        rows,
        acts,
        all_in,
        all_out,
        specs={
            2: pl.BlockSpec(
                ((last - middle) * chunk, inner), lambda step: (middle // (last - middle), 0)
            )
        },
    )
    sums = exchanged(columns, n_pipe)
    grad_high = exchanged([dot(late, weight_out[s], LAST) for s in range(middle, last)], n_pipe)

    turned = run(
        turning_kernel(middle, last, width, inner, n_pipe),
        [((tok_rows, 2 * (last - middle) * inner + LANES), jnp.bfloat16)],
        sums,
        grad_high,
        gram_high,
    )[0]
    turned = swap(turned, "pipe")

    def packed_shape(group):
        rows_packed = 2 * group * chunk * inner // (n_dp * LANES)
        return (n_dp // 2, rows_packed, LANES)

    dp = lax.axis_index("dp")
    core, chip = dp % 2, dp // 2
    chips = jnp.arange(n_dp // 2)
    xs = n_dp // 4
    away = (chips // 2 - chip // 2 + xs) % xs * 2 + (chips % 2 + chip % 2) % 2
    fixed = jnp.concatenate([chips, core[None]]).astype(jnp.int32)
    place = jnp.concatenate([away, core[None]]).astype(jnp.int32)
    in_smem = {0: pl.BlockSpec(memory_space=pltpu.SMEM)}

    grads_high, mine, other, upstream, columns = run(
        grads_kernel(middle, last, first, inner, chunk, n_dp, (last - middle) * inner + LANES),
        [
            ((last - middle, tok_rows, chunk), jnp.bfloat16),
            (packed_shape(last - middle), jnp.bfloat16),
            (packed_shape(last - middle), jnp.bfloat16),
            ((tok_rows, chunk), jnp.float32),
            ((tok_rows, count * inner), jnp.bfloat16),
        ],
        fixed,
        exact,
        turned,
        turned,
        seed,
        all_in,
        all_out,
        specs=in_smem,
    )
    grad_low = exchanged(columns, n_pipe)
    other = other_core(other, n_dp)
    mine = (mine.astype(jnp.float32) + other.astype(jnp.float32)).astype(jnp.bfloat16)
    grad_low, mine = lax.optimization_barrier((grad_low, mine))
    arrived_high = reduce_apart(mine, n_dp)

    packs = run(
        backward_kernel(first, middle, width, inner, n_pipe),
        [((tok_rows, count * inner + LANES), jnp.bfloat16)],
        grad_low,
        hidden,
        scale,
        cross,
        gram_in_low,
    )[0]
    packs = swap(packs, "pipe")
    grads_low, mine, other, _ = run(
        grads_kernel(first, middle, first, inner, chunk, n_dp, 0),
        [
            ((count, tok_rows, chunk), jnp.bfloat16),
            (packed_shape(count), jnp.bfloat16),
            (packed_shape(count), jnp.bfloat16),
            ((tok_rows, chunk), jnp.float32),
        ],
        place,
        rows,
        packs,
        acts,
        upstream,
        all_in,
        all_out,
        specs=in_smem,
    )
    blocks = run(
        add_kernel,
        [(mine.shape[1:], jnp.bfloat16)] * mine.shape[0],
        mine,
        other_core(other, n_dp),
    )
    arrived_low = between_chips(blocks, n_dp)

    input_grads = swap(jnp.concatenate([grads_low, grads_high], axis=0), "pipe")
    input_grads, arrived_low = lax.optimization_barrier((input_grads, arrived_low))
    input_grads = input_grads.transpose(1, 0, 2).reshape(1, tok_rows, width)

    ins, outs = [], []
    for (low, high), arrived in zip(BLOCKS, (arrived_low, arrived_high)):
        share = (high - low) * chunk // n_dp
        sum_in, sum_out = run(
            unpack_kernel(inner, share, len(arrived)),
            [
                ((share, inner), jnp.bfloat16),
                ((arrived[0].shape[0] - share * inner // LANES, LANES), jnp.bfloat16),
            ],
            *arrived,
        )
        ins.append(sum_in)
        outs.append(sum_out.reshape(high - low, -1, LANES))
    grad_out = swap(jnp.concatenate(outs, axis=0), "pipe")
    grad_in = move_in(*ins, n_pipe, n_dp)
    is_high = (me >= middle).astype(jnp.int32).reshape(1)

    shape_in, shape_out = (share_in, inner), (share_out, width)
    *updated, pieces = run(
        adam_kernel(share_out, chunk // LANES, share_in),
        [(shape_in, jnp.float32)] * 3
        + [(shape_out, jnp.float32)] * 3
        + [((n_dp, 2, share_out, share_in), jnp.bfloat16)],
        is_high,
        *grad_in,
        grad_out,
        master_in[0],
        moment_in[0],
        second_in[0],
        master_out[0],
        moment_out[0],
        second_out[0],
        specs=in_smem,
    )
    new_in, new_moment_in, new_second_in, new_out, new_moment_out, new_second_out = updated
    roll_in, roll_out = run(
        rollout_kernel(share_out, share_in),
        [(shape_out, jnp.bfloat16), (shape_in, jnp.bfloat16)],
        swap(pieces, "dp"),
    )
    return (
        input_grads,
        new_in[None],
        new_moment_in[None],
        new_second_in[None],
        new_out[None],
        new_moment_out[None],
        new_second_out[None],
        roll_in[None],
        roll_out[None],
    )


def solution(mesh):
    in_specs = (P("dp", None), P("dp", None)) + (P("pipe", "dp", None),) * 6
    out_specs = (P("pipe", "dp", None),) * 9
    return jax.shard_map(
        on_device, mesh=mesh, in_specs=in_specs, out_specs=out_specs, check_vma=False
    )
```

```python
import jax
import jax.numpy as jnp
from jax import lax
from jax.experimental import pallas as pl
from jax.experimental.pallas import tpu as pltpu
from jax.sharding import PartitionSpec as P

norm_eps = 1e-06
beta_one = 0.9
beta_two = 0.999
learn_rate = 0.02
decay_rate = 0.1
adam_eps = 1e-08
adam_step = 100

BLOCKS = ((0, 4), (4, 8))
LANES = 128
VMEM_BYTES = 48 * 1024 * 1024


def dot(left, right, dims):
    return lax.dot_general(left, right, (dims, ((), ())), preferred_element_type=jnp.float32)


ROWS = ((1,), (0,))
LAST = ((1,), (1,))
FIRST = ((0,), (0,))


def swap(x, axis):
    return lax.all_to_all(x, axis, 0, 0, tiled=True)


def split_scalars(scalars):
    columns = []
    for value in scalars:
        high = value.astype(jnp.bfloat16)
        columns += [high, (value - high.astype(jnp.float32)).astype(jnp.bfloat16)]
    columns.append(jnp.zeros((scalars[0].shape[0], 128 - len(columns)), jnp.bfloat16))
    return columns


def exchanged(columns, count):
    packed = columns
    if isinstance(columns, list):
        packed = jnp.concatenate([c.astype(jnp.bfloat16) for c in columns], axis=1)
    return swap(packed, "pipe").reshape(count, packed.shape[0] // count, packed.shape[1])


def adam_update(master, moment, second, grad):
    moment_new = beta_one * moment + (1.0 - beta_one) * grad
    second_new = beta_two * second + (1.0 - beta_two) * grad * grad
    moment_hat = moment_new / (1.0 - beta_one**adam_step)
    second_hat = second_new / (1.0 - beta_two**adam_step)
    master_new = master - learn_rate * (
        moment_hat / (jnp.sqrt(second_hat) + adam_eps) + decay_rate * master
    )
    return (master_new, moment_new, second_new)


def run(kernel, shapes, *operands, specs=None):
    more = {}
    if specs is not None:
        whole = [pl.BlockSpec(x.shape, zeros_map(x.ndim)) for x in operands]
        outs = [pl.BlockSpec(shape, zeros_map(len(shape))) for shape, _ in shapes]
        given = [specs.get(at, spec) for at, spec in enumerate(whole)]
        more = {"grid": (1,), "in_specs": given, "out_specs": outs}
    return pl.pallas_call(
        kernel,
        out_shape=[jax.ShapeDtypeStruct(shape, kind) for shape, kind in shapes],
        compiler_params=pltpu.CompilerParams(vmem_limit_bytes=VMEM_BYTES),
        **more,
    )(*operands)


def zeros_map(ndim):
    return lambda step: (0,) * ndim


def part(ref, at, inner):
    return ref[:, at * inner : (at + 1) * inner]


def scalar_block(scalars):
    lane = lax.broadcasted_iota(jnp.int32, (scalars[0].shape[0], LANES), 1)
    packed = jnp.zeros(lane.shape, jnp.float32)
    for at, value in enumerate(scalars):
        high = value.astype(jnp.bfloat16).astype(jnp.float32)
        packed = jnp.where(lane == 2 * at, high, packed)
        packed = jnp.where(lane == 2 * at + 1, value - high, packed)
    return packed.astype(jnp.bfloat16)


def summed_part(ref, start, size):
    total = ref[0, :, start : start + size].astype(jnp.float32)
    for source in range(1, ref.shape[0]):
        total = total + ref[source, :, start : start + size].astype(jnp.float32)
    return total


def down_units(first, last):
    return [(j, t, True) for j in range(first, last) for t in range(j + 1, last)]


def up_units(first, last):
    return [(j, t, False) for j in range(first, last - 1) for t in range(j, last - 1)]


def finder(first, last, inner, down_ref, up_ref, up_start):
    places = {unit: (down_ref, at) for at, unit in enumerate(down_units(first, last))}
    if up_ref is not None:
        for at, unit in enumerate(up_units(first, last)):
            places[unit] = (up_ref, up_start + at)

    def find(unit):
        ref, at = places[unit]
        return part(ref, at, inner)

    return find


def forward_chain(first, last, width, inner, down_ref, up_ref, up_start, find):
    count = last - first
    raw = {s: summed_part(down_ref, (s - first) * inner, inner) for s in range(first, last)}
    cross = {
        s: summed_part(up_ref, up_start + (s - first) * inner, inner)
        for s in range(first, last - 1)
    }
    square = summed_part(down_ref, count * inner, LANES)
    square = square[:, 0:1] + square[:, 1:2]
    state, crosses = {}, {}
    for s in range(first, last):
        scale = lax.rsqrt(jnp.maximum(square, 0.0) / width + norm_eps)
        hidden = raw[s] * scale
        gate = jax.nn.sigmoid(hidden)
        act = (hidden * gate).astype(jnp.bfloat16)
        state[s] = (hidden, scale, act)
        if s == last - 1:
            break
        added = {}
        for k in range(first, last - 1):
            if k >= s:
                added[k] = dot(act, find((s, k, False)), ROWS)
            else:
                added[k] = dot(act, find((k, s, False)), LAST)
        wide = act.astype(jnp.float32)
        square = square + jnp.sum(wide * (2.0 * cross[s] + added[s]), axis=1, keepdims=True)
        cross = {k: cross[k] + added[k] for k in cross}
        for t in range(s + 1, last):
            raw[t] = raw[t] + dot(act, find((s, t, True)), ROWS)
        crosses[s + 1] = cross
    return state, crosses


def backward_chain(first, last, width, inner, grad_ref, hidden_of, scale_of, cross_of, find):
    grad_act = {s: summed_part(grad_ref, (s - first) * inner, inner) for s in range(first, last)}
    packs, pulls = {}, {}
    for s in reversed(range(first, last)):
        hidden, scale = hidden_of(s), scale_of(s)
        gate = jax.nn.sigmoid(hidden)
        grad_hidden = grad_act[s] * gate * (1.0 + hidden * (1.0 - gate))
        mean = jnp.sum(grad_hidden * hidden, axis=1, keepdims=True) / width
        packs[s] = (grad_hidden * scale).astype(jnp.bfloat16)
        pulls[s] = mean * scale * scale
        for t in range(first, s):
            grad_act[t] = (
                grad_act[t]
                + dot(packs[s], find((t, s, True)), LAST)
                - pulls[s] * cross_of(s, t)
            )
    return packs, pulls


def kept_crosses(first, last):
    return [(s, t) for s in range(first + 1, last) for t in range(first, s)]


def forward_kernel(first, last, width, inner, copies):
    def kernel(
        down_ref, up_ref, gram_in_ref, gram_out_ref, acts_ref, hidden_ref, scale_ref, cross_ref
    ):
        find = finder(first, last, inner, gram_in_ref, gram_out_ref, 0)
        state, crosses = forward_chain(first, last, width, inner, down_ref, up_ref, 0, find)
        rows = down_ref.shape[1]
        for s in range(first, last):
            hidden, scale, act = state[s]
            at = s - first
            for copy in range(copies):
                acts_ref[copy * rows : (copy + 1) * rows, at * inner : (at + 1) * inner] = act
            hidden_ref[at] = hidden
            scale_ref[at] = jnp.broadcast_to(scale, (rows, LANES))
        for at, (s, t) in enumerate(kept_crosses(first, last)):
            cross_ref[at] = crosses[s][t]

    return kernel


def store_packs(ref, packs, pulls, first, last, inner, rows, copies):
    scalars = scalar_block([pulls[s] for s in range(first, last)])
    for copy in range(copies):
        there = slice(copy * rows, (copy + 1) * rows)
        for s in range(first, last):
            ref[there, (s - first) * inner : (s - first + 1) * inner] = packs[s]
        at = (last - first) * inner
        ref[there, at : at + LANES] = scalars


def backward_kernel(first, last, width, inner, copies):
    kept = {pair: at for at, pair in enumerate(kept_crosses(first, last))}

    def kernel(grad_ref, hidden_ref, scale_ref, cross_ref, gram_ref, out_ref):
        packs, pulls = backward_chain(
            first,
            last,
            width,
            inner,
            grad_ref,
            lambda s: hidden_ref[s - first],
            lambda s: scale_ref[s - first][:, 0:1],
            lambda s, t: cross_ref[kept[(s, t)]],
            finder(first, last, inner, gram_ref, None, 0),
        )
        store_packs(out_ref, packs, pulls, first, last, inner, grad_ref.shape[1], copies)

    return kernel


def turning_kernel(first, last, width, inner, copies):
    def kernel(sums_ref, grad_ref, gram_ref, out_ref):
        count = last - first
        find = finder(first, last, inner, gram_ref, gram_ref, len(down_units(first, last)))
        state, crosses = forward_chain(
            first, last, width, inner, sums_ref, sums_ref, count * inner + LANES, find
        )
        packs, pulls = backward_chain(
            first,
            last,
            width,
            inner,
            grad_ref,
            lambda s: state[s][0],
            lambda s: state[s][1],
            lambda s, t: crosses[s][t],
            find,
        )
        rows = sums_ref.shape[1]
        store_packs(out_ref, packs, pulls, first, last, inner, rows, copies)
        for copy in range(copies):
            for s in range(first, last):
                at = count * inner + LANES + (s - first) * inner
                out_ref[copy * rows : (copy + 1) * rows, at : at + inner] = state[s][2]

    return kernel


def next_rows_kernel(first, last, then, inner, chunk):
    def kernel(rows_ref, acts_ref, in_ref, out_ref, exact_ref, columns_ref):
        exact = rows_ref[...].astype(jnp.float32)
        for s in range(first, last):
            exact = exact + dot(
                part(acts_ref, s - first, inner), part(out_ref, s, chunk), ROWS
            )
        exact_ref[...] = exact
        rows = exact.astype(jnp.bfloat16)
        at = 0
        for s in range(last, then):
            weight = in_ref[(s - last) * chunk : (s - last + 1) * chunk]
            columns_ref[:, at : at + inner] = dot(rows, weight, ROWS).astype(jnp.bfloat16)
            at += inner
        squares = jnp.sum(exact * exact, axis=1, keepdims=True)
        columns_ref[:, at : at + LANES] = scalar_block([squares])
        at += LANES
        for s in range(last, then - 1):
            columns = dot(rows, part(out_ref, s, chunk), LAST)
            columns_ref[:, at : at + inner] = columns.astype(jnp.bfloat16)
            at += inner

    return kernel


def grads_kernel(first, last, before, inner, chunk, n_dp, acts_start):
    group = last - first
    share_in = group * chunk // n_dp
    share_out = inner // n_dp
    lanes_in = inner // LANES
    lanes_out = chunk // LANES

    def kernel(*refs):
        place_ref, exact_ref, packs_ref, acts_ref, up_ref, in_ref, out_ref = refs[:7]
        grads_ref, mine_ref, other_ref, up_new_ref = refs[7:11]
        exact = exact_ref[...].astype(jnp.float32)
        rows = {first: exact.astype(jnp.bfloat16)}

        def act_of(s):
            at = acts_start + (s - first) * inner
            return acts_ref[:, at : at + inner]

        for s in range(first, last - 1):
            exact = exact + dot(act_of(s), part(out_ref, s, chunk), ROWS)
            rows[s + 1] = exact.astype(jnp.bfloat16)
        upstream = up_ref[...].astype(jnp.float32)
        narrow = upstream.astype(jnp.bfloat16)
        for s in reversed(range(first, last)):
            pack = part(packs_ref, s - first, inner)
            at = group * inner + 2 * (s - first)
            pull = packs_ref[:, group * inner : group * inner + LANES].astype(jnp.float32)
            at = 2 * (s - first)
            pull = pull[:, at : at + 1] + pull[:, at + 1 : at + 2]
            into = dot(rows[s], pack, FIRST).astype(jnp.bfloat16)
            onto = dot(act_of(s), narrow, FIRST).astype(jnp.bfloat16)
            base = lanes_in * share_in + (s - first) * lanes_out * share_out

            def store(refs_of, into=into, onto=onto, base=base, s=s):
                for piece in range(chunk // share_in):
                    device = (s - first) * (chunk // share_in) + piece
                    ref = refs_of[device % 2]
                    for c in range(lanes_in):
                        ref[place_ref[device // 2], c * share_in : (c + 1) * share_in] = into[
                            piece * share_in : (piece + 1) * share_in,
                            c * LANES : (c + 1) * LANES,
                        ]
                for device in range(n_dp):
                    ref = refs_of[device % 2]
                    for c in range(lanes_out):
                        row = base + c * share_out
                        ref[place_ref[device // 2], row : row + share_out] = onto[
                            device * share_out : (device + 1) * share_out,
                            c * LANES : (c + 1) * LANES,
                        ]

            @pl.when(place_ref[n_dp // 2] == 0)
            def _():
                store((mine_ref, other_ref))

            @pl.when(place_ref[n_dp // 2] == 1)
            def _():
                store((other_ref, mine_ref))

            weight = in_ref[s * chunk : (s + 1) * chunk]
            upstream = (
                upstream + dot(pack, weight, LAST) - pull * rows[s].astype(jnp.float32)
            )
            narrow = upstream.astype(jnp.bfloat16)
            grads_ref[s - first] = narrow
        up_new_ref[...] = upstream
        if before < first:
            for s in range(before, first):
                columns = dot(narrow, part(out_ref, s, chunk), LAST).astype(jnp.bfloat16)
                refs[11][:, (s - before) * inner : (s - before + 1) * inner] = columns

    return kernel


def unpack_kernel(inner, share_in, sources):
    def kernel(*refs):
        in_ref, out_ref = refs[sources:]
        given = refs[:sources]
        if sources == 1:
            given = [refs[0].at[k] for k in range(refs[0].shape[0])]
        lanes = inner // LANES

        def total_of(start, stop):
            total = given[0][start:stop].astype(jnp.float32)
            for ref in given[1:]:
                total = total + ref[start:stop].astype(jnp.float32)
            return total.astype(jnp.bfloat16)

        for c in range(lanes):
            in_ref[:, c * LANES : (c + 1) * LANES] = total_of(c * share_in, (c + 1) * share_in)
        out_ref[...] = total_of(lanes * share_in, given[0].shape[0])

    return kernel


def adam_kernel(share, lanes, share_in):
    def kernel(*refs):
        swapped_ref, one_ref, two_ref, onto_ref = refs[:4]
        state_in, state_out = refs[4:7], refs[7:10]
        new_in, new_out, pieces_ref = refs[10:13], refs[13:16], refs[16]
        per = LANES // share
        for c in range(one_ref.shape[1] // LANES):
            there = slice(c * LANES, (c + 1) * LANES)
            one = one_ref[:, there].astype(jnp.float32)
            two = two_ref[:, there].astype(jnp.float32)
            swapped = swapped_ref[0] == 1
            grad = jnp.concatenate(
                [jnp.where(swapped, two, one), jnp.where(swapped, one, two)], axis=0
            )
            results = adam_update(*(ref[:, there] for ref in state_in), grad)
            for ref, value in zip(new_in, results):
                ref[:, there] = value
            turned = results[0].T.astype(jnp.bfloat16)
            for q in range(per):
                pieces_ref[c * per + q, 0] = turned[q * share : (q + 1) * share]
        for device in range(onto_ref.shape[0]):
            for c in range(lanes):
                at = (device * lanes + c) * LANES
                grad = onto_ref[device, c * share : (c + 1) * share].astype(jnp.float32)
                results = adam_update(*(ref[:, at : at + LANES] for ref in state_out), grad)
                for ref, value in zip(new_out, results):
                    ref[:, at : at + LANES] = value
        for device in range(pieces_ref.shape[0]):
            at = device * share_in
            start = at // LANES * LANES
            stop = -(-(at + share_in) // LANES) * LANES
            values = new_out[0][:, start:stop][:, at - start : at - start + share_in]
            pieces_ref[device, 1] = values.astype(jnp.bfloat16)

    return kernel


def rollout_kernel(share, share_in):
    def kernel(pieces_ref, in_ref, out_ref):
        per = LANES // share
        for pair in range(pieces_ref.shape[0] // 2):
            both = [pieces_ref[2 * pair + h, 0].astype(jnp.float32) for h in range(2)]
            at = 2 * pair * share_in
            in_ref[:, at : at + 2 * share_in] = jnp.concatenate(both, axis=1).astype(jnp.bfloat16)
        for c in range(pieces_ref.shape[0] // per):
            rows = [pieces_ref[c * per + q, 1].astype(jnp.float32) for q in range(per)]
            out_ref[:, c * LANES : (c + 1) * LANES] = jnp.concatenate(rows, axis=0).T.astype(
                jnp.bfloat16
            )

    return kernel


def columns_kernel(orders):
    def kernel(every_ref, *out_refs):
        size = every_ref.shape[2]
        for out_ref, order in zip(out_refs, orders):
            for at, unit in enumerate(order):
                out_ref[:, at * size : (at + 1) * size] = every_ref[unit]

    return kernel


def other_core(x, n_dp):
    return lax.ppermute(x, "dp", [(j, j + 1 - 2 * (j % 2)) for j in range(n_dp)])


def add_kernel(mine_ref, other_ref, *out_refs):
    for at in range(mine_ref.shape[0]):
        total = mine_ref[at].astype(jnp.float32) + other_ref[at].astype(jnp.float32)
        if len(out_refs) == 1:
            out_refs[0][at] = total.astype(jnp.bfloat16)
        else:
            out_refs[at][...] = total.astype(jnp.bfloat16)


def added(mine, other, count):
    shape = mine.shape if count == 1 else mine.shape[1:]
    return run(add_kernel, [(shape, jnp.bfloat16)] * count, mine, other)


def chip_steps(n_dp):
    return [(dx, dz) for dx in range(n_dp // 4) for dz in range(2)]


def between_chips(blocks, n_dp):
    arrived = [blocks[0]]
    for (dx, dz), block in list(zip(chip_steps(n_dp), blocks))[1:]:
        pairs = []
        for j in range(n_dp):
            x, z, core = j // 4, j // 2 % 2, j % 2
            pairs.append((j, (x + dx) % (n_dp // 4) * 4 + (z ^ dz) * 2 + core))
        arrived.append(lax.ppermute(block, "dp", pairs))
    return arrived


def move_in(low, high, n_pipe, n_dp):
    odd = lax.axis_index("dp") % 2 == 1
    group = n_pipe // 2
    moved = []
    for q in range(2):
        pairs = []
        for i in range(n_pipe):
            for j in range(n_dp):
                section = j * group // n_dp + (0 if j % 2 == q else group)
                pairs.append((i * n_dp + j, section * n_dp + 2 * i + j // 2 % 2))
        payload = jnp.where(odd, low, high) if q == 1 else jnp.where(odd, high, low)
        moved.append(lax.ppermute(payload, ("pipe", "dp"), pairs))
    return moved


def on_device(
    inputs_x, cotangent, master_in, master_out, moment_in, moment_out, second_in, second_out
):
    n_pipe = lax.axis_size("pipe")
    n_dp = lax.axis_size("dp")
    me = lax.axis_index("pipe")
    tok_rows, width = inputs_x.shape
    chunk = width // n_pipe
    inner = master_in.shape[2]
    share_in = master_in.shape[1]
    share_out = master_out.shape[1]
    block = tok_rows // n_pipe

    own_in = master_in[0].astype(jnp.bfloat16)
    own_out = master_out[0].astype(jnp.bfloat16)
    pairs = [
        (s * n_dp + 2 * i + h, i * n_dp + 2 * s + h)
        for s in range(n_pipe)
        for i in range(n_pipe)
        for h in range(2)
    ]
    piece_in = lax.ppermute(own_in, ("pipe", "dp"), pairs)
    piece_out = swap(own_out.reshape(share_out, n_pipe, chunk).transpose(1, 0, 2), "pipe")
    flat_out = piece_out.transpose(1, 0, 2).reshape(share_out, width)
    all_in = lax.all_gather(piece_in, "dp", axis=0, tiled=True)
    all_out = lax.all_gather(flat_out, "dp", axis=0, tiled=True)
    weight_in = [all_in[s * chunk : (s + 1) * chunk] for s in range(n_pipe)]

    def products(down, blocks):
        units, partial, orders = [], [], []
        for first, last in blocks:
            wanted = (down_units if down else up_units)(first, last)
            for t in sorted({t for _, t, _ in wanted}):
                ks = [k for k, other, _ in wanted if other == t]
                left = piece_out[ks[0] : ks[-1] + 1].reshape(-1, chunk)
                if down:
                    partial.append(dot(left, weight_in[t], ROWS))
                else:
                    partial.append(dot(left, weight_out[t], LAST))
                units += [(k, t, down) for k in ks]
        for first, last in blocks:
            wanted = (down_units if down else up_units)(first, last)
            orders.append([units.index(unit) for unit in wanted])
        padded = -(-len(units) // n_pipe) * n_pipe
        partial = [p.astype(jnp.bfloat16) for p in partial]
        if padded > len(units):
            partial.append(jnp.zeros(((padded - len(units)) * share_out, inner), jnp.bfloat16))
        arrived = swap(jnp.concatenate(partial, axis=0), "pipe")
        arrived = arrived.reshape(n_pipe, -1, inner)
        mine = jnp.sum(arrived.astype(jnp.float32), axis=0).astype(jnp.bfloat16)
        every = swap(jnp.tile(mine, (n_pipe, 1)), "pipe").reshape(padded, share_out, inner)
        shapes = [((share_out, len(order) * inner), jnp.bfloat16) for order in orders]
        return run(columns_kernel(orders), shapes, every)

    def over_dp(columns):
        return lax.all_gather(columns, "dp", axis=0, tiled=True)

    rows = lax.dynamic_slice_in_dim(inputs_x, me * chunk, chunk, 1)
    seed = lax.dynamic_slice_in_dim(cotangent, me * chunk, chunk, 1)

    (first, middle), (_, last) = BLOCKS
    count = middle - first
    wide = rows.astype(jnp.float32)
    down = [dot(rows, weight_in[s], ROWS) for s in range(first, middle)]
    down += split_scalars([jnp.sum(wide * wide, axis=1, keepdims=True)])
    down = exchanged(down, n_pipe)
    (down_low,) = products(True, BLOCKS[:1])
    all_out, down, down_low = lax.optimization_barrier((all_out, down, down_low))
    weight_out = [all_out[:, s * chunk : (s + 1) * chunk] for s in range(n_pipe)]
    gram_in_low = over_dp(down_low)
    up_low, up_high = products(False, BLOCKS)
    gram_out_low = over_dp(up_low)
    held_in, up_low = lax.optimization_barrier((all_in, up_low))
    weight_in = [held_in[s * chunk : (s + 1) * chunk] for s in range(n_pipe)]
    (down_high,) = products(True, BLOCKS[1:])
    up = exchanged([dot(rows, weight_out[s], LAST) for s in range(first, middle - 1)], n_pipe)
    gram_in_low, gram_out_low, up, columns = lax.optimization_barrier(
        (gram_in_low, gram_out_low, up, jnp.concatenate([down_high, up_high], axis=1))
    )
    gram_high = over_dp(columns)

    kept = len(kept_crosses(first, middle))
    acts, hidden, scale, cross = run(
        forward_kernel(first, middle, width, inner, n_pipe),
        [
            ((tok_rows, count * inner), jnp.bfloat16),
            ((count, block, inner), jnp.float32),
            ((count, block, LANES), jnp.float32),
            ((kept, block, inner), jnp.float32),
        ],
        down,
        up,
        gram_in_low,
        gram_out_low,
    )
    late, acts = lax.optimization_barrier((seed, acts))
    acts = swap(acts, "pipe")
    exact, columns = run(
        next_rows_kernel(first, middle, last, inner, chunk),
        [
            ((tok_rows, chunk), jnp.float32),
            ((tok_rows, (2 * (last - middle) - 1) * inner + LANES), jnp.bfloat16),
        ],
        rows,
        acts,
        all_in,
        all_out,
        specs={
            2: pl.BlockSpec(
                ((last - middle) * chunk, inner), lambda step: (middle // (last - middle), 0)
            )
        },
    )
    sums = exchanged(columns, n_pipe)
    grad_high = exchanged([dot(late, weight_out[s], LAST) for s in range(middle, last)], n_pipe)

    turned = run(
        turning_kernel(middle, last, width, inner, n_pipe),
        [((tok_rows, 2 * (last - middle) * inner + LANES), jnp.bfloat16)],
        sums,
        grad_high,
        gram_high,
    )[0]
    turned = swap(turned, "pipe")

    def packed_shape(group):
        rows_packed = 2 * group * chunk * inner // (n_dp * LANES)
        return (n_dp // 2, rows_packed, LANES)

    dp = lax.axis_index("dp")
    core, chip = dp % 2, dp // 2
    chips = jnp.arange(n_dp // 2)
    xs = n_dp // 4
    away = (chips // 2 - chip // 2 + xs) % xs * 2 + (chips % 2 + chip % 2) % 2
    fixed = jnp.concatenate([chips, core[None]]).astype(jnp.int32)
    place = jnp.concatenate([away, core[None]]).astype(jnp.int32)
    in_smem = {0: pl.BlockSpec(memory_space=pltpu.SMEM)}

    grads_high, mine, other, upstream, columns = run(
        grads_kernel(middle, last, first, inner, chunk, n_dp, (last - middle) * inner + LANES),
        [
            ((last - middle, tok_rows, chunk), jnp.bfloat16),
            (packed_shape(last - middle), jnp.bfloat16),
            (packed_shape(last - middle), jnp.bfloat16),
            ((tok_rows, chunk), jnp.float32),
            ((tok_rows, count * inner), jnp.bfloat16),
        ],
        place,
        exact,
        turned,
        turned,
        seed,
        all_in,
        all_out,
        specs=in_smem,
    )
    grad_low = exchanged(columns, n_pipe)
    other = other_core(other, n_dp)
    grad_low, mine, other = lax.optimization_barrier((grad_low, mine, other))
    arrived_high = between_chips(added(mine, other, mine.shape[0]), n_dp)

    packs = run(
        backward_kernel(first, middle, width, inner, n_pipe),
        [((tok_rows, count * inner + LANES), jnp.bfloat16)],
        grad_low,
        hidden,
        scale,
        cross,
        gram_in_low,
    )[0]
    packs = swap(packs, "pipe")
    grads_low, mine, other, _ = run(
        grads_kernel(first, middle, first, inner, chunk, n_dp, 0),
        [
            ((count, tok_rows, chunk), jnp.bfloat16),
            (packed_shape(count), jnp.bfloat16),
            (packed_shape(count), jnp.bfloat16),
            ((tok_rows, chunk), jnp.float32),
        ],
        fixed,
        rows,
        packs,
        acts,
        upstream,
        all_in,
        all_out,
        specs=in_smem,
    )
    mine, other, arrived_high = lax.optimization_barrier((mine, other, arrived_high))
    arrived_low = lax.all_to_all(
        added(mine, other_core(other, n_dp), 1)[0],
        "dp",
        0,
        0,
        tiled=True,
        axis_index_groups=[list(range(c, n_dp, 2)) for c in range(2)],
    )

    ins, outs = [], []
    for (low, high), arrived in zip(BLOCKS, ([arrived_low], arrived_high)):
        share = (high - low) * chunk // n_dp
        sum_in, sum_out = run(
            unpack_kernel(inner, share, len(arrived)),
            [
                ((share, inner), jnp.bfloat16),
                ((arrived[0].shape[-2] - share * inner // LANES, LANES), jnp.bfloat16),
            ],
            *arrived,
        )
        ins.append(sum_in)
        outs.append(sum_out.reshape(high - low, -1, LANES))
    grad_out = swap(jnp.concatenate(outs, axis=0), "pipe")
    grads = jnp.concatenate([grads_low, grads_high], axis=0)
    grads, grad_out = lax.optimization_barrier((grads, grad_out))
    input_grads = swap(grads, "pipe")
    input_grads = input_grads.transpose(1, 0, 2).reshape(1, tok_rows, width)
    grad_in = move_in(*ins, n_pipe, n_dp)
    is_high = (me >= middle).astype(jnp.int32).reshape(1)

    shape_in, shape_out = (share_in, inner), (share_out, width)
    *updated, pieces = run(
        adam_kernel(share_out, chunk // LANES, share_in),
        [(shape_in, jnp.float32)] * 3
        + [(shape_out, jnp.float32)] * 3
        + [((n_dp, 2, share_out, share_in), jnp.bfloat16)],
        is_high,
        *grad_in,
        grad_out,
        master_in[0],
        moment_in[0],
        second_in[0],
        master_out[0],
        moment_out[0],
        second_out[0],
        specs=in_smem,
    )
    new_in, new_moment_in, new_second_in, new_out, new_moment_out, new_second_out = updated
    roll_in, roll_out = run(
        rollout_kernel(share_out, share_in),
        [(shape_out, jnp.bfloat16), (shape_in, jnp.bfloat16)],
        swap(pieces, "dp"),
    )
    return (
        input_grads,
        new_in[None],
        new_moment_in[None],
        new_second_in[None],
        new_out[None],
        new_moment_out[None],
        new_second_out[None],
        roll_in[None],
        roll_out[None],
    )


def solution(mesh):
    in_specs = (P("dp", None), P("dp", None)) + (P("pipe", "dp", None),) * 6
    out_specs = (P("pipe", "dp", None),) * 9
    return jax.shard_map(
        on_device, mesh=mesh, in_specs=in_specs, out_specs=out_specs, check_vma=False
    )
```

```python
import jax
import jax.numpy as jnp
from jax import lax
from jax.experimental import pallas as pl
from jax.experimental.pallas import tpu as pltpu
from jax.sharding import PartitionSpec as P

norm_eps = 1e-06
beta_one = 0.9
beta_two = 0.999
learn_rate = 0.02
decay_rate = 0.1
adam_eps = 1e-08
adam_step = 100

BLOCKS = ((0, 4), (4, 8))
LANES = 128
VMEM_BYTES = 34 * 1024 * 1024


def dot(left, right, dims):
    return lax.dot_general(left, right, (dims, ((), ())), preferred_element_type=jnp.float32)


ROWS = ((1,), (0,))
LAST = ((1,), (1,))
FIRST = ((0,), (0,))


def swap(x, axis):
    return lax.all_to_all(x, axis, 0, 0, tiled=True)


def split_scalars(scalars):
    columns = []
    for value in scalars:
        high = value.astype(jnp.bfloat16)
        columns += [high, (value - high.astype(jnp.float32)).astype(jnp.bfloat16)]
    columns.append(jnp.zeros((scalars[0].shape[0], 128 - len(columns)), jnp.bfloat16))
    return columns


def exchanged(columns, count):
    packed = columns
    if isinstance(columns, list):
        packed = jnp.concatenate([c.astype(jnp.bfloat16) for c in columns], axis=1)
    return swap(packed, "pipe").reshape(count, packed.shape[0] // count, packed.shape[1])


def adam_update(master, moment, second, grad):
    moment_new = beta_one * moment + (1.0 - beta_one) * grad
    second_new = beta_two * second + (1.0 - beta_two) * grad * grad
    moment_hat = moment_new / (1.0 - beta_one**adam_step)
    second_hat = second_new / (1.0 - beta_two**adam_step)
    master_new = master - learn_rate * (
        moment_hat / (jnp.sqrt(second_hat) + adam_eps) + decay_rate * master
    )
    return (master_new, moment_new, second_new)


def run(kernel, shapes, *operands, specs=None, smem=False):
    more = {}
    if specs is not None:
        whole = [pl.BlockSpec(x.shape, zeros_map(x.ndim)) for x in operands]
        outs = [pl.BlockSpec(shape, zeros_map(len(shape))) for shape, _ in shapes]
        given = [specs.get(at, spec) for at, spec in enumerate(whole)]
        more = {"grid": (1,), "in_specs": given, "out_specs": outs}
    if smem:
        rest = [pl.BlockSpec(memory_space=pltpu.VMEM)] * (len(operands) - 1)
        more = {"in_specs": [pl.BlockSpec(memory_space=pltpu.SMEM)] + rest}
    return pl.pallas_call(
        kernel,
        out_shape=[jax.ShapeDtypeStruct(shape, kind) for shape, kind in shapes],
        compiler_params=pltpu.CompilerParams(vmem_limit_bytes=VMEM_BYTES),
        **more,
    )(*operands)


def columns_in_place(x):
    count, rows, columns = x.shape

    def kernel(x_ref, out_ref):
        out_ref[...] = x_ref[0]

    return pl.pallas_call(
        kernel,
        out_shape=jax.ShapeDtypeStruct((rows, count * columns), x.dtype),
        grid=(count,),
        in_specs=[pl.BlockSpec((1, rows, columns), lambda at: (at, 0, 0))],
        out_specs=pl.BlockSpec((rows, columns), lambda at: (0, at)),
        compiler_params=pltpu.CompilerParams(vmem_limit_bytes=VMEM_BYTES),
    )(x)


def zeros_map(ndim):
    return lambda step: (0,) * ndim


def part(ref, at, inner):
    return ref[:, at * inner : (at + 1) * inner]


def scalar_block(scalars):
    lane = lax.broadcasted_iota(jnp.int32, (scalars[0].shape[0], LANES), 1)
    packed = jnp.zeros(lane.shape, jnp.float32)
    for at, value in enumerate(scalars):
        high = value.astype(jnp.bfloat16).astype(jnp.float32)
        packed = jnp.where(lane == 2 * at, high, packed)
        packed = jnp.where(lane == 2 * at + 1, value - high, packed)
    return packed.astype(jnp.bfloat16)


def summed_part(ref, start, size):
    total = ref[0, :, start : start + size].astype(jnp.float32)
    for source in range(1, ref.shape[0]):
        total = total + ref[source, :, start : start + size].astype(jnp.float32)
    return total


def down_units(first, last):
    return [(j, t, True) for j in range(first, last) for t in range(j + 1, last)]


def up_units(first, last):
    return [(j, t, False) for j in range(first, last - 1) for t in range(j, last - 1)]


def finder(first, last, inner, down_ref, up_ref, up_start):
    places = {unit: (down_ref, at) for at, unit in enumerate(down_units(first, last))}
    if up_ref is not None:
        for at, unit in enumerate(up_units(first, last)):
            places[unit] = (up_ref, up_start + at)

    def find(unit):
        ref, at = places[unit]
        return part(ref, at, inner)

    return find


def forward_chain(first, last, width, inner, down_ref, up_ref, up_start, find):
    count = last - first
    raw = {s: summed_part(down_ref, (s - first) * inner, inner) for s in range(first, last)}
    cross = {
        s: summed_part(up_ref, up_start + (s - first) * inner, inner)
        for s in range(first, last - 1)
    }
    square = summed_part(down_ref, count * inner, LANES)
    square = square[:, 0:1] + square[:, 1:2]
    state, crosses = {}, {}
    for s in range(first, last):
        scale = lax.rsqrt(jnp.maximum(square, 0.0) / width + norm_eps)
        hidden = raw[s] * scale
        gate = jax.nn.sigmoid(hidden)
        act = (hidden * gate).astype(jnp.bfloat16)
        state[s] = (hidden, scale, act)
        if s == last - 1:
            break
        added = {}
        for k in range(first, last - 1):
            if k >= s:
                added[k] = dot(act, find((s, k, False)), ROWS)
            else:
                added[k] = dot(act, find((k, s, False)), LAST)
        wide = act.astype(jnp.float32)
        square = square + jnp.sum(wide * (2.0 * cross[s] + added[s]), axis=1, keepdims=True)
        cross = {k: cross[k] + added[k] for k in cross}
        for t in range(s + 1, last):
            raw[t] = raw[t] + dot(act, find((s, t, True)), ROWS)
        crosses[s + 1] = cross
    return state, crosses


def backward_chain(first, last, width, inner, grad_ref, hidden_of, scale_of, cross_of, find):
    grad_act = {s: summed_part(grad_ref, (s - first) * inner, inner) for s in range(first, last)}
    packs, pulls = {}, {}
    for s in reversed(range(first, last)):
        hidden, scale = hidden_of(s), scale_of(s)
        gate = jax.nn.sigmoid(hidden)
        grad_hidden = grad_act[s] * gate * (1.0 + hidden * (1.0 - gate))
        mean = jnp.sum(grad_hidden * hidden, axis=1, keepdims=True) / width
        packs[s] = (grad_hidden * scale).astype(jnp.bfloat16)
        pulls[s] = mean * scale * scale
        for t in range(first, s):
            grad_act[t] = (
                grad_act[t]
                + dot(packs[s], find((t, s, True)), LAST)
                - pulls[s] * cross_of(s, t)
            )
    return packs, pulls


def kept_crosses(first, last):
    return [(s, t) for s in range(first + 1, last) for t in range(first, s)]


def forward_kernel(first, last, width, inner, copies):
    def kernel(
        down_ref, up_ref, gram_in_ref, gram_out_ref, acts_ref, hidden_ref, scale_ref, cross_ref
    ):
        find = finder(first, last, inner, gram_in_ref, gram_out_ref, 0)
        state, crosses = forward_chain(first, last, width, inner, down_ref, up_ref, 0, find)
        rows = down_ref.shape[1]
        for s in range(first, last):
            hidden, scale, act = state[s]
            at = s - first
            for copy in range(copies):
                acts_ref[copy * rows : (copy + 1) * rows, at * inner : (at + 1) * inner] = act
            hidden_ref[at] = hidden
            scale_ref[at] = jnp.broadcast_to(scale, (rows, LANES))
        for at, (s, t) in enumerate(kept_crosses(first, last)):
            cross_ref[at] = crosses[s][t]

    return kernel


def store_packs(ref, packs, pulls, first, last, inner, rows, copies):
    scalars = scalar_block([pulls[s] for s in range(first, last)])
    for copy in range(copies):
        there = slice(copy * rows, (copy + 1) * rows)
        for s in range(first, last):
            ref[there, (s - first) * inner : (s - first + 1) * inner] = packs[s]
        at = (last - first) * inner
        ref[there, at : at + LANES] = scalars


def backward_kernel(first, last, width, inner, copies):
    kept = {pair: at for at, pair in enumerate(kept_crosses(first, last))}

    def kernel(grad_ref, hidden_ref, scale_ref, cross_ref, gram_ref, out_ref):
        packs, pulls = backward_chain(
            first,
            last,
            width,
            inner,
            grad_ref,
            lambda s: hidden_ref[s - first],
            lambda s: scale_ref[s - first][:, 0:1],
            lambda s, t: cross_ref[kept[(s, t)]],
            finder(first, last, inner, gram_ref, None, 0),
        )
        store_packs(out_ref, packs, pulls, first, last, inner, grad_ref.shape[1], copies)

    return kernel


def turning_kernel(first, last, width, inner, copies):
    def kernel(sums_ref, grad_ref, gram_ref, out_ref):
        count = last - first
        find = finder(first, last, inner, gram_ref, gram_ref, len(down_units(first, last)))
        state, crosses = forward_chain(
            first, last, width, inner, sums_ref, sums_ref, count * inner + LANES, find
        )
        packs, pulls = backward_chain(
            first,
            last,
            width,
            inner,
            grad_ref,
            lambda s: state[s][0],
            lambda s: state[s][1],
            lambda s, t: crosses[s][t],
            find,
        )
        rows = sums_ref.shape[1]
        store_packs(out_ref, packs, pulls, first, last, inner, rows, copies)
        for copy in range(copies):
            for s in range(first, last):
                at = count * inner + LANES + (s - first) * inner
                out_ref[copy * rows : (copy + 1) * rows, at : at + inner] = state[s][2]

    return kernel


def next_rows_kernel(first, last, then, inner, chunk):
    def kernel(rows_ref, acts_ref, in_ref, out_ref, exact_ref, columns_ref):
        exact = rows_ref[...].astype(jnp.float32)
        for s in range(first, last):
            exact = exact + dot(
                part(acts_ref, s - first, inner), part(out_ref, s, chunk), ROWS
            )
        exact_ref[...] = exact
        rows = exact.astype(jnp.bfloat16)
        at = 0
        for s in range(last, then):
            weight = in_ref[(s - last) * chunk : (s - last + 1) * chunk]
            columns_ref[:, at : at + inner] = dot(rows, weight, ROWS).astype(jnp.bfloat16)
            at += inner
        squares = jnp.sum(exact * exact, axis=1, keepdims=True)
        columns_ref[:, at : at + LANES] = scalar_block([squares])
        at += LANES
        for s in range(last, then - 1):
            columns = dot(rows, part(out_ref, s, chunk), LAST)
            columns_ref[:, at : at + inner] = columns.astype(jnp.bfloat16)
            at += inner

    return kernel


def grads_kernel(first, last, before, inner, chunk, n_dp, acts_start):
    group = last - first
    share_in = group * chunk // n_dp
    share_out = inner // n_dp
    lanes_in = inner // LANES
    lanes_out = chunk // LANES

    def kernel(*refs):
        place_ref, exact_ref, packs_ref, acts_ref, up_ref, in_ref, out_ref = refs[:7]
        refs = refs[7:]
        if first == 0:
            refs[1][last:] = refs[0][...]
            refs = refs[1:]
        grads_ref, mine_ref, other_ref, up_new_ref = refs[:4]
        exact = exact_ref[...].astype(jnp.float32)
        rows = {first: exact.astype(jnp.bfloat16)}

        def act_of(s):
            at = acts_start + (s - first) * inner
            return acts_ref[:, at : at + inner]

        for s in range(first, last - 1):
            exact = exact + dot(act_of(s), part(out_ref, s, chunk), ROWS)
            rows[s + 1] = exact.astype(jnp.bfloat16)
        upstream = up_ref[...].astype(jnp.float32)
        narrow = upstream.astype(jnp.bfloat16)
        for s in reversed(range(first, last)):
            pack = part(packs_ref, s - first, inner)
            at = group * inner + 2 * (s - first)
            pull = packs_ref[:, group * inner : group * inner + LANES].astype(jnp.float32)
            at = 2 * (s - first)
            pull = pull[:, at : at + 1] + pull[:, at + 1 : at + 2]
            into = dot(rows[s], pack, FIRST).astype(jnp.bfloat16)
            onto = dot(act_of(s), narrow, FIRST).astype(jnp.bfloat16)
            base = lanes_in * share_in + (s - first) * lanes_out * share_out

            def store(refs_of, into=into, onto=onto, base=base, s=s):
                for piece in range(chunk // share_in):
                    device = (s - first) * (chunk // share_in) + piece
                    ref = refs_of[device % 2]
                    for c in range(lanes_in):
                        ref[place_ref[device // 2], c * share_in : (c + 1) * share_in] = into[
                            piece * share_in : (piece + 1) * share_in,
                            c * LANES : (c + 1) * LANES,
                        ]
                for device in range(n_dp):
                    ref = refs_of[device % 2]
                    for c in range(lanes_out):
                        row = base + c * share_out
                        ref[place_ref[device // 2], row : row + share_out] = onto[
                            device * share_out : (device + 1) * share_out,
                            c * LANES : (c + 1) * LANES,
                        ]

            @pl.when(place_ref[n_dp // 2] == 0)
            def _():
                store((mine_ref, other_ref))

            @pl.when(place_ref[n_dp // 2] == 1)
            def _():
                store((other_ref, mine_ref))

            weight = in_ref[s * chunk : (s + 1) * chunk]
            upstream = (
                upstream + dot(pack, weight, LAST) - pull * rows[s].astype(jnp.float32)
            )
            narrow = upstream.astype(jnp.bfloat16)
            grads_ref[s - first] = narrow
        up_new_ref[...] = upstream
        if before < first:
            for s in range(before, first):
                columns = dot(narrow, part(out_ref, s, chunk), LAST).astype(jnp.bfloat16)
                refs[4][:, (s - before) * inner : (s - before + 1) * inner] = columns

    return kernel


def unpack_kernel(inner, share_in, sources):
    def kernel(*refs):
        in_ref, out_ref = refs[sources:]
        given = refs[:sources]
        if sources == 1:
            given = [refs[0].at[k] for k in range(refs[0].shape[0])]
        lanes = inner // LANES

        def total_of(start, stop):
            total = given[0][start:stop].astype(jnp.float32)
            for ref in given[1:]:
                total = total + ref[start:stop].astype(jnp.float32)
            return total.astype(jnp.bfloat16)

        for c in range(lanes):
            in_ref[:, c * LANES : (c + 1) * LANES] = total_of(c * share_in, (c + 1) * share_in)
        out_ref[...] = total_of(lanes * share_in, given[0].shape[0])

    return kernel


def adam_kernel(share, lanes, share_in):
    def kernel(*refs):
        swapped_ref, one_ref, two_ref, onto_ref = refs[:4]
        state_in, state_out = refs[4:7], refs[7:10]
        new_in, new_out, pieces_ref = refs[10:13], refs[13:16], refs[16]
        per = LANES // share
        for c in range(one_ref.shape[1] // LANES):
            there = slice(c * LANES, (c + 1) * LANES)
            one = one_ref[:, there].astype(jnp.float32)
            two = two_ref[:, there].astype(jnp.float32)
            swapped = swapped_ref[0] == 1
            grad = jnp.concatenate(
                [jnp.where(swapped, two, one), jnp.where(swapped, one, two)], axis=0
            )
            results = adam_update(*(ref[:, there] for ref in state_in), grad)
            for ref, value in zip(new_in, results):
                ref[:, there] = value
            turned = results[0].T.astype(jnp.bfloat16)
            for q in range(per):
                pieces_ref[c * per + q, 0] = turned[q * share : (q + 1) * share]
        for device in range(onto_ref.shape[0]):
            for c in range(lanes):
                at = (device * lanes + c) * LANES
                grad = onto_ref[device, c * share : (c + 1) * share].astype(jnp.float32)
                results = adam_update(*(ref[:, at : at + LANES] for ref in state_out), grad)
                for ref, value in zip(new_out, results):
                    ref[:, at : at + LANES] = value
        for device in range(pieces_ref.shape[0]):
            at = device * share_in
            start = at // LANES * LANES
            stop = -(-(at + share_in) // LANES) * LANES
            values = new_out[0][:, start:stop][:, at - start : at - start + share_in]
            pieces_ref[device, 1] = values.astype(jnp.bfloat16)

    return kernel


def rollout_kernel(share, share_in):
    def kernel(pieces_ref, in_ref, out_ref):
        per = LANES // share
        for pair in range(pieces_ref.shape[0] // 2):
            both = [pieces_ref[2 * pair + h, 0].astype(jnp.float32) for h in range(2)]
            at = 2 * pair * share_in
            in_ref[:, at : at + 2 * share_in] = jnp.concatenate(both, axis=1).astype(jnp.bfloat16)
        for c in range(pieces_ref.shape[0] // per):
            rows = [pieces_ref[c * per + q, 1].astype(jnp.float32) for q in range(per)]
            out_ref[:, c * LANES : (c + 1) * LANES] = jnp.concatenate(rows, axis=0).T.astype(
                jnp.bfloat16
            )

    return kernel


def columns_kernel(orders):
    def kernel(every_ref, *out_refs):
        size = every_ref.shape[2]
        for out_ref, order in zip(out_refs, orders):
            for at, unit in enumerate(order):
                out_ref[:, at * size : (at + 1) * size] = every_ref[unit]

    return kernel


def other_core(x, n_dp):
    return lax.ppermute(x, "dp", [(j, j + 1 - 2 * (j % 2)) for j in range(n_dp)])


def add_kernel(mine_ref, other_ref, *out_refs):
    for at in range(mine_ref.shape[0]):
        total = mine_ref[at].astype(jnp.float32) + other_ref[at].astype(jnp.float32)
        if len(out_refs) == 1:
            out_refs[0][at] = total.astype(jnp.bfloat16)
        else:
            out_refs[at][...] = total.astype(jnp.bfloat16)


def added(mine, other, count):
    shape = mine.shape if count == 1 else mine.shape[1:]
    return run(add_kernel, [(shape, jnp.bfloat16)] * count, mine, other)


def chip_steps(n_dp):
    return [(dx, dz) for dx in range(n_dp // 4) for dz in range(2)]


def between_chips(blocks, n_dp):
    arrived = [blocks[0]]
    for (dx, dz), block in list(zip(chip_steps(n_dp), blocks))[1:]:
        pairs = []
        for j in range(n_dp):
            x, z, core = j // 4, j // 2 % 2, j % 2
            pairs.append((j, (x + dx) % (n_dp // 4) * 4 + (z ^ dz) * 2 + core))
        arrived.append(lax.ppermute(block, "dp", pairs))
    return arrived


def move_in(low, high, n_pipe, n_dp):
    odd = lax.axis_index("dp") % 2 == 1
    group = n_pipe // 2
    moved = []
    for q in range(2):
        pairs = []
        for i in range(n_pipe):
            for j in range(n_dp):
                section = j * group // n_dp + (0 if j % 2 == q else group)
                pairs.append((i * n_dp + j, section * n_dp + 2 * i + j // 2 % 2))
        payload = jnp.where(odd, low, high) if q == 1 else jnp.where(odd, high, low)
        moved.append(lax.ppermute(payload, ("pipe", "dp"), pairs))
    return moved


def on_device(
    inputs_x, cotangent, master_in, master_out, moment_in, moment_out, second_in, second_out
):
    n_pipe = lax.axis_size("pipe")
    n_dp = lax.axis_size("dp")
    me = lax.axis_index("pipe")
    tok_rows, width = inputs_x.shape
    chunk = width // n_pipe
    inner = master_in.shape[2]
    share_in = master_in.shape[1]
    share_out = master_out.shape[1]
    block = tok_rows // n_pipe

    own_in = master_in[0].astype(jnp.bfloat16)
    own_out = master_out[0].astype(jnp.bfloat16)
    pairs = [
        (s * n_dp + 2 * i + h, i * n_dp + 2 * s + h)
        for s in range(n_pipe)
        for i in range(n_pipe)
        for h in range(2)
    ]
    piece_in = lax.ppermute(own_in, ("pipe", "dp"), pairs)
    piece_out = swap(own_out.reshape(share_out, n_pipe, chunk).transpose(1, 0, 2), "pipe")
    flat_out = piece_out.transpose(1, 0, 2).reshape(share_out, width)
    all_in = lax.all_gather(piece_in, "dp", axis=0, tiled=True)
    all_out = lax.all_gather(flat_out, "dp", axis=0, tiled=True)
    weight_in = [all_in[s * chunk : (s + 1) * chunk] for s in range(n_pipe)]

    def products(down, blocks):
        units, partial, orders = [], [], []
        for first, last in blocks:
            wanted = (down_units if down else up_units)(first, last)
            for t in sorted({t for _, t, _ in wanted}):
                ks = [k for k, other, _ in wanted if other == t]
                left = piece_out[ks[0] : ks[-1] + 1].reshape(-1, chunk)
                if down:
                    partial.append(dot(left, weight_in[t], ROWS))
                else:
                    partial.append(dot(left, weight_out[t], LAST))
                units += [(k, t, down) for k in ks]
        for first, last in blocks:
            wanted = (down_units if down else up_units)(first, last)
            orders.append([units.index(unit) for unit in wanted])
        partial = [p.astype(jnp.bfloat16) for p in partial]
        arrived = swap(jnp.concatenate(partial, axis=0), "pipe")
        arrived = arrived.reshape(n_pipe, -1, inner)
        mine = jnp.sum(arrived.astype(jnp.float32), axis=0).astype(jnp.bfloat16)
        every = swap(jnp.tile(mine, (n_pipe, 1)), "pipe").reshape(-1, share_out, inner)
        shapes = [((share_out, len(order) * inner), jnp.bfloat16) for order in orders]
        return run(columns_kernel(orders), shapes, every)

    def over_dp(columns):
        return lax.all_gather(columns, "dp", axis=0, tiled=True)

    rows = lax.dynamic_slice_in_dim(inputs_x, me * chunk, chunk, 1)
    seed = lax.dynamic_slice_in_dim(cotangent, me * chunk, chunk, 1)

    (first, middle), (_, last) = BLOCKS
    count = middle - first
    wide = rows.astype(jnp.float32)
    down = [dot(rows, weight_in[s], ROWS) for s in range(first, middle)]
    down += split_scalars([jnp.sum(wide * wide, axis=1, keepdims=True)])
    down = exchanged(down, n_pipe)
    (down_low,) = products(True, BLOCKS[:1])
    all_out, down, down_low = lax.optimization_barrier((all_out, down, down_low))
    weight_out = [all_out[:, s * chunk : (s + 1) * chunk] for s in range(n_pipe)]
    gram_in_low = over_dp(down_low)
    up_low, up_high = products(False, BLOCKS)
    gram_out_low = over_dp(up_low)
    held_in, up_low = lax.optimization_barrier((all_in, up_low))
    weight_in = [held_in[s * chunk : (s + 1) * chunk] for s in range(n_pipe)]
    (down_high,) = products(True, BLOCKS[1:])
    up = exchanged([dot(rows, weight_out[s], LAST) for s in range(first, middle - 1)], n_pipe)
    gram_in_low, gram_out_low, up, columns = lax.optimization_barrier(
        (gram_in_low, gram_out_low, up, jnp.concatenate([down_high, up_high], axis=1))
    )
    gram_high = over_dp(columns)

    kept = len(kept_crosses(first, middle))
    acts, hidden, scale, cross = run(
        forward_kernel(first, middle, width, inner, n_pipe),
        [
            ((tok_rows, count * inner), jnp.bfloat16),
            ((count, block, inner), jnp.float32),
            ((count, block, LANES), jnp.float32),
            ((kept, block, inner), jnp.float32),
        ],
        down,
        up,
        gram_in_low,
        gram_out_low,
    )
    late, acts = lax.optimization_barrier((seed, acts))
    acts = swap(acts, "pipe")
    exact, columns = run(
        next_rows_kernel(first, middle, last, inner, chunk),
        [
            ((tok_rows, chunk), jnp.float32),
            ((tok_rows, (2 * (last - middle) - 1) * inner + LANES), jnp.bfloat16),
        ],
        rows,
        acts,
        all_in,
        all_out,
        specs={
            2: pl.BlockSpec(
                ((last - middle) * chunk, inner), lambda step: (middle // (last - middle), 0)
            )
        },
    )
    sums = exchanged(columns, n_pipe)
    grad_high = exchanged([dot(late, weight_out[s], LAST) for s in range(middle, last)], n_pipe)

    turned = run(
        turning_kernel(middle, last, width, inner, n_pipe),
        [((tok_rows, 2 * (last - middle) * inner + LANES), jnp.bfloat16)],
        sums,
        grad_high,
        gram_high,
    )[0]
    turned = swap(turned, "pipe")

    def packed_shape(group):
        rows_packed = 2 * group * chunk * inner // (n_dp * LANES)
        return (n_dp // 2, rows_packed, LANES)

    dp = lax.axis_index("dp")
    core, chip = dp % 2, dp // 2
    chips = jnp.arange(n_dp // 2)
    xs = n_dp // 4
    away = (chips // 2 - chip // 2 + xs) % xs * 2 + (chips % 2 + chip % 2) % 2
    fixed = jnp.concatenate([chips, core[None]]).astype(jnp.int32)
    place = jnp.concatenate([away, core[None]]).astype(jnp.int32)

    grads_high, mine, other, upstream, columns = run(
        grads_kernel(middle, last, first, inner, chunk, n_dp, (last - middle) * inner + LANES),
        [
            ((last - middle, tok_rows, chunk), jnp.bfloat16),
            (packed_shape(last - middle), jnp.bfloat16),
            (packed_shape(last - middle), jnp.bfloat16),
            ((tok_rows, chunk), jnp.float32),
            ((tok_rows, count * inner), jnp.bfloat16),
        ],
        place,
        exact,
        turned,
        turned,
        seed,
        all_in,
        all_out,
        smem=True,
    )
    grad_low = exchanged(columns, n_pipe)
    other = other_core(other, n_dp)
    grad_low, mine, other = lax.optimization_barrier((grad_low, mine, other))
    arrived_high = between_chips(added(mine, other, mine.shape[0]), n_dp)

    packs = run(
        backward_kernel(first, middle, width, inner, n_pipe),
        [((tok_rows, count * inner + LANES), jnp.bfloat16)],
        grad_low,
        hidden,
        scale,
        cross,
        gram_in_low,
    )[0]
    packs = swap(packs, "pipe")
    grads, mine, other, _ = run(
        grads_kernel(first, middle, first, inner, chunk, n_dp, 0),
        [
            ((n_pipe, tok_rows, chunk), jnp.bfloat16),
            (packed_shape(count), jnp.bfloat16),
            (packed_shape(count), jnp.bfloat16),
            ((tok_rows, chunk), jnp.float32),
        ],
        fixed,
        rows,
        packs,
        acts,
        upstream,
        all_in,
        all_out,
        grads_high,
        smem=True,
    )
    mine, other, arrived_high = lax.optimization_barrier((mine, other, arrived_high))
    arrived_low = lax.all_to_all(
        added(mine, other_core(other, n_dp), 1)[0],
        "dp",
        0,
        0,
        tiled=True,
        axis_index_groups=[list(range(c, n_dp, 2)) for c in range(2)],
    )

    ins, outs = [], []
    for (low, high), arrived in zip(BLOCKS, ([arrived_low], arrived_high)):
        share = (high - low) * chunk // n_dp
        sum_in, sum_out = run(
            unpack_kernel(inner, share, len(arrived)),
            [
                ((share, inner), jnp.bfloat16),
                ((arrived[0].shape[-2] - share * inner // LANES, LANES), jnp.bfloat16),
            ],
            *arrived,
        )
        ins.append(sum_in)
        outs.append(sum_out.reshape(high - low, -1, LANES))
    grad_out = swap(jnp.concatenate(outs, axis=0), "pipe")
    grads, grad_out = lax.optimization_barrier((grads, grad_out))
    input_grads = swap(grads, "pipe")
    grad_in = move_in(*ins, n_pipe, n_dp)
    is_high = (me >= middle).astype(jnp.int32).reshape(1)

    shape_in, shape_out = (share_in, inner), (share_out, width)
    *updated, pieces = run(
        adam_kernel(share_out, chunk // LANES, share_in),
        [(shape_in, jnp.float32)] * 3
        + [(shape_out, jnp.float32)] * 3
        + [((n_dp, 2, share_out, share_in), jnp.bfloat16)],
        is_high,
        *grad_in,
        grad_out,
        master_in[0],
        moment_in[0],
        second_in[0],
        master_out[0],
        moment_out[0],
        second_out[0],
        smem=True,
    )
    new_in, new_moment_in, new_second_in, new_out, new_moment_out, new_second_out = updated
    pieces, input_grads = lax.optimization_barrier((pieces, input_grads))
    input_grads = columns_in_place(input_grads)[None]
    roll_in, roll_out = run(
        rollout_kernel(share_out, share_in),
        [(shape_out, jnp.bfloat16), (shape_in, jnp.bfloat16)],
        swap(pieces, "dp"),
    )
    return (
        input_grads,
        new_in[None],
        new_moment_in[None],
        new_second_in[None],
        new_out[None],
        new_moment_out[None],
        new_second_out[None],
        roll_in[None],
        roll_out[None],
    )


def solution(mesh):
    in_specs = (P("dp", None), P("dp", None)) + (P("pipe", "dp", None),) * 6
    out_specs = (P("pipe", "dp", None),) * 9
    return jax.shard_map(
        on_device, mesh=mesh, in_specs=in_specs, out_specs=out_specs, check_vma=False
    )
```

```python
import jax
import jax.numpy as jnp
from jax import lax
from jax.experimental import pallas as pl
from jax.experimental.pallas import tpu as pltpu
from jax.sharding import PartitionSpec as P

norm_eps = 1e-06
beta_one = 0.9
beta_two = 0.999
learn_rate = 0.02
decay_rate = 0.1
adam_eps = 1e-08
adam_step = 100

BLOCKS = ((0, 4), (4, 8))
LANES = 128
VMEM_BYTES = 34 * 1024 * 1024


def dot(left, right, dims):
    return lax.dot_general(left, right, (dims, ((), ())), preferred_element_type=jnp.float32)


ROWS = ((1,), (0,))
LAST = ((1,), (1,))
FIRST = ((0,), (0,))


def swap(x, axis):
    return lax.all_to_all(x, axis, 0, 0, tiled=True)


def split_scalars(scalars):
    columns = []
    for value in scalars:
        high = value.astype(jnp.bfloat16)
        columns += [high, (value - high.astype(jnp.float32)).astype(jnp.bfloat16)]
    columns.append(jnp.zeros((scalars[0].shape[0], 128 - len(columns)), jnp.bfloat16))
    return columns


def exchanged(columns, count):
    packed = columns
    if isinstance(columns, list):
        packed = jnp.concatenate([c.astype(jnp.bfloat16) for c in columns], axis=1)
    return swap(packed, "pipe").reshape(count, packed.shape[0] // count, packed.shape[1])


def adam_update(master, moment, second, grad):
    moment_new = beta_one * moment + (1.0 - beta_one) * grad
    second_new = beta_two * second + (1.0 - beta_two) * grad * grad
    moment_hat = moment_new / (1.0 - beta_one**adam_step)
    second_hat = second_new / (1.0 - beta_two**adam_step)
    master_new = master - learn_rate * (
        moment_hat / (jnp.sqrt(second_hat) + adam_eps) + decay_rate * master
    )
    return (master_new, moment_new, second_new)


def run(kernel, shapes, *operands, specs=None, smem=False):
    more = {}
    if specs is not None:
        whole = [pl.BlockSpec(x.shape, zeros_map(x.ndim)) for x in operands]
        outs = [pl.BlockSpec(shape, zeros_map(len(shape))) for shape, _ in shapes]
        given = [specs.get(at, spec) for at, spec in enumerate(whole)]
        more = {"grid": (1,), "in_specs": given, "out_specs": outs}
    if smem:
        rest = [pl.BlockSpec(memory_space=pltpu.VMEM)] * (len(operands) - 1)
        more = {"in_specs": [pl.BlockSpec(memory_space=pltpu.SMEM)] + rest}
    return pl.pallas_call(
        kernel,
        out_shape=[jax.ShapeDtypeStruct(shape, kind) for shape, kind in shapes],
        compiler_params=pltpu.CompilerParams(vmem_limit_bytes=VMEM_BYTES),
        **more,
    )(*operands)


def columns_in_place(x):
    count, rows, columns = x.shape

    def kernel(x_ref, out_ref):
        out_ref[...] = x_ref[0]

    return pl.pallas_call(
        kernel,
        out_shape=jax.ShapeDtypeStruct((rows, count * columns), x.dtype),
        grid=(count,),
        in_specs=[pl.BlockSpec((1, rows, columns), lambda at: (at, 0, 0))],
        out_specs=pl.BlockSpec((rows, columns), lambda at: (0, at)),
        compiler_params=pltpu.CompilerParams(vmem_limit_bytes=VMEM_BYTES),
    )(x)


def zeros_map(ndim):
    return lambda step: (0,) * ndim


def part(ref, at, inner):
    return ref[:, at * inner : (at + 1) * inner]


def scalar_block(scalars):
    lane = lax.broadcasted_iota(jnp.int32, (scalars[0].shape[0], LANES), 1)
    packed = jnp.zeros(lane.shape, jnp.float32)
    for at, value in enumerate(scalars):
        high = value.astype(jnp.bfloat16).astype(jnp.float32)
        packed = jnp.where(lane == 2 * at, high, packed)
        packed = jnp.where(lane == 2 * at + 1, value - high, packed)
    return packed.astype(jnp.bfloat16)


def summed_part(ref, start, size):
    total = ref[0, :, start : start + size].astype(jnp.float32)
    for source in range(1, ref.shape[0]):
        total = total + ref[source, :, start : start + size].astype(jnp.float32)
    return total


def down_units(first, last):
    return [(j, t, True) for j in range(first, last) for t in range(j + 1, last)]


def up_units(first, last):
    return [(j, t, False) for j in range(first, last - 1) for t in range(j, last - 1)]


def finder(first, last, inner, down_ref, up_ref, up_start):
    places = {unit: (down_ref, at) for at, unit in enumerate(down_units(first, last))}
    if up_ref is not None:
        for at, unit in enumerate(up_units(first, last)):
            places[unit] = (up_ref, up_start + at)

    def find(unit):
        ref, at = places[unit]
        return part(ref, at, inner)

    return find


def forward_chain(first, last, width, inner, down_ref, up_ref, up_start, find):
    count = last - first
    raw = {s: summed_part(down_ref, (s - first) * inner, inner) for s in range(first, last)}
    cross = {
        s: summed_part(up_ref, up_start + (s - first) * inner, inner)
        for s in range(first, last - 1)
    }
    square = summed_part(down_ref, count * inner, LANES)
    square = square[:, 0:1] + square[:, 1:2]
    state, crosses = {}, {}
    for s in range(first, last):
        scale = lax.rsqrt(jnp.maximum(square, 0.0) / width + norm_eps)
        hidden = raw[s] * scale
        gate = jax.nn.sigmoid(hidden)
        act = (hidden * gate).astype(jnp.bfloat16)
        state[s] = (hidden, scale, act)
        if s == last - 1:
            break
        added = {}
        for k in range(first, last - 1):
            if k >= s:
                added[k] = dot(act, find((s, k, False)), ROWS)
            else:
                added[k] = dot(act, find((k, s, False)), LAST)
        wide = act.astype(jnp.float32)
        square = square + jnp.sum(wide * (2.0 * cross[s] + added[s]), axis=1, keepdims=True)
        cross = {k: cross[k] + added[k] for k in cross}
        for t in range(s + 1, last):
            raw[t] = raw[t] + dot(act, find((s, t, True)), ROWS)
        crosses[s + 1] = cross
    return state, crosses


def backward_chain(first, last, width, inner, grad_ref, hidden_of, scale_of, cross_of, find):
    grad_act = {s: summed_part(grad_ref, (s - first) * inner, inner) for s in range(first, last)}
    packs, pulls = {}, {}
    for s in reversed(range(first, last)):
        hidden, scale = hidden_of(s), scale_of(s)
        gate = jax.nn.sigmoid(hidden)
        grad_hidden = grad_act[s] * gate * (1.0 + hidden * (1.0 - gate))
        mean = jnp.sum(grad_hidden * hidden, axis=1, keepdims=True) / width
        packs[s] = (grad_hidden * scale).astype(jnp.bfloat16)
        pulls[s] = mean * scale * scale
        for t in range(first, s):
            grad_act[t] = (
                grad_act[t]
                + dot(packs[s], find((t, s, True)), LAST)
                - pulls[s] * cross_of(s, t)
            )
    return packs, pulls


def kept_crosses(first, last):
    return [(s, t) for s in range(first + 1, last) for t in range(first, s)]


def forward_kernel(first, last, width, inner, copies):
    def kernel(
        sums_ref, gram_in_ref, gram_out_ref, acts_ref, hidden_ref, scale_ref, cross_ref
    ):
        find = finder(first, last, inner, gram_in_ref, gram_out_ref, 0)
        up_start = (last - first) * inner + LANES
        state, crosses = forward_chain(
            first, last, width, inner, sums_ref, sums_ref, up_start, find
        )
        rows = sums_ref.shape[1]
        for s in range(first, last):
            hidden, scale, act = state[s]
            at = s - first
            for copy in range(copies):
                acts_ref[copy * rows : (copy + 1) * rows, at * inner : (at + 1) * inner] = act
            hidden_ref[at] = hidden
            scale_ref[at] = jnp.broadcast_to(scale, (rows, LANES))
        for at, (s, t) in enumerate(kept_crosses(first, last)):
            cross_ref[at] = crosses[s][t]

    return kernel


def store_packs(ref, packs, pulls, first, last, inner, rows, copies):
    scalars = scalar_block([pulls[s] for s in range(first, last)])
    for copy in range(copies):
        there = slice(copy * rows, (copy + 1) * rows)
        for s in range(first, last):
            ref[there, (s - first) * inner : (s - first + 1) * inner] = packs[s]
        at = (last - first) * inner
        ref[there, at : at + LANES] = scalars


def backward_kernel(first, last, width, inner, copies):
    kept = {pair: at for at, pair in enumerate(kept_crosses(first, last))}

    def kernel(grad_ref, hidden_ref, scale_ref, cross_ref, gram_ref, out_ref):
        packs, pulls = backward_chain(
            first,
            last,
            width,
            inner,
            grad_ref,
            lambda s: hidden_ref[s - first],
            lambda s: scale_ref[s - first][:, 0:1],
            lambda s, t: cross_ref[kept[(s, t)]],
            finder(first, last, inner, gram_ref, None, 0),
        )
        store_packs(out_ref, packs, pulls, first, last, inner, grad_ref.shape[1], copies)

    return kernel


def turning_kernel(first, last, width, inner, copies):
    def kernel(sums_ref, grad_ref, gram_ref, out_ref):
        count = last - first
        find = finder(first, last, inner, gram_ref, gram_ref, len(down_units(first, last)))
        state, crosses = forward_chain(
            first, last, width, inner, sums_ref, sums_ref, count * inner + LANES, find
        )
        packs, pulls = backward_chain(
            first,
            last,
            width,
            inner,
            grad_ref,
            lambda s: state[s][0],
            lambda s: state[s][1],
            lambda s, t: crosses[s][t],
            find,
        )
        rows = sums_ref.shape[1]
        store_packs(out_ref, packs, pulls, first, last, inner, rows, copies)
        for copy in range(copies):
            for s in range(first, last):
                at = count * inner + LANES + (s - first) * inner
                out_ref[copy * rows : (copy + 1) * rows, at : at + inner] = state[s][2]

    return kernel


def next_rows_kernel(first, last, then, inner, chunk):
    def kernel(rows_ref, acts_ref, in_ref, out_ref, exact_ref, columns_ref):
        exact = rows_ref[...].astype(jnp.float32)
        for s in range(first, last):
            exact = exact + dot(
                part(acts_ref, s - first, inner), part(out_ref, s, chunk), ROWS
            )
        exact_ref[...] = exact
        rows = exact.astype(jnp.bfloat16)
        at = 0
        for s in range(last, then):
            weight = in_ref[(s - last) * chunk : (s - last + 1) * chunk]
            columns_ref[:, at : at + inner] = dot(rows, weight, ROWS).astype(jnp.bfloat16)
            at += inner
        squares = jnp.sum(exact * exact, axis=1, keepdims=True)
        columns_ref[:, at : at + LANES] = scalar_block([squares])
        at += LANES
        for s in range(last, then - 1):
            columns = dot(rows, part(out_ref, s, chunk), LAST)
            columns_ref[:, at : at + inner] = columns.astype(jnp.bfloat16)
            at += inner

    return kernel


def grads_kernel(first, last, before, inner, chunk, n_dp, acts_start):
    group = last - first
    share_in = group * chunk // n_dp
    share_out = inner // n_dp
    lanes_in = inner // LANES
    lanes_out = chunk // LANES

    def kernel(*refs):
        place_ref, exact_ref, packs_ref, acts_ref, up_ref, in_ref, out_ref = refs[:7]
        refs = refs[7:]
        if first == 0:
            refs[1][last:] = refs[0][...]
            refs = refs[1:]
        grads_ref, mine_ref, other_ref, up_new_ref = refs[:4]
        exact = exact_ref[...].astype(jnp.float32)
        rows = {first: exact.astype(jnp.bfloat16)}

        def act_of(s):
            at = acts_start + (s - first) * inner
            return acts_ref[:, at : at + inner]

        for s in range(first, last - 1):
            exact = exact + dot(act_of(s), part(out_ref, s, chunk), ROWS)
            rows[s + 1] = exact.astype(jnp.bfloat16)
        upstream = up_ref[...].astype(jnp.float32)
        narrow = upstream.astype(jnp.bfloat16)
        for s in reversed(range(first, last)):
            pack = part(packs_ref, s - first, inner)
            at = group * inner + 2 * (s - first)
            pull = packs_ref[:, group * inner : group * inner + LANES].astype(jnp.float32)
            at = 2 * (s - first)
            pull = pull[:, at : at + 1] + pull[:, at + 1 : at + 2]
            into = dot(rows[s], pack, FIRST).astype(jnp.bfloat16)
            onto = dot(act_of(s), narrow, FIRST).astype(jnp.bfloat16)
            base = lanes_in * share_in + (s - first) * lanes_out * share_out

            def store(refs_of, into=into, onto=onto, base=base, s=s):
                for piece in range(chunk // share_in):
                    device = (s - first) * (chunk // share_in) + piece
                    ref = refs_of[device % 2]
                    for c in range(lanes_in):
                        ref[place_ref[device // 2], c * share_in : (c + 1) * share_in] = into[
                            piece * share_in : (piece + 1) * share_in,
                            c * LANES : (c + 1) * LANES,
                        ]
                for device in range(n_dp):
                    ref = refs_of[device % 2]
                    for c in range(lanes_out):
                        row = base + c * share_out
                        ref[place_ref[device // 2], row : row + share_out] = onto[
                            device * share_out : (device + 1) * share_out,
                            c * LANES : (c + 1) * LANES,
                        ]

            @pl.when(place_ref[n_dp // 2] == 0)
            def _():
                store((mine_ref, other_ref))

            @pl.when(place_ref[n_dp // 2] == 1)
            def _():
                store((other_ref, mine_ref))

            weight = in_ref[s * chunk : (s + 1) * chunk]
            upstream = (
                upstream + dot(pack, weight, LAST) - pull * rows[s].astype(jnp.float32)
            )
            narrow = upstream.astype(jnp.bfloat16)
            grads_ref[s - first] = narrow
        up_new_ref[...] = upstream
        if before < first:
            for s in range(before, first):
                columns = dot(narrow, part(out_ref, s, chunk), LAST).astype(jnp.bfloat16)
                refs[4][:, (s - before) * inner : (s - before + 1) * inner] = columns

    return kernel


def unpack_kernel(inner, share_in, sources):
    def kernel(*refs):
        in_ref, out_ref = refs[sources:]
        given = refs[:sources]
        if sources == 1:
            given = [refs[0].at[k] for k in range(refs[0].shape[0])]
        lanes = inner // LANES

        def total_of(start, stop):
            total = given[0][start:stop].astype(jnp.float32)
            for ref in given[1:]:
                total = total + ref[start:stop].astype(jnp.float32)
            return total.astype(jnp.bfloat16)

        for c in range(lanes):
            in_ref[:, c * LANES : (c + 1) * LANES] = total_of(c * share_in, (c + 1) * share_in)
        out_ref[...] = total_of(lanes * share_in, given[0].shape[0])

    return kernel


def adam_kernel(share, lanes, share_in):
    def kernel(*refs):
        swapped_ref, one_ref, two_ref, onto_ref = refs[:4]
        state_in, state_out = refs[4:7], refs[7:10]
        new_in, new_out, pieces_ref = refs[10:13], refs[13:16], refs[16]
        per = LANES // share
        for c in range(one_ref.shape[1] // LANES):
            there = slice(c * LANES, (c + 1) * LANES)
            one = one_ref[:, there].astype(jnp.float32)
            two = two_ref[:, there].astype(jnp.float32)
            swapped = swapped_ref[0] == 1
            grad = jnp.concatenate(
                [jnp.where(swapped, two, one), jnp.where(swapped, one, two)], axis=0
            )
            results = adam_update(*(ref[:, there] for ref in state_in), grad)
            for ref, value in zip(new_in, results):
                ref[:, there] = value
            turned = results[0].T.astype(jnp.bfloat16)
            for q in range(per):
                pieces_ref[c * per + q, 0] = turned[q * share : (q + 1) * share]
        for device in range(onto_ref.shape[0]):
            for c in range(lanes):
                at = (device * lanes + c) * LANES
                grad = onto_ref[device, c * share : (c + 1) * share].astype(jnp.float32)
                results = adam_update(*(ref[:, at : at + LANES] for ref in state_out), grad)
                for ref, value in zip(new_out, results):
                    ref[:, at : at + LANES] = value
        for device in range(pieces_ref.shape[0]):
            at = device * share_in
            start = at // LANES * LANES
            stop = -(-(at + share_in) // LANES) * LANES
            values = new_out[0][:, start:stop][:, at - start : at - start + share_in]
            pieces_ref[device, 1] = values.astype(jnp.bfloat16)

    return kernel


def rollout_kernel(share, share_in):
    def kernel(pieces_ref, in_ref, out_ref):
        per = LANES // share
        for pair in range(pieces_ref.shape[0] // 2):
            both = [pieces_ref[2 * pair + h, 0].astype(jnp.float32) for h in range(2)]
            at = 2 * pair * share_in
            in_ref[:, at : at + 2 * share_in] = jnp.concatenate(both, axis=1).astype(jnp.bfloat16)
        for c in range(pieces_ref.shape[0] // per):
            rows = [pieces_ref[c * per + q, 1].astype(jnp.float32) for q in range(per)]
            out_ref[:, c * LANES : (c + 1) * LANES] = jnp.concatenate(rows, axis=0).T.astype(
                jnp.bfloat16
            )

    return kernel


def columns_kernel(orders):
    def kernel(every_ref, *out_refs):
        size = every_ref.shape[2]
        for out_ref, order in zip(out_refs, orders):
            for at, unit in enumerate(order):
                out_ref[:, at * size : (at + 1) * size] = every_ref[unit]

    return kernel


def other_core(x, n_dp):
    return lax.ppermute(x, "dp", [(j, j + 1 - 2 * (j % 2)) for j in range(n_dp)])


def add_kernel(mine_ref, other_ref, *out_refs):
    for at in range(mine_ref.shape[0]):
        total = mine_ref[at].astype(jnp.float32) + other_ref[at].astype(jnp.float32)
        if len(out_refs) == 1:
            out_refs[0][at] = total.astype(jnp.bfloat16)
        else:
            out_refs[at][...] = total.astype(jnp.bfloat16)


def added(mine, other, count):
    shape = mine.shape if count == 1 else mine.shape[1:]
    return run(add_kernel, [(shape, jnp.bfloat16)] * count, mine, other)


def chip_steps(n_dp):
    return [(dx, dz) for dx in range(n_dp // 4) for dz in range(2)]


def between_chips(blocks, n_dp):
    arrived = [blocks[0]]
    for (dx, dz), block in list(zip(chip_steps(n_dp), blocks))[1:]:
        pairs = []
        for j in range(n_dp):
            x, z, core = j // 4, j // 2 % 2, j % 2
            pairs.append((j, (x + dx) % (n_dp // 4) * 4 + (z ^ dz) * 2 + core))
        arrived.append(lax.ppermute(block, "dp", pairs))
    return arrived


def move_in(low, high, n_pipe, n_dp):
    odd = lax.axis_index("dp") % 2 == 1
    group = n_pipe // 2
    moved = []
    for q in range(2):
        pairs = []
        for i in range(n_pipe):
            for j in range(n_dp):
                section = j * group // n_dp + (0 if j % 2 == q else group)
                pairs.append((i * n_dp + j, section * n_dp + 2 * i + j // 2 % 2))
        payload = jnp.where(odd, low, high) if q == 1 else jnp.where(odd, high, low)
        moved.append(lax.ppermute(payload, ("pipe", "dp"), pairs))
    return moved


def on_device(
    inputs_x, cotangent, master_in, master_out, moment_in, moment_out, second_in, second_out
):
    n_pipe = lax.axis_size("pipe")
    n_dp = lax.axis_size("dp")
    me = lax.axis_index("pipe")
    tok_rows, width = inputs_x.shape
    chunk = width // n_pipe
    inner = master_in.shape[2]
    share_in = master_in.shape[1]
    share_out = master_out.shape[1]
    block = tok_rows // n_pipe

    own_in = master_in[0].astype(jnp.bfloat16)
    own_out = master_out[0].astype(jnp.bfloat16)
    pairs = [
        (s * n_dp + 2 * i + h, i * n_dp + 2 * s + h)
        for s in range(n_pipe)
        for i in range(n_pipe)
        for h in range(2)
    ]
    piece_in = lax.ppermute(own_in, ("pipe", "dp"), pairs)
    piece_out = swap(own_out.reshape(share_out, n_pipe, chunk).transpose(1, 0, 2), "pipe")
    flat_out = piece_out.transpose(1, 0, 2).reshape(share_out, width)
    all_in = lax.all_gather(piece_in, "dp", axis=0, tiled=True)
    all_out = lax.all_gather(flat_out, "dp", axis=0, tiled=True)
    weight_in = [all_in[s * chunk : (s + 1) * chunk] for s in range(n_pipe)]

    def products(down, blocks):
        units, partial, orders = [], [], []
        for first, last in blocks:
            wanted = (down_units if down else up_units)(first, last)
            for t in sorted({t for _, t, _ in wanted}):
                ks = [k for k, other, _ in wanted if other == t]
                left = piece_out[ks[0] : ks[-1] + 1].reshape(-1, chunk)
                if down:
                    partial.append(dot(left, weight_in[t], ROWS))
                else:
                    partial.append(dot(left, weight_out[t], LAST))
                units += [(k, t, down) for k in ks]
        for first, last in blocks:
            wanted = (down_units if down else up_units)(first, last)
            orders.append([units.index(unit) for unit in wanted])
        partial = [p.astype(jnp.bfloat16) for p in partial]
        arrived = swap(jnp.concatenate(partial, axis=0), "pipe")
        arrived = arrived.reshape(n_pipe, -1, inner)
        mine = jnp.sum(arrived.astype(jnp.float32), axis=0).astype(jnp.bfloat16)
        every = swap(jnp.tile(mine, (n_pipe, 1)), "pipe").reshape(-1, share_out, inner)
        shapes = [((share_out, len(order) * inner), jnp.bfloat16) for order in orders]
        return run(columns_kernel(orders), shapes, every)

    def over_dp(columns):
        return lax.all_gather(columns, "dp", axis=0, tiled=True)

    rows = lax.dynamic_slice_in_dim(inputs_x, me * chunk, chunk, 1)
    seed = lax.dynamic_slice_in_dim(cotangent, me * chunk, chunk, 1)

    (first, middle), (_, last) = BLOCKS
    count = middle - first
    wide = rows.astype(jnp.float32)
    down_low, down_high = products(True, BLOCKS)
    all_out, down_low = lax.optimization_barrier((all_out, down_low))
    weight_out = [all_out[:, s * chunk : (s + 1) * chunk] for s in range(n_pipe)]
    gram_in_low = over_dp(down_low)
    up_low, up_high = products(False, BLOCKS)
    gram_out_low = over_dp(up_low)
    columns = [dot(rows, weight_in[s], ROWS) for s in range(first, middle)]
    columns += split_scalars([jnp.sum(wide * wide, axis=1, keepdims=True)])
    columns += [dot(rows, weight_out[s], LAST) for s in range(first, middle - 1)]
    columns, up_low = lax.optimization_barrier((columns, up_low))
    sums_low = exchanged(columns, n_pipe)
    columns = [dot(seed, weight_out[s], LAST) for s in range(middle, last)]
    columns, sums_low = lax.optimization_barrier((columns, sums_low))
    grad_high = exchanged(columns, n_pipe)
    columns = jnp.concatenate([down_high, up_high], axis=1)
    gram_in_low, gram_out_low, sums_low, grad_high, columns = lax.optimization_barrier(
        (gram_in_low, gram_out_low, sums_low, grad_high, columns)
    )
    gram_high = over_dp(columns)

    kept = len(kept_crosses(first, middle))
    acts, hidden, scale, cross = run(
        forward_kernel(first, middle, width, inner, n_pipe),
        [
            ((tok_rows, count * inner), jnp.bfloat16),
            ((count, block, inner), jnp.float32),
            ((count, block, LANES), jnp.float32),
            ((kept, block, inner), jnp.float32),
        ],
        sums_low,
        gram_in_low,
        gram_out_low,
    )
    acts = swap(acts, "pipe")
    exact, columns = run(
        next_rows_kernel(first, middle, last, inner, chunk),
        [
            ((tok_rows, chunk), jnp.float32),
            ((tok_rows, (2 * (last - middle) - 1) * inner + LANES), jnp.bfloat16),
        ],
        rows,
        acts,
        all_in,
        all_out,
        specs={
            2: pl.BlockSpec(
                ((last - middle) * chunk, inner), lambda step: (middle // (last - middle), 0)
            )
        },
    )
    sums = exchanged(columns, n_pipe)

    turned = run(
        turning_kernel(middle, last, width, inner, n_pipe),
        [((tok_rows, 2 * (last - middle) * inner + LANES), jnp.bfloat16)],
        sums,
        grad_high,
        gram_high,
    )[0]
    turned = swap(turned, "pipe")

    def packed_shape(group):
        rows_packed = 2 * group * chunk * inner // (n_dp * LANES)
        return (n_dp // 2, rows_packed, LANES)

    dp = lax.axis_index("dp")
    core, chip = dp % 2, dp // 2
    chips = jnp.arange(n_dp // 2)
    xs = n_dp // 4
    away = (chips // 2 - chip // 2 + xs) % xs * 2 + (chips % 2 + chip % 2) % 2
    place = jnp.concatenate([away, core[None]]).astype(jnp.int32)

    grads_high, mine, other, upstream, columns = run(
        grads_kernel(middle, last, first, inner, chunk, n_dp, (last - middle) * inner + LANES),
        [
            ((last - middle, tok_rows, chunk), jnp.bfloat16),
            (packed_shape(last - middle), jnp.bfloat16),
            (packed_shape(last - middle), jnp.bfloat16),
            ((tok_rows, chunk), jnp.float32),
            ((tok_rows, count * inner), jnp.bfloat16),
        ],
        place,
        exact,
        turned,
        turned,
        seed,
        all_in,
        all_out,
        smem=True,
    )
    grad_low = exchanged(columns, n_pipe)
    other = other_core(other, n_dp)
    grad_low, mine, other = lax.optimization_barrier((grad_low, mine, other))
    arrived_high = between_chips(added(mine, other, mine.shape[0]), n_dp)

    packs = run(
        backward_kernel(first, middle, width, inner, n_pipe),
        [((tok_rows, count * inner + LANES), jnp.bfloat16)],
        grad_low,
        hidden,
        scale,
        cross,
        gram_in_low,
    )[0]
    packs = swap(packs, "pipe")
    grads, mine, other, _ = run(
        grads_kernel(first, middle, first, inner, chunk, n_dp, 0),
        [
            ((n_pipe, tok_rows, chunk), jnp.bfloat16),
            (packed_shape(count), jnp.bfloat16),
            (packed_shape(count), jnp.bfloat16),
            ((tok_rows, chunk), jnp.float32),
        ],
        place,
        rows,
        packs,
        acts,
        upstream,
        all_in,
        all_out,
        grads_high,
        smem=True,
    )
    mine, other, arrived_high = lax.optimization_barrier((mine, other, arrived_high))
    blocks = added(mine, other_core(other, n_dp), mine.shape[0])
    arrived_low = between_chips(blocks, n_dp)
    input_grads = swap(grads, "pipe")
    input_grads, arrived_low = lax.optimization_barrier((input_grads, arrived_low))

    ins, outs = [], []
    for (low, high), arrived in zip(BLOCKS, (arrived_low, arrived_high)):
        share = (high - low) * chunk // n_dp
        sum_in, sum_out = run(
            unpack_kernel(inner, share, len(arrived)),
            [
                ((share, inner), jnp.bfloat16),
                ((arrived[0].shape[-2] - share * inner // LANES, LANES), jnp.bfloat16),
            ],
            *arrived,
        )
        ins.append(sum_in)
        outs.append(sum_out.reshape(high - low, -1, LANES))
    grad_out = swap(jnp.concatenate(outs, axis=0), "pipe")
    grad_in = move_in(*ins, n_pipe, n_dp)
    is_high = (me >= middle).astype(jnp.int32).reshape(1)

    shape_in, shape_out = (share_in, inner), (share_out, width)
    *updated, pieces = run(
        adam_kernel(share_out, chunk // LANES, share_in),
        [(shape_in, jnp.float32)] * 3
        + [(shape_out, jnp.float32)] * 3
        + [((n_dp, 2, share_out, share_in), jnp.bfloat16)],
        is_high,
        *grad_in,
        grad_out,
        master_in[0],
        moment_in[0],
        second_in[0],
        master_out[0],
        moment_out[0],
        second_out[0],
        smem=True,
    )
    new_in, new_moment_in, new_second_in, new_out, new_moment_out, new_second_out = updated
    input_grads = columns_in_place(input_grads)[None]
    roll_in, roll_out = run(
        rollout_kernel(share_out, share_in),
        [(shape_out, jnp.bfloat16), (shape_in, jnp.bfloat16)],
        swap(pieces, "dp"),
    )
    return (
        input_grads,
        new_in[None],
        new_moment_in[None],
        new_second_in[None],
        new_out[None],
        new_moment_out[None],
        new_second_out[None],
        roll_in[None],
        roll_out[None],
    )


def solution(mesh):
    in_specs = (P("dp", None), P("dp", None)) + (P("pipe", "dp", None),) * 6
    out_specs = (P("pipe", "dp", None),) * 9
    return jax.shard_map(
        on_device, mesh=mesh, in_specs=in_specs, out_specs=out_specs, check_vma=False
    )
```

```python
import jax
import jax.numpy as jnp
from jax import lax
from jax.experimental import pallas as pl
from jax.experimental.pallas import tpu as pltpu
from jax.sharding import PartitionSpec as P

norm_eps = 1e-06
beta_one = 0.9
beta_two = 0.999
learn_rate = 0.02
decay_rate = 0.1
adam_eps = 1e-08
adam_step = 100

BLOCKS = ((0, 4), (4, 8))
LANES = 128
VMEM_BYTES = 60 * 1024 * 1024


def dot(left, right, dims):
    return lax.dot_general(left, right, (dims, ((), ())), preferred_element_type=jnp.float32)


ROWS = ((1,), (0,))
LAST = ((1,), (1,))
FIRST = ((0,), (0,))


def swap(x, axis):
    return lax.all_to_all(x, axis, 0, 0, tiled=True)


def split_scalars(scalars):
    columns = []
    for value in scalars:
        high = value.astype(jnp.bfloat16)
        columns += [high, (value - high.astype(jnp.float32)).astype(jnp.bfloat16)]
    columns.append(jnp.zeros((scalars[0].shape[0], 128 - len(columns)), jnp.bfloat16))
    return columns


def exchanged(columns, count):
    packed = columns
    if isinstance(columns, list):
        packed = jnp.concatenate([c.astype(jnp.bfloat16) for c in columns], axis=1)
    return swap(packed, "pipe").reshape(count, packed.shape[0] // count, packed.shape[1])


def adam_update(master, moment, second, grad):
    moment_new = beta_one * moment + (1.0 - beta_one) * grad
    second_new = beta_two * second + (1.0 - beta_two) * grad * grad
    moment_hat = moment_new / (1.0 - beta_one**adam_step)
    second_hat = second_new / (1.0 - beta_two**adam_step)
    master_new = master - learn_rate * (
        moment_hat / (jnp.sqrt(second_hat) + adam_eps) + decay_rate * master
    )
    return (master_new, moment_new, second_new)


def run(kernel, shapes, *operands, specs=None, smem=False):
    more = {}
    if specs is not None:
        whole = [pl.BlockSpec(x.shape, zeros_map(x.ndim)) for x in operands]
        outs = [pl.BlockSpec(shape, zeros_map(len(shape))) for shape, _ in shapes]
        given = [specs.get(at, spec) for at, spec in enumerate(whole)]
        more = {"grid": (1,), "in_specs": given, "out_specs": outs}
    if smem:
        rest = [pl.BlockSpec(memory_space=pltpu.VMEM)] * (len(operands) - 1)
        more = {"in_specs": [pl.BlockSpec(memory_space=pltpu.SMEM)] + rest}
    return pl.pallas_call(
        kernel,
        out_shape=[jax.ShapeDtypeStruct(shape, kind) for shape, kind in shapes],
        compiler_params=pltpu.CompilerParams(vmem_limit_bytes=VMEM_BYTES),
        **more,
    )(*operands)


def columns_in_place(x):
    count, rows, columns = x.shape

    def kernel(x_ref, out_ref):
        out_ref[...] = x_ref[0]

    return pl.pallas_call(
        kernel,
        out_shape=jax.ShapeDtypeStruct((rows, count * columns), x.dtype),
        grid=(count,),
        in_specs=[pl.BlockSpec((1, rows, columns), lambda at: (at, 0, 0))],
        out_specs=pl.BlockSpec((rows, columns), lambda at: (0, at)),
        compiler_params=pltpu.CompilerParams(vmem_limit_bytes=VMEM_BYTES),
    )(x)


def zeros_map(ndim):
    return lambda step: (0,) * ndim


def part(ref, at, inner):
    return ref[:, at * inner : (at + 1) * inner]


def scalar_block(scalars):
    lane = lax.broadcasted_iota(jnp.int32, (scalars[0].shape[0], LANES), 1)
    packed = jnp.zeros(lane.shape, jnp.float32)
    for at, value in enumerate(scalars):
        high = value.astype(jnp.bfloat16).astype(jnp.float32)
        packed = jnp.where(lane == 2 * at, high, packed)
        packed = jnp.where(lane == 2 * at + 1, value - high, packed)
    return packed.astype(jnp.bfloat16)


def summed_part(ref, start, size):
    total = ref[0, :, start : start + size].astype(jnp.float32)
    for source in range(1, ref.shape[0]):
        total = total + ref[source, :, start : start + size].astype(jnp.float32)
    return total


def down_units(first, last):
    return [(j, t, True) for j in range(first, last) for t in range(j + 1, last)]


def up_units(first, last):
    return [(j, t, False) for j in range(first, last - 1) for t in range(j, last - 1)]


def finder(first, last, inner, down_ref, up_ref, up_start):
    places = {unit: (down_ref, at) for at, unit in enumerate(down_units(first, last))}
    if up_ref is not None:
        for at, unit in enumerate(up_units(first, last)):
            places[unit] = (up_ref, up_start + at)

    def find(unit):
        ref, at = places[unit]
        return part(ref, at, inner)

    return find


def forward_chain(first, last, width, inner, down_ref, up_ref, up_start, find):
    count = last - first
    raw = {s: summed_part(down_ref, (s - first) * inner, inner) for s in range(first, last)}
    cross = {
        s: summed_part(up_ref, up_start + (s - first) * inner, inner)
        for s in range(first, last - 1)
    }
    square = summed_part(down_ref, count * inner, LANES)
    square = square[:, 0:1] + square[:, 1:2]
    state, crosses = {}, {}
    for s in range(first, last):
        scale = lax.rsqrt(jnp.maximum(square, 0.0) / width + norm_eps)
        hidden = raw[s] * scale
        gate = jax.nn.sigmoid(hidden)
        act = (hidden * gate).astype(jnp.bfloat16)
        state[s] = (hidden, scale, act)
        if s == last - 1:
            break
        added = {}
        for k in range(first, last - 1):
            if k >= s:
                added[k] = dot(act, find((s, k, False)), ROWS)
            else:
                added[k] = dot(act, find((k, s, False)), LAST)
        wide = act.astype(jnp.float32)
        square = square + jnp.sum(wide * (2.0 * cross[s] + added[s]), axis=1, keepdims=True)
        cross = {k: cross[k] + added[k] for k in cross}
        for t in range(s + 1, last):
            raw[t] = raw[t] + dot(act, find((s, t, True)), ROWS)
        crosses[s + 1] = cross
    return state, crosses


def backward_chain(first, last, width, inner, grad_ref, hidden_of, scale_of, cross_of, find):
    grad_act = {s: summed_part(grad_ref, (s - first) * inner, inner) for s in range(first, last)}
    packs, pulls = {}, {}
    for s in reversed(range(first, last)):
        hidden, scale = hidden_of(s), scale_of(s)
        gate = jax.nn.sigmoid(hidden)
        grad_hidden = grad_act[s] * gate * (1.0 + hidden * (1.0 - gate))
        mean = jnp.sum(grad_hidden * hidden, axis=1, keepdims=True) / width
        packs[s] = (grad_hidden * scale).astype(jnp.bfloat16)
        pulls[s] = mean * scale * scale
        for t in range(first, s):
            grad_act[t] = (
                grad_act[t]
                + dot(packs[s], find((t, s, True)), LAST)
                - pulls[s] * cross_of(s, t)
            )
    return packs, pulls


def kept_crosses(first, last):
    return [(s, t) for s in range(first + 1, last) for t in range(first, s)]


def forward_kernel(first, last, width, inner, copies):
    def kernel(
        down_ref, up_ref, gram_in_ref, gram_out_ref, acts_ref, hidden_ref, scale_ref, cross_ref
    ):
        find = finder(first, last, inner, gram_in_ref, gram_out_ref, 0)
        state, crosses = forward_chain(first, last, width, inner, down_ref, up_ref, 0, find)
        rows = down_ref.shape[1]
        for s in range(first, last):
            hidden, scale, act = state[s]
            at = s - first
            for copy in range(copies):
                acts_ref[copy * rows : (copy + 1) * rows, at * inner : (at + 1) * inner] = act
            hidden_ref[at] = hidden
            scale_ref[at] = jnp.broadcast_to(scale, (rows, LANES))
        for at, (s, t) in enumerate(kept_crosses(first, last)):
            cross_ref[at] = crosses[s][t]

    return kernel


def store_packs(ref, packs, pulls, first, last, inner, rows, copies):
    scalars = scalar_block([pulls[s] for s in range(first, last)])
    for copy in range(copies):
        there = slice(copy * rows, (copy + 1) * rows)
        for s in range(first, last):
            ref[there, (s - first) * inner : (s - first + 1) * inner] = packs[s]
        at = (last - first) * inner
        ref[there, at : at + LANES] = scalars


def backward_kernel(first, last, width, inner, copies):
    kept = {pair: at for at, pair in enumerate(kept_crosses(first, last))}

    def kernel(grad_ref, hidden_ref, scale_ref, cross_ref, gram_ref, out_ref):
        packs, pulls = backward_chain(
            first,
            last,
            width,
            inner,
            grad_ref,
            lambda s: hidden_ref[s - first],
            lambda s: scale_ref[s - first][:, 0:1],
            lambda s, t: cross_ref[kept[(s, t)]],
            finder(first, last, inner, gram_ref, None, 0),
        )
        store_packs(out_ref, packs, pulls, first, last, inner, grad_ref.shape[1], copies)

    return kernel


def turning_kernel(first, last, width, inner, copies):
    def kernel(sums_ref, grad_ref, gram_ref, out_ref):
        count = last - first
        find = finder(first, last, inner, gram_ref, gram_ref, len(down_units(first, last)))
        state, crosses = forward_chain(
            first, last, width, inner, sums_ref, sums_ref, count * inner + LANES, find
        )
        packs, pulls = backward_chain(
            first,
            last,
            width,
            inner,
            grad_ref,
            lambda s: state[s][0],
            lambda s: state[s][1],
            lambda s, t: crosses[s][t],
            find,
        )
        rows = sums_ref.shape[1]
        store_packs(out_ref, packs, pulls, first, last, inner, rows, copies)
        for copy in range(copies):
            for s in range(first, last):
                at = count * inner + LANES + (s - first) * inner
                out_ref[copy * rows : (copy + 1) * rows, at : at + inner] = state[s][2]

    return kernel


def next_rows_kernel(first, last, then, inner, chunk):
    def kernel(rows_ref, acts_ref, in_ref, out_ref, exact_ref, columns_ref):
        exact = rows_ref[...].astype(jnp.float32)
        for s in range(first, last):
            exact = exact + dot(
                part(acts_ref, s - first, inner), part(out_ref, s, chunk), ROWS
            )
        exact_ref[...] = exact
        rows = exact.astype(jnp.bfloat16)
        at = 0
        for s in range(last, then):
            weight = in_ref[(s - last) * chunk : (s - last + 1) * chunk]
            columns_ref[:, at : at + inner] = dot(rows, weight, ROWS).astype(jnp.bfloat16)
            at += inner
        squares = jnp.sum(exact * exact, axis=1, keepdims=True)
        columns_ref[:, at : at + LANES] = scalar_block([squares])
        at += LANES
        for s in range(last, then - 1):
            columns = dot(rows, part(out_ref, s, chunk), LAST)
            columns_ref[:, at : at + inner] = columns.astype(jnp.bfloat16)
            at += inner

    return kernel


def grads_kernel(first, last, before, inner, chunk, n_dp, acts_start):
    group = last - first
    share_in = group * chunk // n_dp
    share_out = inner // n_dp
    lanes_in = inner // LANES
    lanes_out = chunk // LANES

    def kernel(*refs):
        place_ref, exact_ref, packs_ref, acts_ref, up_ref, in_ref, out_ref = refs[:7]
        refs = refs[7:]
        if first == 0:
            refs[1][last:] = refs[0][...]
            refs = refs[1:]
        grads_ref, mine_ref, other_ref, up_new_ref = refs[:4]
        exact = exact_ref[...].astype(jnp.float32)
        rows = {first: exact.astype(jnp.bfloat16)}

        def act_of(s):
            at = acts_start + (s - first) * inner
            return acts_ref[:, at : at + inner]

        for s in range(first, last - 1):
            exact = exact + dot(act_of(s), part(out_ref, s, chunk), ROWS)
            rows[s + 1] = exact.astype(jnp.bfloat16)
        upstream = up_ref[...].astype(jnp.float32)
        narrow = upstream.astype(jnp.bfloat16)
        for s in reversed(range(first, last)):
            pack = part(packs_ref, s - first, inner)
            at = group * inner + 2 * (s - first)
            pull = packs_ref[:, group * inner : group * inner + LANES].astype(jnp.float32)
            at = 2 * (s - first)
            pull = pull[:, at : at + 1] + pull[:, at + 1 : at + 2]
            into = dot(rows[s], pack, FIRST).astype(jnp.bfloat16)
            onto = dot(act_of(s), narrow, FIRST).astype(jnp.bfloat16)
            base = lanes_in * share_in + (s - first) * lanes_out * share_out

            def store(refs_of, into=into, onto=onto, base=base, s=s):
                for piece in range(chunk // share_in):
                    device = (s - first) * (chunk // share_in) + piece
                    ref = refs_of[device % 2]
                    for c in range(lanes_in):
                        ref[place_ref[device // 2], c * share_in : (c + 1) * share_in] = into[
                            piece * share_in : (piece + 1) * share_in,
                            c * LANES : (c + 1) * LANES,
                        ]
                for device in range(n_dp):
                    ref = refs_of[device % 2]
                    for c in range(lanes_out):
                        row = base + c * share_out
                        ref[place_ref[device // 2], row : row + share_out] = onto[
                            device * share_out : (device + 1) * share_out,
                            c * LANES : (c + 1) * LANES,
                        ]

            @pl.when(place_ref[n_dp // 2] == 0)
            def _():
                store((mine_ref, other_ref))

            @pl.when(place_ref[n_dp // 2] == 1)
            def _():
                store((other_ref, mine_ref))

            weight = in_ref[s * chunk : (s + 1) * chunk]
            upstream = (
                upstream + dot(pack, weight, LAST) - pull * rows[s].astype(jnp.float32)
            )
            narrow = upstream.astype(jnp.bfloat16)
            grads_ref[s - first] = narrow
        up_new_ref[...] = upstream
        if before < first:
            for s in range(before, first):
                columns = dot(narrow, part(out_ref, s, chunk), LAST).astype(jnp.bfloat16)
                refs[4][:, (s - before) * inner : (s - before + 1) * inner] = columns

    return kernel


def unpack_kernel(inner, share_in, sources):
    def kernel(*refs):
        in_ref, out_ref = refs[sources:]
        given = refs[:sources]
        if sources == 1:
            given = [refs[0].at[k] for k in range(refs[0].shape[0])]
        lanes = inner // LANES

        def total_of(start, stop):
            total = given[0][start:stop].astype(jnp.float32)
            for ref in given[1:]:
                total = total + ref[start:stop].astype(jnp.float32)
            return total.astype(jnp.bfloat16)

        for c in range(lanes):
            in_ref[:, c * LANES : (c + 1) * LANES] = total_of(c * share_in, (c + 1) * share_in)
        out_ref[...] = total_of(lanes * share_in, given[0].shape[0])

    return kernel


def adam_kernel(share, lanes, share_in):
    def kernel(*refs):
        swapped_ref, one_ref, two_ref, onto_ref = refs[:4]
        state_in, state_out = refs[4:7], refs[7:10]
        new_in, new_out, pieces_ref = refs[10:13], refs[13:16], refs[16]
        per = LANES // share
        for c in range(one_ref.shape[1] // LANES):
            there = slice(c * LANES, (c + 1) * LANES)
            one = one_ref[:, there].astype(jnp.float32)
            two = two_ref[:, there].astype(jnp.float32)
            swapped = swapped_ref[0] == 1
            grad = jnp.concatenate(
                [jnp.where(swapped, two, one), jnp.where(swapped, one, two)], axis=0
            )
            results = adam_update(*(ref[:, there] for ref in state_in), grad)
            for ref, value in zip(new_in, results):
                ref[:, there] = value
            turned = results[0].T.astype(jnp.bfloat16)
            for q in range(per):
                pieces_ref[c * per + q, 0] = turned[q * share : (q + 1) * share]
        for device in range(onto_ref.shape[0]):
            for c in range(lanes):
                at = (device * lanes + c) * LANES
                grad = onto_ref[device, c * share : (c + 1) * share].astype(jnp.float32)
                results = adam_update(*(ref[:, at : at + LANES] for ref in state_out), grad)
                for ref, value in zip(new_out, results):
                    ref[:, at : at + LANES] = value
        for device in range(pieces_ref.shape[0]):
            at = device * share_in
            start = at // LANES * LANES
            stop = -(-(at + share_in) // LANES) * LANES
            values = new_out[0][:, start:stop][:, at - start : at - start + share_in]
            pieces_ref[device, 1] = values.astype(jnp.bfloat16)

    return kernel


def rollout_kernel(share, share_in):
    def kernel(pieces_ref, in_ref, out_ref):
        per = LANES // share
        for pair in range(pieces_ref.shape[0] // 2):
            both = [pieces_ref[2 * pair + h, 0].astype(jnp.float32) for h in range(2)]
            at = 2 * pair * share_in
            in_ref[:, at : at + 2 * share_in] = jnp.concatenate(both, axis=1).astype(jnp.bfloat16)
        for c in range(pieces_ref.shape[0] // per):
            rows = [pieces_ref[c * per + q, 1].astype(jnp.float32) for q in range(per)]
            out_ref[:, c * LANES : (c + 1) * LANES] = jnp.concatenate(rows, axis=0).T.astype(
                jnp.bfloat16
            )

    return kernel


def columns_kernel(orders):
    def kernel(every_ref, *out_refs):
        size = every_ref.shape[2]
        for out_ref, order in zip(out_refs, orders):
            for at, unit in enumerate(order):
                out_ref[:, at * size : (at + 1) * size] = every_ref[unit]

    return kernel


def other_core(x, n_dp):
    return lax.ppermute(x, "dp", [(j, j + 1 - 2 * (j % 2)) for j in range(n_dp)])


def add_kernel(mine_ref, other_ref, *out_refs):
    for at in range(mine_ref.shape[0]):
        total = mine_ref[at].astype(jnp.float32) + other_ref[at].astype(jnp.float32)
        if len(out_refs) == 1:
            out_refs[0][at] = total.astype(jnp.bfloat16)
        else:
            out_refs[at][...] = total.astype(jnp.bfloat16)


def added(mine, other, count):
    shape = mine.shape if count == 1 else mine.shape[1:]
    return run(add_kernel, [(shape, jnp.bfloat16)] * count, mine, other)


def chip_steps(n_dp):
    return [(dx, dz) for dx in range(n_dp // 4) for dz in range(2)]


def between_chips(blocks, n_dp):
    arrived = [blocks[0]]
    for (dx, dz), block in list(zip(chip_steps(n_dp), blocks))[1:]:
        pairs = []
        for j in range(n_dp):
            x, z, core = j // 4, j // 2 % 2, j % 2
            pairs.append((j, (x + dx) % (n_dp // 4) * 4 + (z ^ dz) * 2 + core))
        arrived.append(lax.ppermute(block, "dp", pairs))
    return arrived


def move_in(low, high, n_pipe, n_dp):
    odd = lax.axis_index("dp") % 2 == 1
    group = n_pipe // 2
    moved = []
    for q in range(2):
        pairs = []
        for i in range(n_pipe):
            for j in range(n_dp):
                section = j * group // n_dp + (0 if j % 2 == q else group)
                pairs.append((i * n_dp + j, section * n_dp + 2 * i + j // 2 % 2))
        payload = jnp.where(odd, low, high) if q == 1 else jnp.where(odd, high, low)
        moved.append(lax.ppermute(payload, ("pipe", "dp"), pairs))
    return moved


def on_device(
    inputs_x, cotangent, master_in, master_out, moment_in, moment_out, second_in, second_out
):
    n_pipe = lax.axis_size("pipe")
    n_dp = lax.axis_size("dp")
    me = lax.axis_index("pipe")
    tok_rows, width = inputs_x.shape
    chunk = width // n_pipe
    inner = master_in.shape[2]
    share_in = master_in.shape[1]
    share_out = master_out.shape[1]
    block = tok_rows // n_pipe

    own_in = master_in[0].astype(jnp.bfloat16)
    own_out = master_out[0].astype(jnp.bfloat16)
    pairs = [
        (s * n_dp + 2 * i + h, i * n_dp + 2 * s + h)
        for s in range(n_pipe)
        for i in range(n_pipe)
        for h in range(2)
    ]
    piece_in = lax.ppermute(own_in, ("pipe", "dp"), pairs)
    piece_out = swap(own_out.reshape(share_out, n_pipe, chunk).transpose(1, 0, 2), "pipe")
    flat_out = piece_out.transpose(1, 0, 2).reshape(share_out, width)
    all_in = lax.all_gather(piece_in, "dp", axis=0, tiled=True)
    all_out = lax.all_gather(flat_out, "dp", axis=0, tiled=True)
    weight_in = [all_in[s * chunk : (s + 1) * chunk] for s in range(n_pipe)]

    def products(down, blocks):
        units, partial, orders = [], [], []
        for first, last in blocks:
            wanted = (down_units if down else up_units)(first, last)
            for t in sorted({t for _, t, _ in wanted}):
                ks = [k for k, other, _ in wanted if other == t]
                left = piece_out[ks[0] : ks[-1] + 1].reshape(-1, chunk)
                if down:
                    partial.append(dot(left, weight_in[t], ROWS))
                else:
                    partial.append(dot(left, weight_out[t], LAST))
                units += [(k, t, down) for k in ks]
        for first, last in blocks:
            wanted = (down_units if down else up_units)(first, last)
            orders.append([units.index(unit) for unit in wanted])
        partial = [p.astype(jnp.bfloat16) for p in partial]
        arrived = swap(jnp.concatenate(partial, axis=0), "pipe")
        arrived = arrived.reshape(n_pipe, -1, inner)
        mine = jnp.sum(arrived.astype(jnp.float32), axis=0).astype(jnp.bfloat16)
        every = swap(jnp.tile(mine, (n_pipe, 1)), "pipe").reshape(-1, share_out, inner)
        shapes = [((share_out, len(order) * inner), jnp.bfloat16) for order in orders]
        return run(columns_kernel(orders), shapes, every)

    def over_dp(columns):
        return lax.all_gather(columns, "dp", axis=0, tiled=True)

    rows = lax.dynamic_slice_in_dim(inputs_x, me * chunk, chunk, 1)
    seed = lax.dynamic_slice_in_dim(cotangent, me * chunk, chunk, 1)

    (first, middle), (_, last) = BLOCKS
    count = middle - first
    wide = rows.astype(jnp.float32)
    down_low, down_high = products(True, BLOCKS)
    columns = [dot(rows, weight_in[s], ROWS) for s in range(first, middle)]
    columns += split_scalars([jnp.sum(wide * wide, axis=1, keepdims=True)])
    down = exchanged(columns, n_pipe)
    all_out, down_low, down = lax.optimization_barrier((all_out, down_low, down))
    weight_out = [all_out[:, s * chunk : (s + 1) * chunk] for s in range(n_pipe)]
    gram_in_low = over_dp(down_low)
    up_low, up_high = products(False, BLOCKS)
    gram_out_low = over_dp(up_low)
    columns = [dot(rows, weight_out[s], LAST) for s in range(first, middle - 1)]
    columns, up_low = lax.optimization_barrier((columns, up_low))
    up = exchanged(columns, n_pipe)
    columns = [dot(seed, weight_out[s], LAST) for s in range(middle, last)]
    columns, up = lax.optimization_barrier((columns, up))
    grad_high = exchanged(columns, n_pipe)
    columns = jnp.concatenate([down_high, up_high], axis=1)
    gram_in_low, gram_out_low, up, grad_high, columns = lax.optimization_barrier(
        (gram_in_low, gram_out_low, up, grad_high, columns)
    )
    gram_high = over_dp(columns)

    kept = len(kept_crosses(first, middle))
    acts, hidden, scale, cross = run(
        forward_kernel(first, middle, width, inner, n_pipe),
        [
            ((tok_rows, count * inner), jnp.bfloat16),
            ((count, block, inner), jnp.float32),
            ((count, block, LANES), jnp.float32),
            ((kept, block, inner), jnp.float32),
        ],
        down,
        up,
        gram_in_low,
        gram_out_low,
    )
    acts = swap(acts, "pipe")
    exact, columns = run(
        next_rows_kernel(first, middle, last, inner, chunk),
        [
            ((tok_rows, chunk), jnp.float32),
            ((tok_rows, (2 * (last - middle) - 1) * inner + LANES), jnp.bfloat16),
        ],
        rows,
        acts,
        all_in,
        all_out,
        specs={
            2: pl.BlockSpec(
                ((last - middle) * chunk, inner), lambda step: (middle // (last - middle), 0)
            )
        },
    )
    sums = exchanged(columns, n_pipe)

    turned = run(
        turning_kernel(middle, last, width, inner, n_pipe),
        [((tok_rows, 2 * (last - middle) * inner + LANES), jnp.bfloat16)],
        sums,
        grad_high,
        gram_high,
    )[0]
    turned = swap(turned, "pipe")

    def packed_shape(group):
        rows_packed = 2 * group * chunk * inner // (n_dp * LANES)
        return (n_dp // 2, rows_packed, LANES)

    dp = lax.axis_index("dp")
    core, chip = dp % 2, dp // 2
    chips = jnp.arange(n_dp // 2)
    xs = n_dp // 4
    away = (chips // 2 - chip // 2 + xs) % xs * 2 + (chips % 2 + chip % 2) % 2
    place = jnp.concatenate([away, core[None]]).astype(jnp.int32)

    grads_high, mine, other, upstream, columns = run(
        grads_kernel(middle, last, first, inner, chunk, n_dp, (last - middle) * inner + LANES),
        [
            ((last - middle, tok_rows, chunk), jnp.bfloat16),
            (packed_shape(last - middle), jnp.bfloat16),
            (packed_shape(last - middle), jnp.bfloat16),
            ((tok_rows, chunk), jnp.float32),
            ((tok_rows, count * inner), jnp.bfloat16),
        ],
        place,
        exact,
        turned,
        turned,
        seed,
        all_in,
        all_out,
        smem=True,
    )
    grad_low = exchanged(columns, n_pipe)
    other = other_core(other, n_dp)
    grad_low, mine, other = lax.optimization_barrier((grad_low, mine, other))
    arrived_high = between_chips(added(mine, other, mine.shape[0]), n_dp)

    packs = run(
        backward_kernel(first, middle, width, inner, n_pipe),
        [((tok_rows, count * inner + LANES), jnp.bfloat16)],
        grad_low,
        hidden,
        scale,
        cross,
        gram_in_low,
    )[0]
    packs = swap(packs, "pipe")
    grads, mine, other, _ = run(
        grads_kernel(first, middle, first, inner, chunk, n_dp, 0),
        [
            ((n_pipe, tok_rows, chunk), jnp.bfloat16),
            (packed_shape(count), jnp.bfloat16),
            (packed_shape(count), jnp.bfloat16),
            ((tok_rows, chunk), jnp.float32),
        ],
        place,
        rows,
        packs,
        acts,
        upstream,
        all_in,
        all_out,
        grads_high,
        smem=True,
    )

    def unpacked(arrived, group):
        share = group * chunk // n_dp
        rows_out = arrived[0].shape[-2] - share * inner // LANES
        sum_in, sum_out = run(
            unpack_kernel(inner, share, len(arrived)),
            [((share, inner), jnp.bfloat16), ((rows_out, LANES), jnp.bfloat16)],
            *arrived,
        )
        return sum_in, sum_out.reshape(group, -1, LANES)

    high = unpacked(arrived_high, last - middle)
    mine, other, high = lax.optimization_barrier((mine, other, high))
    blocks = added(mine, other_core(other, n_dp), mine.shape[0])
    arrived_low = between_chips(blocks, n_dp)
    input_grads = swap(grads, "pipe")
    input_grads, arrived_low = lax.optimization_barrier((input_grads, arrived_low))
    ins, outs = zip(unpacked(arrived_low, count), high)
    grad_out = swap(jnp.concatenate(outs, axis=0), "pipe")
    grad_in = move_in(*ins, n_pipe, n_dp)
    is_high = (me >= middle).astype(jnp.int32).reshape(1)

    shape_in, shape_out = (share_in, inner), (share_out, width)
    *updated, pieces = run(
        adam_kernel(share_out, chunk // LANES, share_in),
        [(shape_in, jnp.float32)] * 3
        + [(shape_out, jnp.float32)] * 3
        + [((n_dp, 2, share_out, share_in), jnp.bfloat16)],
        is_high,
        *grad_in,
        grad_out,
        master_in[0],
        moment_in[0],
        second_in[0],
        master_out[0],
        moment_out[0],
        second_out[0],
        smem=True,
    )
    new_in, new_moment_in, new_second_in, new_out, new_moment_out, new_second_out = updated
    input_grads = columns_in_place(input_grads)[None]
    roll_in, roll_out = run(
        rollout_kernel(share_out, share_in),
        [(shape_out, jnp.bfloat16), (shape_in, jnp.bfloat16)],
        swap(pieces, "dp"),
    )
    return (
        input_grads,
        new_in[None],
        new_moment_in[None],
        new_second_in[None],
        new_out[None],
        new_moment_out[None],
        new_second_out[None],
        roll_in[None],
        roll_out[None],
    )


def solution(mesh):
    in_specs = (P("dp", None), P("dp", None)) + (P("pipe", "dp", None),) * 6
    out_specs = (P("pipe", "dp", None),) * 9
    return jax.shard_map(
        on_device, mesh=mesh, in_specs=in_specs, out_specs=out_specs, check_vma=False
    )
```

```python
import jax
import jax.numpy as jnp
from jax import lax
from jax.experimental import pallas as pl
from jax.experimental.pallas import tpu as pltpu
from jax.sharding import PartitionSpec as P

norm_eps = 1e-06
beta_one = 0.9
beta_two = 0.999
learn_rate = 0.02
decay_rate = 0.1
adam_eps = 1e-08
adam_step = 100

BLOCKS = ((0, 4), (4, 8))
LANES = 128
VMEM_BYTES = 48 * 1024 * 1024


def dot(left, right, dims):
    return lax.dot_general(left, right, (dims, ((), ())), preferred_element_type=jnp.float32)


ROWS = ((1,), (0,))
LAST = ((1,), (1,))
FIRST = ((0,), (0,))


def swap(x, axis):
    return lax.all_to_all(x, axis, 0, 0, tiled=True)


def split_scalars(scalars):
    columns = []
    for value in scalars:
        high = value.astype(jnp.bfloat16)
        columns += [high, (value - high.astype(jnp.float32)).astype(jnp.bfloat16)]
    columns.append(jnp.zeros((scalars[0].shape[0], 128 - len(columns)), jnp.bfloat16))
    return columns


def exchanged(columns, count):
    packed = columns
    if isinstance(columns, list):
        packed = jnp.concatenate([c.astype(jnp.bfloat16) for c in columns], axis=1)
    return swap(packed, "pipe").reshape(count, packed.shape[0] // count, packed.shape[1])


def adam_update(master, moment, second, grad):
    moment_new = beta_one * moment + (1.0 - beta_one) * grad
    second_new = beta_two * second + (1.0 - beta_two) * grad * grad
    moment_hat = moment_new / (1.0 - beta_one**adam_step)
    second_hat = second_new / (1.0 - beta_two**adam_step)
    master_new = master - learn_rate * (
        moment_hat / (jnp.sqrt(second_hat) + adam_eps) + decay_rate * master
    )
    return (master_new, moment_new, second_new)


def run(kernel, shapes, *operands, specs=None, smem=False):
    more = {}
    if specs is not None:
        whole = [pl.BlockSpec(x.shape, zeros_map(x.ndim)) for x in operands]
        outs = [pl.BlockSpec(shape, zeros_map(len(shape))) for shape, _ in shapes]
        given = [specs.get(at, spec) for at, spec in enumerate(whole)]
        more = {"grid": (1,), "in_specs": given, "out_specs": outs}
    if smem:
        rest = [pl.BlockSpec(memory_space=pltpu.VMEM)] * (len(operands) - 1)
        more = {"in_specs": [pl.BlockSpec(memory_space=pltpu.SMEM)] + rest}
    return pl.pallas_call(
        kernel,
        out_shape=[jax.ShapeDtypeStruct(shape, kind) for shape, kind in shapes],
        compiler_params=pltpu.CompilerParams(vmem_limit_bytes=VMEM_BYTES),
        **more,
    )(*operands)


def columns_in_place(x):
    count, rows, columns = x.shape

    def kernel(x_ref, out_ref):
        out_ref[...] = x_ref[0]

    return pl.pallas_call(
        kernel,
        out_shape=jax.ShapeDtypeStruct((rows, count * columns), x.dtype),
        grid=(count,),
        in_specs=[pl.BlockSpec((1, rows, columns), lambda at: (at, 0, 0))],
        out_specs=pl.BlockSpec((rows, columns), lambda at: (0, at)),
        compiler_params=pltpu.CompilerParams(vmem_limit_bytes=VMEM_BYTES),
    )(x)


def zeros_map(ndim):
    return lambda step: (0,) * ndim


def part(ref, at, inner):
    return ref[:, at * inner : (at + 1) * inner]


def scalar_block(scalars):
    lane = lax.broadcasted_iota(jnp.int32, (scalars[0].shape[0], LANES), 1)
    packed = jnp.zeros(lane.shape, jnp.float32)
    for at, value in enumerate(scalars):
        high = value.astype(jnp.bfloat16).astype(jnp.float32)
        packed = jnp.where(lane == 2 * at, high, packed)
        packed = jnp.where(lane == 2 * at + 1, value - high, packed)
    return packed.astype(jnp.bfloat16)


def summed_part(ref, start, size):
    total = ref[0, :, start : start + size].astype(jnp.float32)
    for source in range(1, ref.shape[0]):
        total = total + ref[source, :, start : start + size].astype(jnp.float32)
    return total


def down_units(first, last):
    return [(j, t, True) for j in range(first, last) for t in range(j + 1, last)]


def up_units(first, last):
    return [(j, t, False) for j in range(first, last - 1) for t in range(j, last - 1)]


def finder(first, last, inner, down_ref, up_ref, up_start):
    places = {unit: (down_ref, at) for at, unit in enumerate(down_units(first, last))}
    if up_ref is not None:
        for at, unit in enumerate(up_units(first, last)):
            places[unit] = (up_ref, up_start + at)

    def find(unit):
        ref, at = places[unit]
        return part(ref, at, inner)

    return find


def forward_chain(first, last, width, inner, down_ref, up_ref, up_start, find):
    count = last - first
    raw = {s: summed_part(down_ref, (s - first) * inner, inner) for s in range(first, last)}
    cross = {
        s: summed_part(up_ref, up_start + (s - first) * inner, inner)
        for s in range(first, last - 1)
    }
    square = summed_part(down_ref, count * inner, LANES)
    square = square[:, 0:1] + square[:, 1:2]
    state, crosses = {}, {}
    for s in range(first, last):
        scale = lax.rsqrt(jnp.maximum(square, 0.0) / width + norm_eps)
        hidden = raw[s] * scale
        gate = jax.nn.sigmoid(hidden)
        act = (hidden * gate).astype(jnp.bfloat16)
        state[s] = (hidden, scale, act)
        if s == last - 1:
            break
        added = {}
        for k in range(first, last - 1):
            if k >= s:
                added[k] = dot(act, find((s, k, False)), ROWS)
            else:
                added[k] = dot(act, find((k, s, False)), LAST)
        wide = act.astype(jnp.float32)
        square = square + jnp.sum(wide * (2.0 * cross[s] + added[s]), axis=1, keepdims=True)
        cross = {k: cross[k] + added[k] for k in cross}
        for t in range(s + 1, last):
            raw[t] = raw[t] + dot(act, find((s, t, True)), ROWS)
        crosses[s + 1] = cross
    return state, crosses


def backward_chain(first, last, width, inner, grad_ref, hidden_of, scale_of, cross_of, find):
    grad_act = {s: summed_part(grad_ref, (s - first) * inner, inner) for s in range(first, last)}
    packs, pulls = {}, {}
    for s in reversed(range(first, last)):
        hidden, scale = hidden_of(s), scale_of(s)
        gate = jax.nn.sigmoid(hidden)
        grad_hidden = grad_act[s] * gate * (1.0 + hidden * (1.0 - gate))
        mean = jnp.sum(grad_hidden * hidden, axis=1, keepdims=True) / width
        packs[s] = (grad_hidden * scale).astype(jnp.bfloat16)
        pulls[s] = mean * scale * scale
        for t in range(first, s):
            grad_act[t] = (
                grad_act[t]
                + dot(packs[s], find((t, s, True)), LAST)
                - pulls[s] * cross_of(s, t)
            )
    return packs, pulls


def kept_crosses(first, last):
    return [(s, t) for s in range(first + 1, last) for t in range(first, s)]


def forward_kernel(first, last, width, inner, copies):
    def kernel(
        down_ref, up_ref, gram_in_ref, gram_out_ref, acts_ref, hidden_ref, scale_ref, cross_ref
    ):
        find = finder(first, last, inner, gram_in_ref, gram_out_ref, 0)
        state, crosses = forward_chain(first, last, width, inner, down_ref, up_ref, 0, find)
        rows = down_ref.shape[1]
        for s in range(first, last):
            hidden, scale, act = state[s]
            at = s - first
            for copy in range(copies):
                acts_ref[copy * rows : (copy + 1) * rows, at * inner : (at + 1) * inner] = act
            hidden_ref[at] = hidden
            scale_ref[at] = jnp.broadcast_to(scale, (rows, LANES))
        for at, (s, t) in enumerate(kept_crosses(first, last)):
            cross_ref[at] = crosses[s][t]

    return kernel


def store_packs(ref, packs, pulls, first, last, inner, rows, copies):
    scalars = scalar_block([pulls[s] for s in range(first, last)])
    for copy in range(copies):
        there = slice(copy * rows, (copy + 1) * rows)
        for s in range(first, last):
            ref[there, (s - first) * inner : (s - first + 1) * inner] = packs[s]
        at = (last - first) * inner
        ref[there, at : at + LANES] = scalars


def backward_kernel(first, last, width, inner, copies):
    kept = {pair: at for at, pair in enumerate(kept_crosses(first, last))}

    def kernel(grad_ref, hidden_ref, scale_ref, cross_ref, gram_ref, out_ref):
        packs, pulls = backward_chain(
            first,
            last,
            width,
            inner,
            grad_ref,
            lambda s: hidden_ref[s - first],
            lambda s: scale_ref[s - first][:, 0:1],
            lambda s, t: cross_ref[kept[(s, t)]],
            finder(first, last, inner, gram_ref, None, 0),
        )
        store_packs(out_ref, packs, pulls, first, last, inner, grad_ref.shape[1], copies)

    return kernel


def turning_kernel(first, last, width, inner, copies):
    def kernel(sums_ref, grad_ref, gram_ref, out_ref):
        count = last - first
        find = finder(first, last, inner, gram_ref, gram_ref, len(down_units(first, last)))
        state, crosses = forward_chain(
            first, last, width, inner, sums_ref, sums_ref, count * inner + LANES, find
        )
        packs, pulls = backward_chain(
            first,
            last,
            width,
            inner,
            grad_ref,
            lambda s: state[s][0],
            lambda s: state[s][1],
            lambda s, t: crosses[s][t],
            find,
        )
        rows = sums_ref.shape[1]
        store_packs(out_ref, packs, pulls, first, last, inner, rows, copies)
        for copy in range(copies):
            for s in range(first, last):
                at = count * inner + LANES + (s - first) * inner
                out_ref[copy * rows : (copy + 1) * rows, at : at + inner] = state[s][2]

    return kernel


def next_rows_kernel(first, last, then, inner, chunk):
    def kernel(rows_ref, acts_ref, in_ref, out_ref, exact_ref, columns_ref):
        exact = rows_ref[...].astype(jnp.float32)
        for s in range(first, last):
            exact = exact + dot(
                part(acts_ref, s - first, inner), part(out_ref, s, chunk), ROWS
            )
        exact_ref[...] = exact
        rows = exact.astype(jnp.bfloat16)
        at = 0
        for s in range(last, then):
            weight = in_ref[(s - last) * chunk : (s - last + 1) * chunk]
            columns_ref[:, at : at + inner] = dot(rows, weight, ROWS).astype(jnp.bfloat16)
            at += inner
        squares = jnp.sum(exact * exact, axis=1, keepdims=True)
        columns_ref[:, at : at + LANES] = scalar_block([squares])
        at += LANES
        for s in range(last, then - 1):
            columns = dot(rows, part(out_ref, s, chunk), LAST)
            columns_ref[:, at : at + inner] = columns.astype(jnp.bfloat16)
            at += inner

    return kernel


def grads_kernel(first, last, before, inner, chunk, n_dp, acts_start, paired):
    group = last - first
    share_in = group * chunk // n_dp
    share_out = inner // n_dp
    lanes_in = inner // LANES
    lanes_out = chunk // LANES

    def kernel(*refs):
        place_ref, exact_ref, packs_ref, acts_ref, up_ref, in_ref, out_ref = refs[:7]
        refs = refs[7:]
        if first == 0:
            refs[1][last:] = refs[0][...]
            refs = refs[1:]
        grads_ref, up_new_ref, mine_ref = refs[:3]
        more = refs[3:]
        exact = exact_ref[...].astype(jnp.float32)
        rows = {first: exact.astype(jnp.bfloat16)}

        def act_of(s):
            at = acts_start + (s - first) * inner
            return acts_ref[:, at : at + inner]

        for s in range(first, last - 1):
            exact = exact + dot(act_of(s), part(out_ref, s, chunk), ROWS)
            rows[s + 1] = exact.astype(jnp.bfloat16)
        upstream = up_ref[...].astype(jnp.float32)
        narrow = upstream.astype(jnp.bfloat16)
        for s in reversed(range(first, last)):
            pack = part(packs_ref, s - first, inner)
            at = group * inner + 2 * (s - first)
            pull = packs_ref[:, group * inner : group * inner + LANES].astype(jnp.float32)
            at = 2 * (s - first)
            pull = pull[:, at : at + 1] + pull[:, at + 1 : at + 2]
            into = dot(rows[s], pack, FIRST).astype(jnp.bfloat16)
            onto = dot(act_of(s), narrow, FIRST).astype(jnp.bfloat16)
            base = lanes_in * share_in + (s - first) * lanes_out * share_out

            def store(target, into=into, onto=onto, base=base, s=s):
                for piece in range(chunk // share_in):
                    ref, at = target((s - first) * (chunk // share_in) + piece)
                    for c in range(lanes_in):
                        ref[at, c * share_in : (c + 1) * share_in] = into[
                            piece * share_in : (piece + 1) * share_in,
                            c * LANES : (c + 1) * LANES,
                        ]
                for device in range(n_dp):
                    ref, at = target(device)
                    for c in range(lanes_out):
                        row = base + c * share_out
                        ref[at, row : row + share_out] = onto[
                            device * share_out : (device + 1) * share_out,
                            c * LANES : (c + 1) * LANES,
                        ]

            if paired:
                for core in range(2):

                    @pl.when(place_ref[n_dp // 2] == core)
                    def _(store=store, core=core):
                        halves = (mine_ref, more[0]) if core == 0 else (more[0], mine_ref)
                        store(lambda device: (halves[device % 2], place_ref[device // 2]))

            else:
                store(lambda device: (mine_ref, device))

            weight = in_ref[s * chunk : (s + 1) * chunk]
            upstream = (
                upstream + dot(pack, weight, LAST) - pull * rows[s].astype(jnp.float32)
            )
            narrow = upstream.astype(jnp.bfloat16)
            grads_ref[s - first] = narrow
        up_new_ref[...] = upstream
        if before < first:
            for s in range(before, first):
                columns = dot(narrow, part(out_ref, s, chunk), LAST).astype(jnp.bfloat16)
                more[0][:, (s - before) * inner : (s - before + 1) * inner] = columns

    return kernel


def unpack_kernel(inner, share_in, sources):
    def kernel(*refs):
        in_ref, out_ref = refs[sources:]
        given = refs[:sources]
        lanes = inner // LANES

        def total_of(start, stop):
            total = given[0][start:stop].astype(jnp.float32)
            for ref in given[1:]:
                total = total + ref[start:stop].astype(jnp.float32)
            return total.astype(jnp.bfloat16)

        for c in range(lanes):
            in_ref[:, c * LANES : (c + 1) * LANES] = total_of(c * share_in, (c + 1) * share_in)
        out_ref[...] = total_of(lanes * share_in, given[0].shape[0])

    return kernel


def adam_kernel(share, lanes, share_in):
    def kernel(*refs):
        swapped_ref, one_ref, two_ref, onto_ref = refs[:4]
        state_in, state_out = refs[4:7], refs[7:10]
        new_in, new_out, pieces_ref = refs[10:13], refs[13:16], refs[16]
        per = LANES // share
        for c in range(one_ref.shape[1] // LANES):
            there = slice(c * LANES, (c + 1) * LANES)
            one = one_ref[:, there].astype(jnp.float32)
            two = two_ref[:, there].astype(jnp.float32)
            swapped = swapped_ref[0] == 1
            grad = jnp.concatenate(
                [jnp.where(swapped, two, one), jnp.where(swapped, one, two)], axis=0
            )
            results = adam_update(*(ref[:, there] for ref in state_in), grad)
            for ref, value in zip(new_in, results):
                ref[:, there] = value
            turned = results[0].T.astype(jnp.bfloat16)
            for q in range(per):
                pieces_ref[c * per + q, 0] = turned[q * share : (q + 1) * share]
        for device in range(onto_ref.shape[0]):
            for c in range(lanes):
                at = (device * lanes + c) * LANES
                grad = onto_ref[device, c * share : (c + 1) * share].astype(jnp.float32)
                results = adam_update(*(ref[:, at : at + LANES] for ref in state_out), grad)
                for ref, value in zip(new_out, results):
                    ref[:, at : at + LANES] = value
        for device in range(pieces_ref.shape[0]):
            at = device * share_in
            start = at // LANES * LANES
            stop = -(-(at + share_in) // LANES) * LANES
            values = new_out[0][:, start:stop][:, at - start : at - start + share_in]
            pieces_ref[device, 1] = values.astype(jnp.bfloat16)

    return kernel


def rollout_kernel(share, share_in):
    def kernel(pieces_ref, in_ref, out_ref):
        per = LANES // share
        for pair in range(pieces_ref.shape[0] // 2):
            both = [pieces_ref[2 * pair + h, 0].astype(jnp.float32) for h in range(2)]
            at = 2 * pair * share_in
            in_ref[:, at : at + 2 * share_in] = jnp.concatenate(both, axis=1).astype(jnp.bfloat16)
        for c in range(pieces_ref.shape[0] // per):
            rows = [pieces_ref[c * per + q, 1].astype(jnp.float32) for q in range(per)]
            out_ref[:, c * LANES : (c + 1) * LANES] = jnp.concatenate(rows, axis=0).T.astype(
                jnp.bfloat16
            )

    return kernel


def columns_kernel(orders):
    def kernel(every_ref, *out_refs):
        size = every_ref.shape[2]
        for out_ref, order in zip(out_refs, orders):
            for at, unit in enumerate(order):
                out_ref[:, at * size : (at + 1) * size] = every_ref[unit]

    return kernel


def other_core(x, n_dp):
    return lax.ppermute(x, "dp", [(j, j + 1 - 2 * (j % 2)) for j in range(n_dp)])


def add_kernel(mine_ref, other_ref, *out_refs):
    for at in range(mine_ref.shape[0]):
        total = mine_ref[at].astype(jnp.float32) + other_ref[at].astype(jnp.float32)
        if len(out_refs) == 1:
            out_refs[0][at] = total.astype(jnp.bfloat16)
        else:
            out_refs[at][...] = total.astype(jnp.bfloat16)


def added(mine, other, count):
    shape = mine.shape if count == 1 else mine.shape[1:]
    return run(add_kernel, [(shape, jnp.bfloat16)] * count, mine, other)


def chip_steps(n_dp):
    return [(dx, dz) for dx in range(n_dp // 4) for dz in range(2)]


def between_chips(blocks, n_dp):
    arrived = [blocks[0]]
    for (dx, dz), block in list(zip(chip_steps(n_dp), blocks))[1:]:
        pairs = []
        for j in range(n_dp):
            x, z, core = j // 4, j // 2 % 2, j % 2
            pairs.append((j, (x + dx) % (n_dp // 4) * 4 + (z ^ dz) * 2 + core))
        arrived.append(lax.ppermute(block, "dp", pairs))
    return arrived


def move_in(low, high, n_pipe, n_dp):
    odd = lax.axis_index("dp") % 2 == 1
    group = n_pipe // 2
    moved = []
    for q in range(2):
        pairs = []
        for i in range(n_pipe):
            for j in range(n_dp):
                section = j * group // n_dp + (0 if j % 2 == q else group)
                pairs.append((i * n_dp + j, section * n_dp + 2 * i + j // 2 % 2))
        payload = jnp.where(odd, low, high) if q == 1 else jnp.where(odd, high, low)
        moved.append(lax.ppermute(payload, ("pipe", "dp"), pairs))
    return moved


def on_device(
    inputs_x, cotangent, master_in, master_out, moment_in, moment_out, second_in, second_out
):
    n_pipe = lax.axis_size("pipe")
    n_dp = lax.axis_size("dp")
    me = lax.axis_index("pipe")
    tok_rows, width = inputs_x.shape
    chunk = width // n_pipe
    inner = master_in.shape[2]
    share_in = master_in.shape[1]
    share_out = master_out.shape[1]
    block = tok_rows // n_pipe

    own_in = master_in[0].astype(jnp.bfloat16)
    own_out = master_out[0].astype(jnp.bfloat16)
    pairs = [
        (s * n_dp + 2 * i + h, i * n_dp + 2 * s + h)
        for s in range(n_pipe)
        for i in range(n_pipe)
        for h in range(2)
    ]
    piece_in = lax.ppermute(own_in, ("pipe", "dp"), pairs)
    piece_out = swap(own_out.reshape(share_out, n_pipe, chunk).transpose(1, 0, 2), "pipe")
    flat_out = piece_out.transpose(1, 0, 2).reshape(share_out, width)
    all_in = lax.all_gather(piece_in, "dp", axis=0, tiled=True)
    all_out = lax.all_gather(flat_out, "dp", axis=0, tiled=True)
    weight_in = [all_in[s * chunk : (s + 1) * chunk] for s in range(n_pipe)]

    def products(down, blocks):
        units, partial, orders = [], [], []
        for first, last in blocks:
            wanted = (down_units if down else up_units)(first, last)
            for t in sorted({t for _, t, _ in wanted}):
                ks = [k for k, other, _ in wanted if other == t]
                left = piece_out[ks[0] : ks[-1] + 1].reshape(-1, chunk)
                if down:
                    partial.append(dot(left, weight_in[t], ROWS))
                else:
                    partial.append(dot(left, weight_out[t], LAST))
                units += [(k, t, down) for k in ks]
        for first, last in blocks:
            wanted = (down_units if down else up_units)(first, last)
            orders.append([units.index(unit) for unit in wanted])
        partial = [p.astype(jnp.bfloat16) for p in partial]
        arrived = swap(jnp.concatenate(partial, axis=0), "pipe")
        arrived = arrived.reshape(n_pipe, -1, inner)
        mine = jnp.sum(arrived.astype(jnp.float32), axis=0).astype(jnp.bfloat16)
        every = swap(jnp.tile(mine, (n_pipe, 1)), "pipe").reshape(-1, share_out, inner)
        shapes = [((share_out, len(order) * inner), jnp.bfloat16) for order in orders]
        return run(columns_kernel(orders), shapes, every)

    def over_dp(columns):
        return lax.all_gather(columns, "dp", axis=0, tiled=True)

    rows = lax.dynamic_slice_in_dim(inputs_x, me * chunk, chunk, 1)
    seed = lax.dynamic_slice_in_dim(cotangent, me * chunk, chunk, 1)

    (first, middle), (_, last) = BLOCKS
    count = middle - first
    wide = rows.astype(jnp.float32)
    down_low, down_high = products(True, BLOCKS)
    columns = [dot(rows, weight_in[s], ROWS) for s in range(first, middle)]
    columns += split_scalars([jnp.sum(wide * wide, axis=1, keepdims=True)])
    down = exchanged(columns, n_pipe)
    all_out, down_low, down = lax.optimization_barrier((all_out, down_low, down))
    weight_out = [all_out[:, s * chunk : (s + 1) * chunk] for s in range(n_pipe)]
    gram_in_low = over_dp(down_low)
    up_low, up_high = products(False, BLOCKS)
    gram_out_low = over_dp(up_low)
    columns = [dot(rows, weight_out[s], LAST) for s in range(first, middle - 1)]
    columns, up_low = lax.optimization_barrier((columns, up_low))
    up = exchanged(columns, n_pipe)
    columns = [dot(seed, weight_out[s], LAST) for s in range(middle, last)]
    columns, up = lax.optimization_barrier((columns, up))
    grad_high = exchanged(columns, n_pipe)
    columns = jnp.concatenate([down_high, up_high], axis=1)
    gram_in_low, gram_out_low, up, grad_high, columns = lax.optimization_barrier(
        (gram_in_low, gram_out_low, up, grad_high, columns)
    )
    gram_high = over_dp(columns)

    kept = len(kept_crosses(first, middle))
    acts, hidden, scale, cross = run(
        forward_kernel(first, middle, width, inner, n_pipe),
        [
            ((tok_rows, count * inner), jnp.bfloat16),
            ((count, block, inner), jnp.float32),
            ((count, block, LANES), jnp.float32),
            ((kept, block, inner), jnp.float32),
        ],
        down,
        up,
        gram_in_low,
        gram_out_low,
    )
    acts = swap(acts, "pipe")
    exact, columns = run(
        next_rows_kernel(first, middle, last, inner, chunk),
        [
            ((tok_rows, chunk), jnp.float32),
            ((tok_rows, (2 * (last - middle) - 1) * inner + LANES), jnp.bfloat16),
        ],
        rows,
        acts,
        all_in,
        all_out,
        specs={
            2: pl.BlockSpec(
                ((last - middle) * chunk, inner), lambda step: (middle // (last - middle), 0)
            )
        },
    )
    sums = exchanged(columns, n_pipe)

    turned = run(
        turning_kernel(middle, last, width, inner, n_pipe),
        [((tok_rows, 2 * (last - middle) * inner + LANES), jnp.bfloat16)],
        sums,
        grad_high,
        gram_high,
    )[0]
    turned = swap(turned, "pipe")

    def packed_shape(group, parts):
        return (parts, 2 * group * chunk * inner // (n_dp * LANES), LANES)

    dp = lax.axis_index("dp")
    core, chip = dp % 2, dp // 2
    chips = jnp.arange(n_dp // 2)
    xs = n_dp // 4
    away = (chips // 2 - chip // 2 + xs) % xs * 2 + (chips % 2 + chip % 2) % 2
    place = jnp.concatenate([away, core[None]]).astype(jnp.int32)

    grads_high, upstream, packed, columns = run(
        grads_kernel(
            middle, last, first, inner, chunk, n_dp, (last - middle) * inner + LANES, False
        ),
        [
            ((last - middle, tok_rows, chunk), jnp.bfloat16),
            ((tok_rows, chunk), jnp.float32),
            (packed_shape(last - middle, n_dp), jnp.bfloat16),
            ((tok_rows, count * inner), jnp.bfloat16),
        ],
        place,
        exact,
        turned,
        turned,
        seed,
        all_in,
        all_out,
        smem=True,
    )
    packed = packed.reshape(-1, LANES)
    packed = lax.psum_scatter(packed, "dp", scatter_dimension=0, tiled=True)
    grad_low = exchanged(columns, n_pipe)

    packs = run(
        backward_kernel(first, middle, width, inner, n_pipe),
        [((tok_rows, count * inner + LANES), jnp.bfloat16)],
        grad_low,
        hidden,
        scale,
        cross,
        gram_in_low,
    )[0]
    packs = swap(packs, "pipe")
    grads, _, mine, other = run(
        grads_kernel(first, middle, first, inner, chunk, n_dp, 0, True),
        [
            ((n_pipe, tok_rows, chunk), jnp.bfloat16),
            ((tok_rows, chunk), jnp.float32),
            (packed_shape(count, n_dp // 2), jnp.bfloat16),
            (packed_shape(count, n_dp // 2), jnp.bfloat16),
        ],
        place,
        rows,
        packs,
        acts,
        upstream,
        all_in,
        all_out,
        grads_high,
        smem=True,
    )

    def unpacked(arrived, group):
        share = group * chunk // n_dp
        rows_out = arrived[0].shape[-2] - share * inner // LANES
        sum_in, sum_out = run(
            unpack_kernel(inner, share, len(arrived)),
            [((share, inner), jnp.bfloat16), ((rows_out, LANES), jnp.bfloat16)],
            *arrived,
        )
        return sum_in, sum_out.reshape(group, -1, LANES)

    blocks = added(mine, other_core(other, n_dp), mine.shape[0])
    arrived_low = between_chips(blocks, n_dp)
    input_grads = swap(grads, "pipe")
    input_grads, arrived_low = lax.optimization_barrier((input_grads, arrived_low))
    ins, outs = zip(unpacked(arrived_low, count), unpacked([packed], last - middle))
    grad_out = swap(jnp.concatenate(outs, axis=0), "pipe")
    grad_in = move_in(*ins, n_pipe, n_dp)
    is_high = (me >= middle).astype(jnp.int32).reshape(1)

    shape_in, shape_out = (share_in, inner), (share_out, width)
    *updated, pieces = run(
        adam_kernel(share_out, chunk // LANES, share_in),
        [(shape_in, jnp.float32)] * 3
        + [(shape_out, jnp.float32)] * 3
        + [((n_dp, 2, share_out, share_in), jnp.bfloat16)],
        is_high,
        *grad_in,
        grad_out,
        master_in[0],
        moment_in[0],
        second_in[0],
        master_out[0],
        moment_out[0],
        second_out[0],
        smem=True,
    )
    new_in, new_moment_in, new_second_in, new_out, new_moment_out, new_second_out = updated
    input_grads = columns_in_place(input_grads)[None]
    roll_in, roll_out = run(
        rollout_kernel(share_out, share_in),
        [(shape_out, jnp.bfloat16), (shape_in, jnp.bfloat16)],
        swap(pieces, "dp"),
    )
    return (
        input_grads,
        new_in[None],
        new_moment_in[None],
        new_second_in[None],
        new_out[None],
        new_moment_out[None],
        new_second_out[None],
        roll_in[None],
        roll_out[None],
    )


def solution(mesh):
    in_specs = (P("dp", None), P("dp", None)) + (P("pipe", "dp", None),) * 6
    out_specs = (P("pipe", "dp", None),) * 9
    return jax.shard_map(
        on_device, mesh=mesh, in_specs=in_specs, out_specs=out_specs, check_vma=False
    )
```

```python
import jax
import jax.numpy as jnp
from jax import lax
from jax.experimental import pallas as pl
from jax.experimental.pallas import tpu as pltpu
from jax.sharding import PartitionSpec as P

norm_eps = 1e-06
beta_one = 0.9
beta_two = 0.999
learn_rate = 0.02
decay_rate = 0.1
adam_eps = 1e-08
adam_step = 100

BLOCKS = ((0, 4), (4, 8))
LANES = 128
VMEM_BYTES = 48 * 1024 * 1024
VMEM_ALMOST_ALL = 60 * 1024 * 1024


def dot(left, right, dims):
    return lax.dot_general(left, right, (dims, ((), ())), preferred_element_type=jnp.float32)


ROWS = ((1,), (0,))
LAST = ((1,), (1,))
FIRST = ((0,), (0,))


def swap(x, axis):
    return lax.all_to_all(x, axis, 0, 0, tiled=True)


def split_scalars(scalars):
    columns = []
    for value in scalars:
        high = value.astype(jnp.bfloat16)
        columns += [high, (value - high.astype(jnp.float32)).astype(jnp.bfloat16)]
    columns.append(jnp.zeros((scalars[0].shape[0], 128 - len(columns)), jnp.bfloat16))
    return columns


def exchanged(columns, count):
    packed = columns
    if isinstance(columns, list):
        packed = jnp.concatenate([c.astype(jnp.bfloat16) for c in columns], axis=1)
    return swap(packed, "pipe").reshape(count, packed.shape[0] // count, packed.shape[1])


def adam_update(master, moment, second, grad):
    moment_new = beta_one * moment + (1.0 - beta_one) * grad
    second_new = beta_two * second + (1.0 - beta_two) * grad * grad
    moment_hat = moment_new / (1.0 - beta_one**adam_step)
    second_hat = second_new / (1.0 - beta_two**adam_step)
    master_new = master - learn_rate * (
        moment_hat / (jnp.sqrt(second_hat) + adam_eps) + decay_rate * master
    )
    return (master_new, moment_new, second_new)


def run(kernel, shapes, *operands, specs=None, smem=False, vmem=VMEM_BYTES):
    more = {}
    if specs is not None:
        whole = [pl.BlockSpec(x.shape, zeros_map(x.ndim)) for x in operands]
        outs = [pl.BlockSpec(shape, zeros_map(len(shape))) for shape, _ in shapes]
        given = [specs.get(at, spec) for at, spec in enumerate(whole)]
        more = {"grid": (1,), "in_specs": given, "out_specs": outs}
    if smem:
        rest = [pl.BlockSpec(memory_space=pltpu.VMEM)] * (len(operands) - 1)
        more = {"in_specs": [pl.BlockSpec(memory_space=pltpu.SMEM)] + rest}
    return pl.pallas_call(
        kernel,
        out_shape=[jax.ShapeDtypeStruct(shape, kind) for shape, kind in shapes],
        compiler_params=pltpu.CompilerParams(vmem_limit_bytes=vmem),
        **more,
    )(*operands)


def columns_in_place(x):
    count, rows, columns = x.shape

    def kernel(x_ref, out_ref):
        out_ref[...] = x_ref[0]

    return pl.pallas_call(
        kernel,
        out_shape=jax.ShapeDtypeStruct((rows, count * columns), x.dtype),
        grid=(count,),
        in_specs=[pl.BlockSpec((1, rows, columns), lambda at: (at, 0, 0))],
        out_specs=pl.BlockSpec((rows, columns), lambda at: (0, at)),
        compiler_params=pltpu.CompilerParams(vmem_limit_bytes=VMEM_BYTES),
    )(x)


def zeros_map(ndim):
    return lambda step: (0,) * ndim


def part(ref, at, inner):
    return ref[:, at * inner : (at + 1) * inner]


def scalar_block(scalars):
    lane = lax.broadcasted_iota(jnp.int32, (scalars[0].shape[0], LANES), 1)
    packed = jnp.zeros(lane.shape, jnp.float32)
    for at, value in enumerate(scalars):
        high = value.astype(jnp.bfloat16).astype(jnp.float32)
        packed = jnp.where(lane == 2 * at, high, packed)
        packed = jnp.where(lane == 2 * at + 1, value - high, packed)
    return packed.astype(jnp.bfloat16)


def summed_part(ref, start, size):
    total = ref[0, :, start : start + size].astype(jnp.float32)
    for source in range(1, ref.shape[0]):
        total = total + ref[source, :, start : start + size].astype(jnp.float32)
    return total


def down_units(first, last):
    return [(j, t, True) for j in range(first, last) for t in range(j + 1, last)]


def up_units(first, last):
    return [(j, t, False) for j in range(first, last - 1) for t in range(j, last - 1)]


def finder(first, last, inner, down_ref, up_ref, up_start):
    places = {unit: (down_ref, at) for at, unit in enumerate(down_units(first, last))}
    if up_ref is not None:
        for at, unit in enumerate(up_units(first, last)):
            places[unit] = (up_ref, up_start + at)

    def find(unit):
        ref, at = places[unit]
        return part(ref, at, inner)

    return find


def forward_chain(first, last, width, inner, down_ref, up_ref, up_start, find):
    count = last - first
    raw = {s: summed_part(down_ref, (s - first) * inner, inner) for s in range(first, last)}
    cross = {
        s: summed_part(up_ref, up_start + (s - first) * inner, inner)
        for s in range(first, last - 1)
    }
    square = summed_part(down_ref, count * inner, LANES)
    square = square[:, 0:1] + square[:, 1:2]
    state, crosses = {}, {}
    for s in range(first, last):
        scale = lax.rsqrt(jnp.maximum(square, 0.0) / width + norm_eps)
        hidden = raw[s] * scale
        gate = jax.nn.sigmoid(hidden)
        act = (hidden * gate).astype(jnp.bfloat16)
        state[s] = (hidden, scale, act)
        if s == last - 1:
            break
        added = {}
        for k in range(first, last - 1):
            if k >= s:
                added[k] = dot(act, find((s, k, False)), ROWS)
            else:
                added[k] = dot(act, find((k, s, False)), LAST)
        wide = act.astype(jnp.float32)
        square = square + jnp.sum(wide * (2.0 * cross[s] + added[s]), axis=1, keepdims=True)
        cross = {k: cross[k] + added[k] for k in cross}
        for t in range(s + 1, last):
            raw[t] = raw[t] + dot(act, find((s, t, True)), ROWS)
        crosses[s + 1] = cross
    return state, crosses


def backward_chain(first, last, width, inner, grad_ref, hidden_of, scale_of, cross_of, find):
    grad_act = {s: summed_part(grad_ref, (s - first) * inner, inner) for s in range(first, last)}
    packs, pulls = {}, {}
    for s in reversed(range(first, last)):
        hidden, scale = hidden_of(s), scale_of(s)
        gate = jax.nn.sigmoid(hidden)
        grad_hidden = grad_act[s] * gate * (1.0 + hidden * (1.0 - gate))
        mean = jnp.sum(grad_hidden * hidden, axis=1, keepdims=True) / width
        packs[s] = (grad_hidden * scale).astype(jnp.bfloat16)
        pulls[s] = mean * scale * scale
        for t in range(first, s):
            grad_act[t] = (
                grad_act[t]
                + dot(packs[s], find((t, s, True)), LAST)
                - pulls[s] * cross_of(s, t)
            )
    return packs, pulls


def kept_crosses(first, last):
    return [(s, t) for s in range(first + 1, last) for t in range(first, s)]


def forward_kernel(first, last, width, inner, copies):
    def kernel(
        down_ref, up_ref, gram_in_ref, gram_out_ref, acts_ref, hidden_ref, scale_ref, cross_ref
    ):
        find = finder(first, last, inner, gram_in_ref, gram_out_ref, 0)
        state, crosses = forward_chain(first, last, width, inner, down_ref, up_ref, 0, find)
        rows = down_ref.shape[1]
        for s in range(first, last):
            hidden, scale, act = state[s]
            at = s - first
            for copy in range(copies):
                acts_ref[copy * rows : (copy + 1) * rows, at * inner : (at + 1) * inner] = act
            hidden_ref[at] = hidden
            scale_ref[at] = jnp.broadcast_to(scale, (rows, LANES))
        for at, (s, t) in enumerate(kept_crosses(first, last)):
            cross_ref[at] = crosses[s][t]

    return kernel


def store_packs(ref, packs, pulls, first, last, inner, rows, copies):
    scalars = scalar_block([pulls[s] for s in range(first, last)])
    for copy in range(copies):
        there = slice(copy * rows, (copy + 1) * rows)
        for s in range(first, last):
            ref[there, (s - first) * inner : (s - first + 1) * inner] = packs[s]
        at = (last - first) * inner
        ref[there, at : at + LANES] = scalars


def backward_kernel(first, last, width, inner, copies):
    kept = {pair: at for at, pair in enumerate(kept_crosses(first, last))}

    def kernel(grad_ref, hidden_ref, scale_ref, cross_ref, gram_ref, out_ref):
        packs, pulls = backward_chain(
            first,
            last,
            width,
            inner,
            grad_ref,
            lambda s: hidden_ref[s - first],
            lambda s: scale_ref[s - first][:, 0:1],
            lambda s, t: cross_ref[kept[(s, t)]],
            finder(first, last, inner, gram_ref, None, 0),
        )
        store_packs(out_ref, packs, pulls, first, last, inner, grad_ref.shape[1], copies)

    return kernel


def turning_kernel(first, last, width, inner, copies):
    def kernel(sums_ref, grad_ref, gram_ref, out_ref):
        count = last - first
        find = finder(first, last, inner, gram_ref, gram_ref, len(down_units(first, last)))
        state, crosses = forward_chain(
            first, last, width, inner, sums_ref, sums_ref, count * inner + LANES, find
        )
        packs, pulls = backward_chain(
            first,
            last,
            width,
            inner,
            grad_ref,
            lambda s: state[s][0],
            lambda s: state[s][1],
            lambda s, t: crosses[s][t],
            find,
        )
        rows = sums_ref.shape[1]
        store_packs(out_ref, packs, pulls, first, last, inner, rows, copies)
        for copy in range(copies):
            for s in range(first, last):
                at = count * inner + LANES + (s - first) * inner
                out_ref[copy * rows : (copy + 1) * rows, at : at + inner] = state[s][2]

    return kernel


def next_rows_kernel(first, last, then, inner, chunk):
    def kernel(rows_ref, acts_ref, in_ref, out_ref, exact_ref, columns_ref):
        exact = rows_ref[...].astype(jnp.float32)
        for s in range(first, last):
            exact = exact + dot(
                part(acts_ref, s - first, inner), part(out_ref, s, chunk), ROWS
            )
        exact_ref[...] = exact
        rows = exact.astype(jnp.bfloat16)
        at = 0
        for s in range(last, then):
            weight = in_ref[(s - last) * chunk : (s - last + 1) * chunk]
            columns_ref[:, at : at + inner] = dot(rows, weight, ROWS).astype(jnp.bfloat16)
            at += inner
        squares = jnp.sum(exact * exact, axis=1, keepdims=True)
        columns_ref[:, at : at + LANES] = scalar_block([squares])
        at += LANES
        for s in range(last, then - 1):
            columns = dot(rows, part(out_ref, s, chunk), LAST)
            columns_ref[:, at : at + inner] = columns.astype(jnp.bfloat16)
            at += inner

    return kernel


def grads_kernel(first, last, before, inner, chunk, n_dp, acts_start, paired):
    group = last - first
    share_in = group * chunk // n_dp
    share_out = inner // n_dp
    lanes_in = inner // LANES
    lanes_out = chunk // LANES

    def kernel(*refs):
        place_ref, exact_ref, packs_ref, acts_ref, up_ref, in_ref, out_ref = refs[:7]
        refs = refs[7:]
        if first == 0:
            refs[1][last:] = refs[0][...]
            refs = refs[1:]
        grads_ref, up_new_ref, mine_ref = refs[:3]
        more = refs[3:]
        exact = exact_ref[...].astype(jnp.float32)
        rows = {first: exact.astype(jnp.bfloat16)}

        def act_of(s):
            at = acts_start + (s - first) * inner
            return acts_ref[:, at : at + inner]

        for s in range(first, last - 1):
            exact = exact + dot(act_of(s), part(out_ref, s, chunk), ROWS)
            rows[s + 1] = exact.astype(jnp.bfloat16)
        upstream = up_ref[...].astype(jnp.float32)
        narrow = upstream.astype(jnp.bfloat16)
        for s in reversed(range(first, last)):
            pack = part(packs_ref, s - first, inner)
            at = group * inner + 2 * (s - first)
            pull = packs_ref[:, group * inner : group * inner + LANES].astype(jnp.float32)
            at = 2 * (s - first)
            pull = pull[:, at : at + 1] + pull[:, at + 1 : at + 2]
            into = dot(rows[s], pack, FIRST).astype(jnp.bfloat16)
            onto = dot(act_of(s), narrow, FIRST).astype(jnp.bfloat16)
            base = lanes_in * share_in + (s - first) * lanes_out * share_out

            def store(target, into=into, onto=onto, base=base, s=s):
                for piece in range(chunk // share_in):
                    ref, at = target((s - first) * (chunk // share_in) + piece)
                    for c in range(lanes_in):
                        ref[at, c * share_in : (c + 1) * share_in] = into[
                            piece * share_in : (piece + 1) * share_in,
                            c * LANES : (c + 1) * LANES,
                        ]
                for device in range(n_dp):
                    ref, at = target(device)
                    for c in range(lanes_out):
                        row = base + c * share_out
                        ref[at, row : row + share_out] = onto[
                            device * share_out : (device + 1) * share_out,
                            c * LANES : (c + 1) * LANES,
                        ]

            if paired:
                for core in range(2):

                    @pl.when(place_ref[n_dp // 2] == core)
                    def _(store=store, core=core):
                        halves = (mine_ref, more[0]) if core == 0 else (more[0], mine_ref)
                        store(lambda device: (halves[device % 2], place_ref[device // 2]))

            else:
                store(lambda device: (mine_ref, device))

            weight = in_ref[s * chunk : (s + 1) * chunk]
            upstream = (
                upstream + dot(pack, weight, LAST) - pull * rows[s].astype(jnp.float32)
            )
            narrow = upstream.astype(jnp.bfloat16)
            grads_ref[s - first] = narrow
        up_new_ref[...] = upstream
        if before < first:
            for s in range(before, first):
                columns = dot(narrow, part(out_ref, s, chunk), LAST).astype(jnp.bfloat16)
                more[0][:, (s - before) * inner : (s - before + 1) * inner] = columns

    return kernel


def unpack_kernel(inner, share_in, sources):
    def kernel(*refs):
        in_ref, out_ref = refs[sources:]
        given = refs[:sources]
        lanes = inner // LANES

        def total_of(start, stop):
            total = given[0][start:stop].astype(jnp.float32)
            for ref in given[1:]:
                total = total + ref[start:stop].astype(jnp.float32)
            return total.astype(jnp.bfloat16)

        for c in range(lanes):
            in_ref[:, c * LANES : (c + 1) * LANES] = total_of(c * share_in, (c + 1) * share_in)
        out_ref[...] = total_of(lanes * share_in, given[0].shape[0])

    return kernel


def adam_kernel(share, lanes, share_in):
    def kernel(*refs):
        swapped_ref, one_ref, two_ref, onto_ref = refs[:4]
        state_in, state_out = refs[4:7], refs[7:10]
        new_in, new_out, pieces_ref = refs[10:13], refs[13:16], refs[16]
        per = LANES // share
        for c in range(one_ref.shape[1] // LANES):
            there = slice(c * LANES, (c + 1) * LANES)
            one = one_ref[:, there].astype(jnp.float32)
            two = two_ref[:, there].astype(jnp.float32)
            swapped = swapped_ref[0] == 1
            grad = jnp.concatenate(
                [jnp.where(swapped, two, one), jnp.where(swapped, one, two)], axis=0
            )
            results = adam_update(*(ref[:, there] for ref in state_in), grad)
            for ref, value in zip(new_in, results):
                ref[:, there] = value
            turned = results[0].T.astype(jnp.bfloat16)
            for q in range(per):
                pieces_ref[c * per + q, 0] = turned[q * share : (q + 1) * share]
        for device in range(onto_ref.shape[0]):
            for c in range(lanes):
                at = (device * lanes + c) * LANES
                grad = onto_ref[device, c * share : (c + 1) * share].astype(jnp.float32)
                results = adam_update(*(ref[:, at : at + LANES] for ref in state_out), grad)
                for ref, value in zip(new_out, results):
                    ref[:, at : at + LANES] = value
        for device in range(pieces_ref.shape[0]):
            at = device * share_in
            start = at // LANES * LANES
            stop = -(-(at + share_in) // LANES) * LANES
            values = new_out[0][:, start:stop][:, at - start : at - start + share_in]
            pieces_ref[device, 1] = values.astype(jnp.bfloat16)

    return kernel


def rollout_kernel(share, share_in):
    def kernel(pieces_ref, in_ref, out_ref):
        per = LANES // share
        for pair in range(pieces_ref.shape[0] // 2):
            both = [pieces_ref[2 * pair + h, 0].astype(jnp.float32) for h in range(2)]
            at = 2 * pair * share_in
            in_ref[:, at : at + 2 * share_in] = jnp.concatenate(both, axis=1).astype(jnp.bfloat16)
        for c in range(pieces_ref.shape[0] // per):
            rows = [pieces_ref[c * per + q, 1].astype(jnp.float32) for q in range(per)]
            out_ref[:, c * LANES : (c + 1) * LANES] = jnp.concatenate(rows, axis=0).T.astype(
                jnp.bfloat16
            )

    return kernel


def columns_kernel(orders):
    def kernel(every_ref, *out_refs):
        size = every_ref.shape[2]
        for out_ref, order in zip(out_refs, orders):
            for at, unit in enumerate(order):
                out_ref[:, at * size : (at + 1) * size] = every_ref[unit]

    return kernel


def other_core(x, n_dp):
    return lax.ppermute(x, "dp", [(j, j + 1 - 2 * (j % 2)) for j in range(n_dp)])


def add_kernel(mine_ref, other_ref, *out_refs):
    for at in range(mine_ref.shape[0]):
        total = mine_ref[at].astype(jnp.float32) + other_ref[at].astype(jnp.float32)
        if len(out_refs) == 1:
            out_refs[0][at] = total.astype(jnp.bfloat16)
        else:
            out_refs[at][...] = total.astype(jnp.bfloat16)


def added(mine, other, count):
    shape = mine.shape if count == 1 else mine.shape[1:]
    shapes = [(shape, jnp.bfloat16)] * count
    return run(add_kernel, shapes, mine, other, vmem=VMEM_ALMOST_ALL)


def chip_steps(n_dp):
    return [(dx, dz) for dx in range(n_dp // 4) for dz in range(2)]


def between_chips(blocks, n_dp):
    arrived = [blocks[0]]
    for (dx, dz), block in list(zip(chip_steps(n_dp), blocks))[1:]:
        pairs = []
        for j in range(n_dp):
            x, z, core = j // 4, j // 2 % 2, j % 2
            pairs.append((j, (x + dx) % (n_dp // 4) * 4 + (z ^ dz) * 2 + core))
        arrived.append(lax.ppermute(block, "dp", pairs))
    return arrived


def move_in(low, high, n_pipe, n_dp):
    odd = lax.axis_index("dp") % 2 == 1
    group = n_pipe // 2
    moved = []
    for q in range(2):
        pairs = []
        for i in range(n_pipe):
            for j in range(n_dp):
                section = j * group // n_dp + (0 if j % 2 == q else group)
                pairs.append((i * n_dp + j, section * n_dp + 2 * i + j // 2 % 2))
        payload = jnp.where(odd, low, high) if q == 1 else jnp.where(odd, high, low)
        moved.append(lax.ppermute(payload, ("pipe", "dp"), pairs))
    return moved


def on_device(
    inputs_x, cotangent, master_in, master_out, moment_in, moment_out, second_in, second_out
):
    n_pipe = lax.axis_size("pipe")
    n_dp = lax.axis_size("dp")
    me = lax.axis_index("pipe")
    tok_rows, width = inputs_x.shape
    chunk = width // n_pipe
    inner = master_in.shape[2]
    share_in = master_in.shape[1]
    share_out = master_out.shape[1]
    block = tok_rows // n_pipe

    own_in = master_in[0].astype(jnp.bfloat16)
    own_out = master_out[0].astype(jnp.bfloat16)
    pairs = [
        (s * n_dp + 2 * i + h, i * n_dp + 2 * s + h)
        for s in range(n_pipe)
        for i in range(n_pipe)
        for h in range(2)
    ]
    piece_in = lax.ppermute(own_in, ("pipe", "dp"), pairs)
    piece_out = swap(own_out.reshape(share_out, n_pipe, chunk).transpose(1, 0, 2), "pipe")
    flat_out = piece_out.transpose(1, 0, 2).reshape(share_out, width)
    all_in = lax.all_gather(piece_in, "dp", axis=0, tiled=True)
    all_out = lax.all_gather(flat_out, "dp", axis=0, tiled=True)
    weight_in = [all_in[s * chunk : (s + 1) * chunk] for s in range(n_pipe)]

    def products(down, blocks):
        units, partial, orders = [], [], []
        for first, last in blocks:
            wanted = (down_units if down else up_units)(first, last)
            for t in sorted({t for _, t, _ in wanted}):
                ks = [k for k, other, _ in wanted if other == t]
                left = piece_out[ks[0] : ks[-1] + 1].reshape(-1, chunk)
                if down:
                    partial.append(dot(left, weight_in[t], ROWS))
                else:
                    partial.append(dot(left, weight_out[t], LAST))
                units += [(k, t, down) for k in ks]
        for first, last in blocks:
            wanted = (down_units if down else up_units)(first, last)
            orders.append([units.index(unit) for unit in wanted])
        partial = [p.astype(jnp.bfloat16) for p in partial]
        arrived = swap(jnp.concatenate(partial, axis=0), "pipe")
        arrived = arrived.reshape(n_pipe, -1, inner)
        mine = jnp.sum(arrived.astype(jnp.float32), axis=0).astype(jnp.bfloat16)
        every = swap(jnp.tile(mine, (n_pipe, 1)), "pipe").reshape(-1, share_out, inner)
        shapes = [((share_out, len(order) * inner), jnp.bfloat16) for order in orders]
        return run(columns_kernel(orders), shapes, every)

    def over_dp(columns):
        return lax.all_gather(columns, "dp", axis=0, tiled=True)

    rows = lax.dynamic_slice_in_dim(inputs_x, me * chunk, chunk, 1)
    seed = lax.dynamic_slice_in_dim(cotangent, me * chunk, chunk, 1)

    (first, middle), (_, last) = BLOCKS
    count = middle - first
    wide = rows.astype(jnp.float32)
    down_low, down_high = products(True, BLOCKS)
    columns = [dot(rows, weight_in[s], ROWS) for s in range(first, middle)]
    columns += split_scalars([jnp.sum(wide * wide, axis=1, keepdims=True)])
    down = exchanged(columns, n_pipe)
    all_out, down_low, down = lax.optimization_barrier((all_out, down_low, down))
    weight_out = [all_out[:, s * chunk : (s + 1) * chunk] for s in range(n_pipe)]
    gram_in_low = over_dp(down_low)
    up_low, up_high = products(False, BLOCKS)
    gram_out_low = over_dp(up_low)
    columns = [dot(rows, weight_out[s], LAST) for s in range(first, middle - 1)]
    columns, up_low = lax.optimization_barrier((columns, up_low))
    up = exchanged(columns, n_pipe)
    columns = [dot(seed, weight_out[s], LAST) for s in range(middle, last)]
    columns, up = lax.optimization_barrier((columns, up))
    grad_high = exchanged(columns, n_pipe)
    columns = jnp.concatenate([down_high, up_high], axis=1)
    gram_in_low, gram_out_low, up, grad_high, columns = lax.optimization_barrier(
        (gram_in_low, gram_out_low, up, grad_high, columns)
    )
    gram_high = over_dp(columns)

    kept = len(kept_crosses(first, middle))
    acts, hidden, scale, cross = run(
        forward_kernel(first, middle, width, inner, n_pipe),
        [
            ((tok_rows, count * inner), jnp.bfloat16),
            ((count, block, inner), jnp.float32),
            ((count, block, LANES), jnp.float32),
            ((kept, block, inner), jnp.float32),
        ],
        down,
        up,
        gram_in_low,
        gram_out_low,
    )
    acts = swap(acts, "pipe")
    exact, columns = run(
        next_rows_kernel(first, middle, last, inner, chunk),
        [
            ((tok_rows, chunk), jnp.float32),
            ((tok_rows, (2 * (last - middle) - 1) * inner + LANES), jnp.bfloat16),
        ],
        rows,
        acts,
        all_in,
        all_out,
        specs={
            2: pl.BlockSpec(
                ((last - middle) * chunk, inner), lambda step: (middle // (last - middle), 0)
            )
        },
    )
    sums = exchanged(columns, n_pipe)

    turned = run(
        turning_kernel(middle, last, width, inner, n_pipe),
        [((tok_rows, 2 * (last - middle) * inner + LANES), jnp.bfloat16)],
        sums,
        grad_high,
        gram_high,
    )[0]
    turned = swap(turned, "pipe")

    def packed_shape(group, parts):
        return (parts, 2 * group * chunk * inner // (n_dp * LANES), LANES)

    dp = lax.axis_index("dp")
    core, chip = dp % 2, dp // 2
    chips = jnp.arange(n_dp // 2)
    xs = n_dp // 4
    away = (chips // 2 - chip // 2 + xs) % xs * 2 + (chips % 2 + chip % 2) % 2
    place = jnp.concatenate([away, core[None]]).astype(jnp.int32)

    grads_high, upstream, packed, columns = run(
        grads_kernel(
            middle, last, first, inner, chunk, n_dp, (last - middle) * inner + LANES, False
        ),
        [
            ((last - middle, tok_rows, chunk), jnp.bfloat16),
            ((tok_rows, chunk), jnp.float32),
            (packed_shape(last - middle, n_dp), jnp.bfloat16),
            ((tok_rows, count * inner), jnp.bfloat16),
        ],
        place,
        exact,
        turned,
        turned,
        seed,
        all_in,
        all_out,
        smem=True,
    )
    packed = packed.reshape(-1, LANES)
    packed = lax.psum_scatter(packed, "dp", scatter_dimension=0, tiled=True)
    grad_low = exchanged(columns, n_pipe)

    packs = run(
        backward_kernel(first, middle, width, inner, n_pipe),
        [((tok_rows, count * inner + LANES), jnp.bfloat16)],
        grad_low,
        hidden,
        scale,
        cross,
        gram_in_low,
    )[0]
    packs = swap(packs, "pipe")
    grads, _, mine, other = run(
        grads_kernel(first, middle, first, inner, chunk, n_dp, 0, True),
        [
            ((n_pipe, tok_rows, chunk), jnp.bfloat16),
            ((tok_rows, chunk), jnp.float32),
            (packed_shape(count, n_dp // 2), jnp.bfloat16),
            (packed_shape(count, n_dp // 2), jnp.bfloat16),
        ],
        place,
        rows,
        packs,
        acts,
        upstream,
        all_in,
        all_out,
        grads_high,
        smem=True,
    )

    def unpacked(arrived, group):
        share = group * chunk // n_dp
        rows_out = arrived[0].shape[-2] - share * inner // LANES
        sum_in, sum_out = run(
            unpack_kernel(inner, share, len(arrived)),
            [((share, inner), jnp.bfloat16), ((rows_out, LANES), jnp.bfloat16)],
            *arrived,
            vmem=VMEM_ALMOST_ALL,
        )
        return sum_in, sum_out.reshape(group, -1, LANES)

    blocks = added(mine, other_core(other, n_dp), mine.shape[0])
    arrived_low = between_chips(blocks, n_dp)
    input_grads = swap(grads, "pipe")
    input_grads, arrived_low = lax.optimization_barrier((input_grads, arrived_low))
    ins, outs = zip(unpacked(arrived_low, count), unpacked([packed], last - middle))
    grad_out = swap(jnp.concatenate(outs, axis=0), "pipe")
    grad_in = move_in(*ins, n_pipe, n_dp)
    is_high = (me >= middle).astype(jnp.int32).reshape(1)

    shape_in, shape_out = (share_in, inner), (share_out, width)
    *updated, pieces = run(
        adam_kernel(share_out, chunk // LANES, share_in),
        [(shape_in, jnp.float32)] * 3
        + [(shape_out, jnp.float32)] * 3
        + [((n_dp, 2, share_out, share_in), jnp.bfloat16)],
        is_high,
        *grad_in,
        grad_out,
        master_in[0],
        moment_in[0],
        second_in[0],
        master_out[0],
        moment_out[0],
        second_out[0],
        smem=True,
        vmem=VMEM_ALMOST_ALL,
    )
    new_in, new_moment_in, new_second_in, new_out, new_moment_out, new_second_out = updated
    input_grads = columns_in_place(input_grads)[None]
    roll_in, roll_out = run(
        rollout_kernel(share_out, share_in),
        [(shape_out, jnp.bfloat16), (shape_in, jnp.bfloat16)],
        swap(pieces, "dp"),
    )
    return (
        input_grads,
        new_in[None],
        new_moment_in[None],
        new_second_in[None],
        new_out[None],
        new_moment_out[None],
        new_second_out[None],
        roll_in[None],
        roll_out[None],
    )


def solution(mesh):
    in_specs = (P("dp", None), P("dp", None)) + (P("pipe", "dp", None),) * 6
    out_specs = (P("pipe", "dp", None),) * 9
    return jax.shard_map(
        on_device, mesh=mesh, in_specs=in_specs, out_specs=out_specs, check_vma=False
    )
```

```python
import jax
import jax.numpy as jnp
from jax import lax
from jax.experimental import pallas as pl
from jax.experimental.pallas import tpu as pltpu
from jax.sharding import PartitionSpec as P

norm_eps = 1e-06
beta_one = 0.9
beta_two = 0.999
learn_rate = 0.02
decay_rate = 0.1
adam_eps = 1e-08
adam_step = 100

BLOCKS = ((0, 4), (4, 8))
LANES = 128
VMEM_BYTES = 48 * 1024 * 1024
VMEM_ALMOST_ALL = 60 * 1024 * 1024


def dot(left, right, dims):
    return lax.dot_general(left, right, (dims, ((), ())), preferred_element_type=jnp.float32)


ROWS = ((1,), (0,))
LAST = ((1,), (1,))
FIRST = ((0,), (0,))


def swap(x, axis):
    return lax.all_to_all(x, axis, 0, 0, tiled=True)


def split_scalars(scalars):
    columns = []
    for value in scalars:
        high = value.astype(jnp.bfloat16)
        columns += [high, (value - high.astype(jnp.float32)).astype(jnp.bfloat16)]
    columns.append(jnp.zeros((scalars[0].shape[0], 128 - len(columns)), jnp.bfloat16))
    return columns


def exchanged(columns, count):
    packed = columns
    if isinstance(columns, list):
        packed = jnp.concatenate([c.astype(jnp.bfloat16) for c in columns], axis=1)
    return swap(packed, "pipe").reshape(count, packed.shape[0] // count, packed.shape[1])


def adam_update(master, moment, second, grad):
    moment_new = beta_one * moment + (1.0 - beta_one) * grad
    second_new = beta_two * second + (1.0 - beta_two) * grad * grad
    moment_hat = moment_new / (1.0 - beta_one**adam_step)
    second_hat = second_new / (1.0 - beta_two**adam_step)
    master_new = master - learn_rate * (
        moment_hat / (jnp.sqrt(second_hat) + adam_eps) + decay_rate * master
    )
    return (master_new, moment_new, second_new)


def run(kernel, shapes, *operands, specs=None, smem=False, vmem=VMEM_BYTES):
    more = {}
    if specs is not None:
        whole = [pl.BlockSpec(x.shape, zeros_map(x.ndim)) for x in operands]
        outs = [pl.BlockSpec(shape, zeros_map(len(shape))) for shape, _ in shapes]
        given = [specs.get(at, spec) for at, spec in enumerate(whole)]
        more = {"grid": (1,), "in_specs": given, "out_specs": outs}
    if smem:
        rest = [pl.BlockSpec(memory_space=pltpu.VMEM)] * (len(operands) - 1)
        more = {"in_specs": [pl.BlockSpec(memory_space=pltpu.SMEM)] + rest}
    return pl.pallas_call(
        kernel,
        out_shape=[jax.ShapeDtypeStruct(shape, kind) for shape, kind in shapes],
        compiler_params=pltpu.CompilerParams(vmem_limit_bytes=vmem),
        **more,
    )(*operands)


def columns_in_place(x):
    count, rows, columns = x.shape

    def kernel(x_ref, out_ref):
        out_ref[...] = x_ref[0]

    return pl.pallas_call(
        kernel,
        out_shape=jax.ShapeDtypeStruct((rows, count * columns), x.dtype),
        grid=(count,),
        in_specs=[pl.BlockSpec((1, rows, columns), lambda at: (at, 0, 0))],
        out_specs=pl.BlockSpec((rows, columns), lambda at: (0, at)),
        compiler_params=pltpu.CompilerParams(vmem_limit_bytes=VMEM_BYTES),
    )(x)


def zeros_map(ndim):
    return lambda step: (0,) * ndim


def part(ref, at, inner):
    return ref[:, at * inner : (at + 1) * inner]


def scalar_block(scalars):
    lane = lax.broadcasted_iota(jnp.int32, (scalars[0].shape[0], LANES), 1)
    packed = jnp.zeros(lane.shape, jnp.float32)
    for at, value in enumerate(scalars):
        high = value.astype(jnp.bfloat16).astype(jnp.float32)
        packed = jnp.where(lane == 2 * at, high, packed)
        packed = jnp.where(lane == 2 * at + 1, value - high, packed)
    return packed.astype(jnp.bfloat16)


def summed_part(ref, start, size):
    total = ref[0, :, start : start + size].astype(jnp.float32)
    for source in range(1, ref.shape[0]):
        total = total + ref[source, :, start : start + size].astype(jnp.float32)
    return total


def down_units(first, last):
    return [(j, t, True) for j in range(first, last) for t in range(j + 1, last)]


def up_units(first, last):
    return [(j, t, False) for j in range(first, last - 1) for t in range(j, last - 1)]


def finder(first, last, inner, down_ref, up_ref, up_start):
    places = {unit: (down_ref, at) for at, unit in enumerate(down_units(first, last))}
    if up_ref is not None:
        for at, unit in enumerate(up_units(first, last)):
            places[unit] = (up_ref, up_start + at)

    def find(unit):
        ref, at = places[unit]
        return part(ref, at, inner)

    return find


def forward_chain(first, last, width, inner, down_ref, up_ref, up_start, find):
    count = last - first
    raw = {s: summed_part(down_ref, (s - first) * inner, inner) for s in range(first, last)}
    cross = {
        s: summed_part(up_ref, up_start + (s - first) * inner, inner)
        for s in range(first, last - 1)
    }
    square = summed_part(down_ref, count * inner, LANES)
    square = square[:, 0:1] + square[:, 1:2]
    state, crosses = {}, {}
    for s in range(first, last):
        scale = lax.rsqrt(jnp.maximum(square, 0.0) / width + norm_eps)
        hidden = raw[s] * scale
        gate = jax.nn.sigmoid(hidden)
        act = (hidden * gate).astype(jnp.bfloat16)
        state[s] = (hidden, scale, act)
        if s == last - 1:
            break
        added = {}
        for k in range(first, last - 1):
            if k >= s:
                added[k] = dot(act, find((s, k, False)), ROWS)
            else:
                added[k] = dot(act, find((k, s, False)), LAST)
        wide = act.astype(jnp.float32)
        square = square + jnp.sum(wide * (2.0 * cross[s] + added[s]), axis=1, keepdims=True)
        cross = {k: cross[k] + added[k] for k in cross}
        for t in range(s + 1, last):
            raw[t] = raw[t] + dot(act, find((s, t, True)), ROWS)
        crosses[s + 1] = cross
    return state, crosses


def backward_chain(first, last, width, inner, grad_ref, hidden_of, scale_of, cross_of, find):
    grad_act = {s: summed_part(grad_ref, (s - first) * inner, inner) for s in range(first, last)}
    packs, pulls = {}, {}
    for s in reversed(range(first, last)):
        hidden, scale = hidden_of(s), scale_of(s)
        gate = jax.nn.sigmoid(hidden)
        grad_hidden = grad_act[s] * gate * (1.0 + hidden * (1.0 - gate))
        mean = jnp.sum(grad_hidden * hidden, axis=1, keepdims=True) / width
        packs[s] = (grad_hidden * scale).astype(jnp.bfloat16)
        pulls[s] = mean * scale * scale
        for t in range(first, s):
            grad_act[t] = (
                grad_act[t]
                + dot(packs[s], find((t, s, True)), LAST)
                - pulls[s] * cross_of(s, t)
            )
    return packs, pulls


def kept_crosses(first, last):
    return [(s, t) for s in range(first + 1, last) for t in range(first, s)]


def forward_kernel(first, last, width, inner, copies):
    def kernel(
        down_ref, up_ref, gram_in_ref, gram_out_ref, acts_ref, hidden_ref, scale_ref, cross_ref
    ):
        find = finder(first, last, inner, gram_in_ref, gram_out_ref, 0)
        state, crosses = forward_chain(first, last, width, inner, down_ref, up_ref, 0, find)
        rows = down_ref.shape[1]
        for s in range(first, last):
            hidden, scale, act = state[s]
            at = s - first
            for copy in range(copies):
                acts_ref[copy * rows : (copy + 1) * rows, at * inner : (at + 1) * inner] = act
            hidden_ref[at] = hidden
            scale_ref[at] = jnp.broadcast_to(scale, (rows, LANES))
        for at, (s, t) in enumerate(kept_crosses(first, last)):
            cross_ref[at] = crosses[s][t]

    return kernel


def store_packs(ref, packs, pulls, first, last, inner, rows, copies):
    scalars = scalar_block([pulls[s] for s in range(first, last)])
    for copy in range(copies):
        there = slice(copy * rows, (copy + 1) * rows)
        for s in range(first, last):
            ref[there, (s - first) * inner : (s - first + 1) * inner] = packs[s]
        at = (last - first) * inner
        ref[there, at : at + LANES] = scalars


def backward_kernel(first, last, width, inner, copies):
    kept = {pair: at for at, pair in enumerate(kept_crosses(first, last))}

    def kernel(grad_ref, hidden_ref, scale_ref, cross_ref, gram_ref, out_ref):
        packs, pulls = backward_chain(
            first,
            last,
            width,
            inner,
            grad_ref,
            lambda s: hidden_ref[s - first],
            lambda s: scale_ref[s - first][:, 0:1],
            lambda s, t: cross_ref[kept[(s, t)]],
            finder(first, last, inner, gram_ref, None, 0),
        )
        store_packs(out_ref, packs, pulls, first, last, inner, grad_ref.shape[1], copies)

    return kernel


def turning_kernel(first, last, width, inner, copies):
    def kernel(sums_ref, grad_ref, gram_ref, out_ref):
        count = last - first
        find = finder(first, last, inner, gram_ref, gram_ref, len(down_units(first, last)))
        state, crosses = forward_chain(
            first, last, width, inner, sums_ref, sums_ref, count * inner + LANES, find
        )
        packs, pulls = backward_chain(
            first,
            last,
            width,
            inner,
            grad_ref,
            lambda s: state[s][0],
            lambda s: state[s][1],
            lambda s, t: crosses[s][t],
            find,
        )
        rows = sums_ref.shape[1]
        store_packs(out_ref, packs, pulls, first, last, inner, rows, copies)
        for copy in range(copies):
            for s in range(first, last):
                at = count * inner + LANES + (s - first) * inner
                out_ref[copy * rows : (copy + 1) * rows, at : at + inner] = state[s][2]

    return kernel


def next_rows_kernel(first, last, then, inner, chunk):
    def kernel(rows_ref, acts_ref, in_ref, out_ref, exact_ref, columns_ref):
        exact = rows_ref[...].astype(jnp.float32)
        for s in range(first, last):
            exact = exact + dot(
                part(acts_ref, s - first, inner), part(out_ref, s, chunk), ROWS
            )
        exact_ref[...] = exact
        rows = exact.astype(jnp.bfloat16)
        at = 0
        for s in range(last, then):
            weight = in_ref[(s - last) * chunk : (s - last + 1) * chunk]
            columns_ref[:, at : at + inner] = dot(rows, weight, ROWS).astype(jnp.bfloat16)
            at += inner
        squares = jnp.sum(exact * exact, axis=1, keepdims=True)
        columns_ref[:, at : at + LANES] = scalar_block([squares])
        at += LANES
        for s in range(last, then - 1):
            columns = dot(rows, part(out_ref, s, chunk), LAST)
            columns_ref[:, at : at + inner] = columns.astype(jnp.bfloat16)
            at += inner

    return kernel


def grads_kernel(first, last, before, inner, chunk, n_dp, acts_start, paired):
    group = last - first
    share_in = group * chunk // n_dp
    share_out = inner // n_dp
    lanes_in = inner // LANES
    lanes_out = chunk // LANES

    def kernel(*refs):
        place_ref, exact_ref, packs_ref, acts_ref, up_ref, in_ref, out_ref = refs[:7]
        refs = refs[7:]
        if first == 0:
            refs[1][last:] = refs[0][...]
            refs = refs[1:]
        grads_ref, up_new_ref, mine_ref = refs[:3]
        more = refs[3:]
        exact = exact_ref[...].astype(jnp.float32)
        rows = {first: exact.astype(jnp.bfloat16)}

        def act_of(s):
            at = acts_start + (s - first) * inner
            return acts_ref[:, at : at + inner]

        for s in range(first, last - 1):
            exact = exact + dot(act_of(s), part(out_ref, s, chunk), ROWS)
            rows[s + 1] = exact.astype(jnp.bfloat16)
        upstream = up_ref[...].astype(jnp.float32)
        narrow = upstream.astype(jnp.bfloat16)
        for s in reversed(range(first, last)):
            pack = part(packs_ref, s - first, inner)
            at = group * inner + 2 * (s - first)
            pull = packs_ref[:, group * inner : group * inner + LANES].astype(jnp.float32)
            at = 2 * (s - first)
            pull = pull[:, at : at + 1] + pull[:, at + 1 : at + 2]
            into = dot(rows[s], pack, FIRST).astype(jnp.bfloat16)
            onto = dot(act_of(s), narrow, FIRST).astype(jnp.bfloat16)
            base = lanes_in * share_in + (s - first) * lanes_out * share_out

            def store(target, into=into, onto=onto, base=base, s=s):
                for piece in range(chunk // share_in):
                    ref, at = target((s - first) * (chunk // share_in) + piece)
                    for c in range(lanes_in):
                        ref[at, c * share_in : (c + 1) * share_in] = into[
                            piece * share_in : (piece + 1) * share_in,
                            c * LANES : (c + 1) * LANES,
                        ]
                for device in range(n_dp):
                    ref, at = target(device)
                    for c in range(lanes_out):
                        row = base + c * share_out
                        ref[at, row : row + share_out] = onto[
                            device * share_out : (device + 1) * share_out,
                            c * LANES : (c + 1) * LANES,
                        ]

            if paired:
                for core in range(2):

                    @pl.when(place_ref[n_dp // 2] == core)
                    def _(store=store, core=core):
                        halves = (mine_ref, more[0]) if core == 0 else (more[0], mine_ref)
                        store(lambda device: (halves[device % 2], place_ref[device // 2]))

            else:
                store(lambda device: (mine_ref, device))

            weight = in_ref[s * chunk : (s + 1) * chunk]
            upstream = (
                upstream + dot(pack, weight, LAST) - pull * rows[s].astype(jnp.float32)
            )
            narrow = upstream.astype(jnp.bfloat16)
            grads_ref[s - first] = narrow
        up_new_ref[...] = upstream
        if before < first:
            for s in range(before, first):
                columns = dot(narrow, part(out_ref, s, chunk), LAST).astype(jnp.bfloat16)
                more[0][:, (s - before) * inner : (s - before + 1) * inner] = columns

    return kernel


def unpack_kernel(inner, share_in, sources):
    def kernel(*refs):
        in_ref, out_ref = refs[sources:]
        given = refs[:sources]
        lanes = inner // LANES

        def total_of(start, stop):
            total = given[0][start:stop].astype(jnp.float32)
            for ref in given[1:]:
                total = total + ref[start:stop].astype(jnp.float32)
            return total.astype(jnp.bfloat16)

        for c in range(lanes):
            in_ref[:, c * LANES : (c + 1) * LANES] = total_of(c * share_in, (c + 1) * share_in)
        out_ref[...] = total_of(lanes * share_in, given[0].shape[0])

    return kernel


def adam_kernel(share, lanes, share_in):
    def kernel(*refs):
        swapped_ref, one_ref, two_ref, onto_ref = refs[:4]
        state_in, state_out = refs[4:7], refs[7:10]
        new_in, new_out, pieces_ref = refs[10:13], refs[13:16], refs[16]
        per = LANES // share
        for c in range(one_ref.shape[1] // LANES):
            there = slice(c * LANES, (c + 1) * LANES)
            one = one_ref[:, there].astype(jnp.float32)
            two = two_ref[:, there].astype(jnp.float32)
            swapped = swapped_ref[0] == 1
            grad = jnp.concatenate(
                [jnp.where(swapped, two, one), jnp.where(swapped, one, two)], axis=0
            )
            results = adam_update(*(ref[:, there] for ref in state_in), grad)
            for ref, value in zip(new_in, results):
                ref[:, there] = value
            turned = results[0].T.astype(jnp.bfloat16)
            for q in range(per):
                pieces_ref[c * per + q, 0] = turned[q * share : (q + 1) * share]
        for device in range(onto_ref.shape[0]):
            for c in range(lanes):
                at = (device * lanes + c) * LANES
                grad = onto_ref[device, c * share : (c + 1) * share].astype(jnp.float32)
                results = adam_update(*(ref[:, at : at + LANES] for ref in state_out), grad)
                for ref, value in zip(new_out, results):
                    ref[:, at : at + LANES] = value
        for device in range(pieces_ref.shape[0]):
            at = device * share_in
            start = at // LANES * LANES
            stop = -(-(at + share_in) // LANES) * LANES
            values = new_out[0][:, start:stop][:, at - start : at - start + share_in]
            pieces_ref[device, 1] = values.astype(jnp.bfloat16)

    return kernel


def rollout_kernel(share, share_in):
    def kernel(pieces_ref, in_ref, out_ref):
        per = LANES // share
        for pair in range(pieces_ref.shape[0] // 2):
            both = [pieces_ref[2 * pair + h, 0].astype(jnp.float32) for h in range(2)]
            at = 2 * pair * share_in
            in_ref[:, at : at + 2 * share_in] = jnp.concatenate(both, axis=1).astype(jnp.bfloat16)
        for c in range(pieces_ref.shape[0] // per):
            rows = [pieces_ref[c * per + q, 1].astype(jnp.float32) for q in range(per)]
            out_ref[:, c * LANES : (c + 1) * LANES] = jnp.concatenate(rows, axis=0).T.astype(
                jnp.bfloat16
            )

    return kernel


def columns_kernel(orders):
    def kernel(every_ref, *out_refs):
        size = every_ref.shape[2]
        for out_ref, order in zip(out_refs, orders):
            for at, unit in enumerate(order):
                out_ref[:, at * size : (at + 1) * size] = every_ref[unit]

    return kernel


def other_core(x, n_dp):
    return lax.ppermute(x, "dp", [(j, j + 1 - 2 * (j % 2)) for j in range(n_dp)])


def add_kernel(mine_ref, other_ref, *out_refs):
    per = mine_ref.shape[0] // len(out_refs)
    for at in range(mine_ref.shape[0]):
        total = mine_ref[at].astype(jnp.float32) + other_ref[at].astype(jnp.float32)
        if per == 1:
            out_refs[at][...] = total.astype(jnp.bfloat16)
        else:
            out_refs[at // per][at % per] = total.astype(jnp.bfloat16)


def added(mine, other, count):
    per = mine.shape[0] // count
    shape = mine.shape[1:] if per == 1 else (per, *mine.shape[1:])
    shapes = [(shape, jnp.bfloat16)] * count
    return run(add_kernel, shapes, mine, other, vmem=VMEM_ALMOST_ALL)


def between_chips(mine, other, n_dp):
    xs = n_dp // 4
    same, across = added(mine, other, 2)
    across = lax.ppermute(across, "dp", [(j, j + 2 - 4 * (j // 2 % 2)) for j in range(n_dp)])
    blocks = added(same, across, xs)
    arrived = [blocks[0]]
    for dx in range(1, xs):
        pairs = [(j, (j + 4 * dx) % n_dp) for j in range(n_dp)]
        arrived.append(lax.ppermute(blocks[dx], "dp", pairs))
    return arrived


def move_in(low, high, n_pipe, n_dp):
    odd = lax.axis_index("dp") % 2 == 1
    group = n_pipe // 2
    moved = []
    for q in range(2):
        pairs = []
        for i in range(n_pipe):
            for j in range(n_dp):
                section = j * group // n_dp + (0 if j % 2 == q else group)
                pairs.append((i * n_dp + j, section * n_dp + 2 * i + j // 2 % 2))
        payload = jnp.where(odd, low, high) if q == 1 else jnp.where(odd, high, low)
        moved.append(lax.ppermute(payload, ("pipe", "dp"), pairs))
    return moved


def on_device(
    inputs_x, cotangent, master_in, master_out, moment_in, moment_out, second_in, second_out
):
    n_pipe = lax.axis_size("pipe")
    n_dp = lax.axis_size("dp")
    me = lax.axis_index("pipe")
    tok_rows, width = inputs_x.shape
    chunk = width // n_pipe
    inner = master_in.shape[2]
    share_in = master_in.shape[1]
    share_out = master_out.shape[1]
    block = tok_rows // n_pipe

    own_in = master_in[0].astype(jnp.bfloat16)
    own_out = master_out[0].astype(jnp.bfloat16)
    pairs = [
        (s * n_dp + 2 * i + h, i * n_dp + 2 * s + h)
        for s in range(n_pipe)
        for i in range(n_pipe)
        for h in range(2)
    ]
    piece_in = lax.ppermute(own_in, ("pipe", "dp"), pairs)
    piece_out = swap(own_out.reshape(share_out, n_pipe, chunk).transpose(1, 0, 2), "pipe")
    flat_out = piece_out.transpose(1, 0, 2).reshape(share_out, width)
    all_in = lax.all_gather(piece_in, "dp", axis=0, tiled=True)
    all_out = lax.all_gather(flat_out, "dp", axis=0, tiled=True)
    weight_in = [all_in[s * chunk : (s + 1) * chunk] for s in range(n_pipe)]

    def products(down, blocks):
        units, partial, orders = [], [], []
        for first, last in blocks:
            wanted = (down_units if down else up_units)(first, last)
            for t in sorted({t for _, t, _ in wanted}):
                ks = [k for k, other, _ in wanted if other == t]
                left = piece_out[ks[0] : ks[-1] + 1].reshape(-1, chunk)
                if down:
                    partial.append(dot(left, weight_in[t], ROWS))
                else:
                    partial.append(dot(left, weight_out[t], LAST))
                units += [(k, t, down) for k in ks]
        for first, last in blocks:
            wanted = (down_units if down else up_units)(first, last)
            orders.append([units.index(unit) for unit in wanted])
        partial = [p.astype(jnp.bfloat16) for p in partial]
        arrived = swap(jnp.concatenate(partial, axis=0), "pipe")
        arrived = arrived.reshape(n_pipe, -1, inner)
        mine = jnp.sum(arrived.astype(jnp.float32), axis=0).astype(jnp.bfloat16)
        every = swap(jnp.tile(mine, (n_pipe, 1)), "pipe").reshape(-1, share_out, inner)
        shapes = [((share_out, len(order) * inner), jnp.bfloat16) for order in orders]
        return run(columns_kernel(orders), shapes, every)

    def over_dp(columns):
        return lax.all_gather(columns, "dp", axis=0, tiled=True)

    rows = lax.dynamic_slice_in_dim(inputs_x, me * chunk, chunk, 1)
    seed = lax.dynamic_slice_in_dim(cotangent, me * chunk, chunk, 1)

    (first, middle), (_, last) = BLOCKS
    count = middle - first
    wide = rows.astype(jnp.float32)
    down_low, down_high = products(True, BLOCKS)
    columns = [dot(rows, weight_in[s], ROWS) for s in range(first, middle)]
    columns += split_scalars([jnp.sum(wide * wide, axis=1, keepdims=True)])
    down = exchanged(columns, n_pipe)
    all_out, down_low, down = lax.optimization_barrier((all_out, down_low, down))
    weight_out = [all_out[:, s * chunk : (s + 1) * chunk] for s in range(n_pipe)]
    gram_in_low = over_dp(down_low)
    up_low, up_high = products(False, BLOCKS)
    gram_out_low = over_dp(up_low)
    columns = [dot(rows, weight_out[s], LAST) for s in range(first, middle - 1)]
    columns, up_low = lax.optimization_barrier((columns, up_low))
    up = exchanged(columns, n_pipe)
    columns = [dot(seed, weight_out[s], LAST) for s in range(middle, last)]
    columns, up = lax.optimization_barrier((columns, up))
    grad_high = exchanged(columns, n_pipe)
    columns = jnp.concatenate([down_high, up_high], axis=1)
    gram_in_low, gram_out_low, up, grad_high, columns = lax.optimization_barrier(
        (gram_in_low, gram_out_low, up, grad_high, columns)
    )
    gram_high = over_dp(columns)

    kept = len(kept_crosses(first, middle))
    acts, hidden, scale, cross = run(
        forward_kernel(first, middle, width, inner, n_pipe),
        [
            ((tok_rows, count * inner), jnp.bfloat16),
            ((count, block, inner), jnp.float32),
            ((count, block, LANES), jnp.float32),
            ((kept, block, inner), jnp.float32),
        ],
        down,
        up,
        gram_in_low,
        gram_out_low,
    )
    acts = swap(acts, "pipe")
    exact, columns = run(
        next_rows_kernel(first, middle, last, inner, chunk),
        [
            ((tok_rows, chunk), jnp.float32),
            ((tok_rows, (2 * (last - middle) - 1) * inner + LANES), jnp.bfloat16),
        ],
        rows,
        acts,
        all_in,
        all_out,
        specs={
            2: pl.BlockSpec(
                ((last - middle) * chunk, inner), lambda step: (middle // (last - middle), 0)
            )
        },
    )
    sums = exchanged(columns, n_pipe)

    turned = run(
        turning_kernel(middle, last, width, inner, n_pipe),
        [((tok_rows, 2 * (last - middle) * inner + LANES), jnp.bfloat16)],
        sums,
        grad_high,
        gram_high,
    )[0]
    turned = swap(turned, "pipe")

    def packed_shape(group, parts):
        return (parts, 2 * group * chunk * inner // (n_dp * LANES), LANES)

    dp = lax.axis_index("dp")
    core, chip = dp % 2, dp // 2
    chips = jnp.arange(n_dp // 2)
    xs = n_dp // 4
    away = (chips % 2 + chip % 2) % 2 * xs + (chips // 2 - chip // 2 + xs) % xs
    place = jnp.concatenate([away, core[None]]).astype(jnp.int32)

    grads_high, upstream, packed, columns = run(
        grads_kernel(
            middle, last, first, inner, chunk, n_dp, (last - middle) * inner + LANES, False
        ),
        [
            ((last - middle, tok_rows, chunk), jnp.bfloat16),
            ((tok_rows, chunk), jnp.float32),
            (packed_shape(last - middle, n_dp), jnp.bfloat16),
            ((tok_rows, count * inner), jnp.bfloat16),
        ],
        place,
        exact,
        turned,
        turned,
        seed,
        all_in,
        all_out,
        smem=True,
    )
    packed = packed.reshape(-1, LANES)
    packed = lax.psum_scatter(packed, "dp", scatter_dimension=0, tiled=True)
    grad_low = exchanged(columns, n_pipe)

    packs = run(
        backward_kernel(first, middle, width, inner, n_pipe),
        [((tok_rows, count * inner + LANES), jnp.bfloat16)],
        grad_low,
        hidden,
        scale,
        cross,
        gram_in_low,
    )[0]
    packs = swap(packs, "pipe")
    grads, _, mine, other = run(
        grads_kernel(first, middle, first, inner, chunk, n_dp, 0, True),
        [
            ((n_pipe, tok_rows, chunk), jnp.bfloat16),
            ((tok_rows, chunk), jnp.float32),
            (packed_shape(count, n_dp // 2), jnp.bfloat16),
            (packed_shape(count, n_dp // 2), jnp.bfloat16),
        ],
        place,
        rows,
        packs,
        acts,
        upstream,
        all_in,
        all_out,
        grads_high,
        smem=True,
    )

    def unpacked(arrived, group):
        share = group * chunk // n_dp
        rows_out = arrived[0].shape[-2] - share * inner // LANES
        sum_in, sum_out = run(
            unpack_kernel(inner, share, len(arrived)),
            [((share, inner), jnp.bfloat16), ((rows_out, LANES), jnp.bfloat16)],
            *arrived,
            vmem=VMEM_ALMOST_ALL,
        )
        return sum_in, sum_out.reshape(group, -1, LANES)

    arrived_low = between_chips(mine, other_core(other, n_dp), n_dp)
    input_grads = swap(grads, "pipe")
    input_grads, arrived_low = lax.optimization_barrier((input_grads, arrived_low))
    ins, outs = zip(unpacked(arrived_low, count), unpacked([packed], last - middle))
    grad_out = swap(jnp.concatenate(outs, axis=0), "pipe")
    grad_in = move_in(*ins, n_pipe, n_dp)
    is_high = (me >= middle).astype(jnp.int32).reshape(1)

    shape_in, shape_out = (share_in, inner), (share_out, width)
    *updated, pieces = run(
        adam_kernel(share_out, chunk // LANES, share_in),
        [(shape_in, jnp.float32)] * 3
        + [(shape_out, jnp.float32)] * 3
        + [((n_dp, 2, share_out, share_in), jnp.bfloat16)],
        is_high,
        *grad_in,
        grad_out,
        master_in[0],
        moment_in[0],
        second_in[0],
        master_out[0],
        moment_out[0],
        second_out[0],
        smem=True,
        vmem=VMEM_ALMOST_ALL,
    )
    new_in, new_moment_in, new_second_in, new_out, new_moment_out, new_second_out = updated
    input_grads = columns_in_place(input_grads)[None]
    roll_in, roll_out = run(
        rollout_kernel(share_out, share_in),
        [(shape_out, jnp.bfloat16), (shape_in, jnp.bfloat16)],
        swap(pieces, "dp"),
    )
    return (
        input_grads,
        new_in[None],
        new_moment_in[None],
        new_second_in[None],
        new_out[None],
        new_moment_out[None],
        new_second_out[None],
        roll_in[None],
        roll_out[None],
    )


def solution(mesh):
    in_specs = (P("dp", None), P("dp", None)) + (P("pipe", "dp", None),) * 6
    out_specs = (P("pipe", "dp", None),) * 9
    return jax.shard_map(
        on_device, mesh=mesh, in_specs=in_specs, out_specs=out_specs, check_vma=False
    )
```

```python
import jax
import jax.numpy as jnp
from jax import lax
from jax.experimental import pallas as pl
from jax.experimental.pallas import tpu as pltpu
from jax.sharding import PartitionSpec as P

norm_eps = 1e-06
beta_one = 0.9
beta_two = 0.999
learn_rate = 0.02
decay_rate = 0.1
adam_eps = 1e-08
adam_step = 100

BLOCKS = ((0, 4), (4, 8))
LANES = 128
VMEM_BYTES = 48 * 1024 * 1024
VMEM_ALMOST_ALL = 60 * 1024 * 1024


def dot(left, right, dims):
    return lax.dot_general(left, right, (dims, ((), ())), preferred_element_type=jnp.float32)


ROWS = ((1,), (0,))
LAST = ((1,), (1,))
FIRST = ((0,), (0,))


def swap(x, axis):
    return lax.all_to_all(x, axis, 0, 0, tiled=True)


def split_scalars(scalars):
    columns = []
    for value in scalars:
        high = value.astype(jnp.bfloat16)
        columns += [high, (value - high.astype(jnp.float32)).astype(jnp.bfloat16)]
    columns.append(jnp.zeros((scalars[0].shape[0], 128 - len(columns)), jnp.bfloat16))
    return columns


def exchanged(columns, count):
    packed = columns
    if isinstance(columns, list):
        packed = jnp.concatenate([c.astype(jnp.bfloat16) for c in columns], axis=1)
    return swap(packed, "pipe").reshape(count, packed.shape[0] // count, packed.shape[1])


def adam_update(master, moment, second, grad):
    moment_new = beta_one * moment + (1.0 - beta_one) * grad
    second_new = beta_two * second + (1.0 - beta_two) * grad * grad
    moment_hat = moment_new / (1.0 - beta_one**adam_step)
    second_hat = second_new / (1.0 - beta_two**adam_step)
    master_new = master - learn_rate * (
        moment_hat / (jnp.sqrt(second_hat) + adam_eps) + decay_rate * master
    )
    return (master_new, moment_new, second_new)


def run(kernel, shapes, *operands, specs=None, smem=False, vmem=VMEM_BYTES):
    more = {}
    if specs is not None:
        whole = [pl.BlockSpec(x.shape, zeros_map(x.ndim)) for x in operands]
        outs = [pl.BlockSpec(shape, zeros_map(len(shape))) for shape, _ in shapes]
        given = [specs.get(at, spec) for at, spec in enumerate(whole)]
        more = {"grid": (1,), "in_specs": given, "out_specs": outs}
    if smem:
        rest = [pl.BlockSpec(memory_space=pltpu.VMEM)] * (len(operands) - 1)
        more = {"in_specs": [pl.BlockSpec(memory_space=pltpu.SMEM)] + rest}
    return pl.pallas_call(
        kernel,
        out_shape=[jax.ShapeDtypeStruct(shape, kind) for shape, kind in shapes],
        compiler_params=pltpu.CompilerParams(vmem_limit_bytes=vmem),
        **more,
    )(*operands)


def columns_in_place(x):
    count, rows, columns = x.shape

    def kernel(x_ref, out_ref):
        out_ref[...] = x_ref[0]

    return pl.pallas_call(
        kernel,
        out_shape=jax.ShapeDtypeStruct((rows, count * columns), x.dtype),
        grid=(count,),
        in_specs=[pl.BlockSpec((1, rows, columns), lambda at: (at, 0, 0))],
        out_specs=pl.BlockSpec((rows, columns), lambda at: (0, at)),
        compiler_params=pltpu.CompilerParams(vmem_limit_bytes=VMEM_BYTES),
    )(x)


def zeros_map(ndim):
    return lambda step: (0,) * ndim


def part(ref, at, inner):
    return ref[:, at * inner : (at + 1) * inner]


def scalar_block(scalars):
    lane = lax.broadcasted_iota(jnp.int32, (scalars[0].shape[0], LANES), 1)
    packed = jnp.zeros(lane.shape, jnp.float32)
    for at, value in enumerate(scalars):
        high = value.astype(jnp.bfloat16).astype(jnp.float32)
        packed = jnp.where(lane == 2 * at, high, packed)
        packed = jnp.where(lane == 2 * at + 1, value - high, packed)
    return packed.astype(jnp.bfloat16)


def summed_part(ref, start, size):
    total = ref[0, :, start : start + size].astype(jnp.float32)
    for source in range(1, ref.shape[0]):
        total = total + ref[source, :, start : start + size].astype(jnp.float32)
    return total


def down_units(first, last):
    return [(j, t, True) for j in range(first, last) for t in range(j + 1, last)]


def up_units(first, last):
    return [(j, t, False) for j in range(first, last - 1) for t in range(j, last - 1)]


def finder(first, last, inner, down_ref, up_ref, up_start):
    places = {unit: (down_ref, at) for at, unit in enumerate(down_units(first, last))}
    if up_ref is not None:
        for at, unit in enumerate(up_units(first, last)):
            places[unit] = (up_ref, up_start + at)

    def find(unit):
        ref, at = places[unit]
        return part(ref, at, inner)

    return find


def forward_chain(first, last, width, inner, down_ref, up_ref, up_start, find):
    count = last - first
    raw = {s: summed_part(down_ref, (s - first) * inner, inner) for s in range(first, last)}
    cross = {
        s: summed_part(up_ref, up_start + (s - first) * inner, inner)
        for s in range(first, last - 1)
    }
    square = summed_part(down_ref, count * inner, LANES)
    square = square[:, 0:1] + square[:, 1:2]
    state, crosses = {}, {}
    for s in range(first, last):
        scale = lax.rsqrt(jnp.maximum(square, 0.0) / width + norm_eps)
        hidden = raw[s] * scale
        gate = jax.nn.sigmoid(hidden)
        act = (hidden * gate).astype(jnp.bfloat16)
        state[s] = (hidden, scale, act)
        if s == last - 1:
            break
        added = {}
        for k in range(first, last - 1):
            if k >= s:
                added[k] = dot(act, find((s, k, False)), ROWS)
            else:
                added[k] = dot(act, find((k, s, False)), LAST)
        wide = act.astype(jnp.float32)
        square = square + jnp.sum(wide * (2.0 * cross[s] + added[s]), axis=1, keepdims=True)
        cross = {k: cross[k] + added[k] for k in cross}
        for t in range(s + 1, last):
            raw[t] = raw[t] + dot(act, find((s, t, True)), ROWS)
        crosses[s + 1] = cross
    return state, crosses


def backward_chain(first, last, width, inner, grad_ref, hidden_of, scale_of, cross_of, find):
    grad_act = {s: summed_part(grad_ref, (s - first) * inner, inner) for s in range(first, last)}
    packs, pulls = {}, {}
    for s in reversed(range(first, last)):
        hidden, scale = hidden_of(s), scale_of(s)
        gate = jax.nn.sigmoid(hidden)
        grad_hidden = grad_act[s] * gate * (1.0 + hidden * (1.0 - gate))
        mean = jnp.sum(grad_hidden * hidden, axis=1, keepdims=True) / width
        packs[s] = (grad_hidden * scale).astype(jnp.bfloat16)
        pulls[s] = mean * scale * scale
        for t in range(first, s):
            grad_act[t] = (
                grad_act[t]
                + dot(packs[s], find((t, s, True)), LAST)
                - pulls[s] * cross_of(s, t)
            )
    return packs, pulls


def kept_crosses(first, last):
    return [(s, t) for s in range(first + 1, last) for t in range(first, s)]


def forward_kernel(first, last, width, inner, copies):
    def kernel(
        down_ref, up_ref, gram_in_ref, gram_out_ref, acts_ref, hidden_ref, scale_ref, cross_ref
    ):
        find = finder(first, last, inner, gram_in_ref, gram_out_ref, 0)
        state, crosses = forward_chain(first, last, width, inner, down_ref, up_ref, 0, find)
        rows = down_ref.shape[1]
        for s in range(first, last):
            hidden, scale, act = state[s]
            at = s - first
            for copy in range(copies):
                acts_ref[copy * rows : (copy + 1) * rows, at * inner : (at + 1) * inner] = act
            hidden_ref[at] = hidden
            scale_ref[at] = jnp.broadcast_to(scale, (rows, LANES))
        for at, (s, t) in enumerate(kept_crosses(first, last)):
            cross_ref[at] = crosses[s][t]

    return kernel


def store_packs(ref, packs, pulls, first, last, inner, rows, copies):
    scalars = scalar_block([pulls[s] for s in range(first, last)])
    for copy in range(copies):
        there = slice(copy * rows, (copy + 1) * rows)
        for s in range(first, last):
            ref[there, (s - first) * inner : (s - first + 1) * inner] = packs[s]
        at = (last - first) * inner
        ref[there, at : at + LANES] = scalars


def backward_kernel(first, last, width, inner, copies):
    kept = {pair: at for at, pair in enumerate(kept_crosses(first, last))}

    def kernel(grad_ref, hidden_ref, scale_ref, cross_ref, gram_ref, out_ref):
        packs, pulls = backward_chain(
            first,
            last,
            width,
            inner,
            grad_ref,
            lambda s: hidden_ref[s - first],
            lambda s: scale_ref[s - first][:, 0:1],
            lambda s, t: cross_ref[kept[(s, t)]],
            finder(first, last, inner, gram_ref, None, 0),
        )
        store_packs(out_ref, packs, pulls, first, last, inner, grad_ref.shape[1], copies)

    return kernel


def turning_kernel(first, last, width, inner, copies):
    def kernel(sums_ref, grad_ref, gram_ref, out_ref):
        count = last - first
        find = finder(first, last, inner, gram_ref, gram_ref, len(down_units(first, last)))
        state, crosses = forward_chain(
            first, last, width, inner, sums_ref, sums_ref, count * inner + LANES, find
        )
        packs, pulls = backward_chain(
            first,
            last,
            width,
            inner,
            grad_ref,
            lambda s: state[s][0],
            lambda s: state[s][1],
            lambda s, t: crosses[s][t],
            find,
        )
        rows = sums_ref.shape[1]
        store_packs(out_ref, packs, pulls, first, last, inner, rows, copies)
        for copy in range(copies):
            for s in range(first, last):
                at = count * inner + LANES + (s - first) * inner
                out_ref[copy * rows : (copy + 1) * rows, at : at + inner] = state[s][2]

    return kernel


def next_rows_kernel(first, last, then, inner, chunk):
    def kernel(rows_ref, acts_ref, in_ref, out_ref, exact_ref, columns_ref):
        exact = rows_ref[...].astype(jnp.float32)
        for s in range(first, last):
            exact = exact + dot(
                part(acts_ref, s - first, inner), part(out_ref, s, chunk), ROWS
            )
        exact_ref[...] = exact
        rows = exact.astype(jnp.bfloat16)
        at = 0
        for s in range(last, then):
            weight = in_ref[(s - last) * chunk : (s - last + 1) * chunk]
            columns_ref[:, at : at + inner] = dot(rows, weight, ROWS).astype(jnp.bfloat16)
            at += inner
        squares = jnp.sum(exact * exact, axis=1, keepdims=True)
        columns_ref[:, at : at + LANES] = scalar_block([squares])
        at += LANES
        for s in range(last, then - 1):
            columns = dot(rows, part(out_ref, s, chunk), LAST)
            columns_ref[:, at : at + inner] = columns.astype(jnp.bfloat16)
            at += inner

    return kernel


def grads_kernel(first, last, before, inner, chunk, n_dp, acts_start, paired):
    group = last - first
    share_in = group * chunk // n_dp
    share_out = inner // n_dp
    lanes_in = inner // LANES
    lanes_out = chunk // LANES

    def kernel(*refs):
        place_ref, exact_ref, packs_ref, acts_ref, up_ref, in_ref, out_ref = refs[:7]
        refs = refs[7:]
        if first == 0:
            refs[1][last:] = refs[0][...]
            refs = refs[1:]
        grads_ref, up_new_ref, mine_ref = refs[:3]
        more = refs[3:]
        exact = exact_ref[...].astype(jnp.float32)
        rows = {first: exact.astype(jnp.bfloat16)}

        def act_of(s):
            at = acts_start + (s - first) * inner
            return acts_ref[:, at : at + inner]

        for s in range(first, last - 1):
            exact = exact + dot(act_of(s), part(out_ref, s, chunk), ROWS)
            rows[s + 1] = exact.astype(jnp.bfloat16)
        upstream = up_ref[...].astype(jnp.float32)
        narrow = upstream.astype(jnp.bfloat16)
        for s in reversed(range(first, last)):
            pack = part(packs_ref, s - first, inner)
            at = group * inner + 2 * (s - first)
            pull = packs_ref[:, group * inner : group * inner + LANES].astype(jnp.float32)
            at = 2 * (s - first)
            pull = pull[:, at : at + 1] + pull[:, at + 1 : at + 2]
            into = dot(rows[s], pack, FIRST).astype(jnp.bfloat16)
            onto = dot(act_of(s), narrow, FIRST).astype(jnp.bfloat16)
            base = lanes_in * share_in + (s - first) * lanes_out * share_out

            def store(target, into=into, onto=onto, base=base, s=s):
                for piece in range(chunk // share_in):
                    ref, at = target((s - first) * (chunk // share_in) + piece)
                    for c in range(lanes_in):
                        ref[at, c * share_in : (c + 1) * share_in] = into[
                            piece * share_in : (piece + 1) * share_in,
                            c * LANES : (c + 1) * LANES,
                        ]
                for device in range(n_dp):
                    ref, at = target(device)
                    for c in range(lanes_out):
                        row = base + c * share_out
                        ref[at, row : row + share_out] = onto[
                            device * share_out : (device + 1) * share_out,
                            c * LANES : (c + 1) * LANES,
                        ]

            if paired:
                for core in range(2):

                    @pl.when(place_ref[n_dp // 2] == core)
                    def _(store=store, core=core):
                        halves = (mine_ref, more[0]) if core == 0 else (more[0], mine_ref)
                        store(lambda device: (halves[device % 2], place_ref[device // 2]))

            else:
                store(lambda device: (mine_ref, device))

            weight = in_ref[s * chunk : (s + 1) * chunk]
            upstream = (
                upstream + dot(pack, weight, LAST) - pull * rows[s].astype(jnp.float32)
            )
            narrow = upstream.astype(jnp.bfloat16)
            grads_ref[s - first] = narrow
        up_new_ref[...] = upstream
        if before < first:
            for s in range(before, first):
                columns = dot(narrow, part(out_ref, s, chunk), LAST).astype(jnp.bfloat16)
                more[0][:, (s - before) * inner : (s - before + 1) * inner] = columns

    return kernel


def unpack_kernel(inner, share_in, sources):
    def kernel(*refs):
        in_ref, out_ref = refs[sources:]
        given = refs[:sources]
        lanes = inner // LANES

        def total_of(start, stop):
            total = given[0][start:stop].astype(jnp.float32)
            for ref in given[1:]:
                total = total + ref[start:stop].astype(jnp.float32)
            return total.astype(jnp.bfloat16)

        for c in range(lanes):
            in_ref[:, c * LANES : (c + 1) * LANES] = total_of(c * share_in, (c + 1) * share_in)
        out_ref[...] = total_of(lanes * share_in, given[0].shape[0])

    return kernel


def adam_kernel(share, lanes, share_in):
    def kernel(*refs):
        swapped_ref, one_ref, two_ref, onto_ref = refs[:4]
        state_in, state_out = refs[4:7], refs[7:10]
        new_in, new_out, pieces_ref = refs[10:13], refs[13:16], refs[16]
        per = LANES // share
        for c in range(one_ref.shape[1] // LANES):
            there = slice(c * LANES, (c + 1) * LANES)
            one = one_ref[:, there].astype(jnp.float32)
            two = two_ref[:, there].astype(jnp.float32)
            swapped = swapped_ref[0] == 1
            grad = jnp.concatenate(
                [jnp.where(swapped, two, one), jnp.where(swapped, one, two)], axis=0
            )
            results = adam_update(*(ref[:, there] for ref in state_in), grad)
            for ref, value in zip(new_in, results):
                ref[:, there] = value
            turned = results[0].T.astype(jnp.bfloat16)
            for q in range(per):
                pieces_ref[c * per + q, 0] = turned[q * share : (q + 1) * share]
        for device in range(onto_ref.shape[0]):
            for c in range(lanes):
                at = (device * lanes + c) * LANES
                grad = onto_ref[device, c * share : (c + 1) * share].astype(jnp.float32)
                results = adam_update(*(ref[:, at : at + LANES] for ref in state_out), grad)
                for ref, value in zip(new_out, results):
                    ref[:, at : at + LANES] = value
        for device in range(pieces_ref.shape[0]):
            at = device * share_in
            start = at // LANES * LANES
            stop = -(-(at + share_in) // LANES) * LANES
            values = new_out[0][:, start:stop][:, at - start : at - start + share_in]
            pieces_ref[device, 1] = values.astype(jnp.bfloat16)

    return kernel


def rollout_kernel(share, share_in):
    def kernel(pieces_ref, in_ref, out_ref):
        per = LANES // share
        for pair in range(pieces_ref.shape[0] // 2):
            both = [pieces_ref[2 * pair + h, 0].astype(jnp.float32) for h in range(2)]
            at = 2 * pair * share_in
            in_ref[:, at : at + 2 * share_in] = jnp.concatenate(both, axis=1).astype(jnp.bfloat16)
        for c in range(pieces_ref.shape[0] // per):
            rows = [pieces_ref[c * per + q, 1].astype(jnp.float32) for q in range(per)]
            out_ref[:, c * LANES : (c + 1) * LANES] = jnp.concatenate(rows, axis=0).T.astype(
                jnp.bfloat16
            )

    return kernel


def columns_kernel(orders):
    def kernel(every_ref, *out_refs):
        size = every_ref.shape[2]
        for out_ref, order in zip(out_refs, orders):
            for at, unit in enumerate(order):
                out_ref[:, at * size : (at + 1) * size] = every_ref[unit]

    return kernel


def other_core(x, n_dp):
    return lax.ppermute(x, "dp", [(j, j + 1 - 2 * (j % 2)) for j in range(n_dp)])


def add_kernel(mine_ref, other_ref, *out_refs):
    for at in range(mine_ref.shape[0]):
        total = mine_ref[at].astype(jnp.float32) + other_ref[at].astype(jnp.float32)
        if len(out_refs) == 1:
            out_refs[0][at] = total.astype(jnp.bfloat16)
        else:
            out_refs[at][...] = total.astype(jnp.bfloat16)


def added(mine, other, count):
    shape = mine.shape if count == 1 else mine.shape[1:]
    shapes = [(shape, jnp.bfloat16)] * count
    return run(add_kernel, shapes, mine, other, vmem=VMEM_ALMOST_ALL)


def chip_steps(n_dp):
    return [(dx, dz) for dx in range(n_dp // 4) for dz in range(2)]


def between_chips(blocks, n_dp):
    arrived = [blocks[0]]
    steps = list(zip(chip_steps(n_dp), blocks))[1:]
    for (dx, dz), block in sorted(steps, key=lambda step: (-step[0][1], step[0][0] % 2)):
        pairs = []
        for j in range(n_dp):
            x, z, core = j // 4, j // 2 % 2, j % 2
            pairs.append((j, (x + dx) % (n_dp // 4) * 4 + (z ^ dz) * 2 + core))
        arrived.append(lax.ppermute(block, "dp", pairs))
    return arrived


def move_in(low, high, n_pipe, n_dp):
    odd = lax.axis_index("dp") % 2 == 1
    group = n_pipe // 2
    moved = []
    for q in range(2):
        pairs = []
        for i in range(n_pipe):
            for j in range(n_dp):
                section = j * group // n_dp + (0 if j % 2 == q else group)
                pairs.append((i * n_dp + j, section * n_dp + 2 * i + j // 2 % 2))
        payload = jnp.where(odd, low, high) if q == 1 else jnp.where(odd, high, low)
        moved.append(lax.ppermute(payload, ("pipe", "dp"), pairs))
    return moved


def on_device(
    inputs_x, cotangent, master_in, master_out, moment_in, moment_out, second_in, second_out
):
    n_pipe = lax.axis_size("pipe")
    n_dp = lax.axis_size("dp")
    me = lax.axis_index("pipe")
    tok_rows, width = inputs_x.shape
    chunk = width // n_pipe
    inner = master_in.shape[2]
    share_in = master_in.shape[1]
    share_out = master_out.shape[1]
    block = tok_rows // n_pipe

    own_in = master_in[0].astype(jnp.bfloat16)
    own_out = master_out[0].astype(jnp.bfloat16)
    pairs = [
        (s * n_dp + 2 * i + h, i * n_dp + 2 * s + h)
        for s in range(n_pipe)
        for i in range(n_pipe)
        for h in range(2)
    ]
    piece_in = lax.ppermute(own_in, ("pipe", "dp"), pairs)
    piece_out = swap(own_out.reshape(share_out, n_pipe, chunk).transpose(1, 0, 2), "pipe")
    flat_out = piece_out.transpose(1, 0, 2).reshape(share_out, width)
    all_in = lax.all_gather(piece_in, "dp", axis=0, tiled=True)
    all_out = lax.all_gather(flat_out, "dp", axis=0, tiled=True)
    weight_in = [all_in[s * chunk : (s + 1) * chunk] for s in range(n_pipe)]

    def products(down, blocks):
        units, partial, orders = [], [], []
        for first, last in blocks:
            wanted = (down_units if down else up_units)(first, last)
            for t in sorted({t for _, t, _ in wanted}):
                ks = [k for k, other, _ in wanted if other == t]
                left = piece_out[ks[0] : ks[-1] + 1].reshape(-1, chunk)
                if down:
                    partial.append(dot(left, weight_in[t], ROWS))
                else:
                    partial.append(dot(left, weight_out[t], LAST))
                units += [(k, t, down) for k in ks]
        for first, last in blocks:
            wanted = (down_units if down else up_units)(first, last)
            orders.append([units.index(unit) for unit in wanted])
        partial = [p.astype(jnp.bfloat16) for p in partial]
        arrived = swap(jnp.concatenate(partial, axis=0), "pipe")
        arrived = arrived.reshape(n_pipe, -1, inner)
        mine = jnp.sum(arrived.astype(jnp.float32), axis=0).astype(jnp.bfloat16)
        every = swap(jnp.tile(mine, (n_pipe, 1)), "pipe").reshape(-1, share_out, inner)
        shapes = [((share_out, len(order) * inner), jnp.bfloat16) for order in orders]
        return run(columns_kernel(orders), shapes, every)

    def over_dp(columns):
        return lax.all_gather(columns, "dp", axis=0, tiled=True)

    rows = lax.dynamic_slice_in_dim(inputs_x, me * chunk, chunk, 1)
    seed = lax.dynamic_slice_in_dim(cotangent, me * chunk, chunk, 1)

    (first, middle), (_, last) = BLOCKS
    count = middle - first
    wide = rows.astype(jnp.float32)
    down_low, down_high = products(True, BLOCKS)
    columns = [dot(rows, weight_in[s], ROWS) for s in range(first, middle)]
    columns += split_scalars([jnp.sum(wide * wide, axis=1, keepdims=True)])
    down = exchanged(columns, n_pipe)
    all_out, down_low, down = lax.optimization_barrier((all_out, down_low, down))
    weight_out = [all_out[:, s * chunk : (s + 1) * chunk] for s in range(n_pipe)]
    gram_in_low = over_dp(down_low)
    up_low, up_high = products(False, BLOCKS)
    gram_out_low = over_dp(up_low)
    columns = [dot(rows, weight_out[s], LAST) for s in range(first, middle - 1)]
    columns, up_low = lax.optimization_barrier((columns, up_low))
    up = exchanged(columns, n_pipe)
    columns = [dot(seed, weight_out[s], LAST) for s in range(middle, last)]
    columns, up = lax.optimization_barrier((columns, up))
    grad_high = exchanged(columns, n_pipe)
    columns = jnp.concatenate([down_high, up_high], axis=1)
    gram_in_low, gram_out_low, up, grad_high, columns = lax.optimization_barrier(
        (gram_in_low, gram_out_low, up, grad_high, columns)
    )
    gram_high = over_dp(columns)

    kept = len(kept_crosses(first, middle))
    acts, hidden, scale, cross = run(
        forward_kernel(first, middle, width, inner, n_pipe),
        [
            ((tok_rows, count * inner), jnp.bfloat16),
            ((count, block, inner), jnp.float32),
            ((count, block, LANES), jnp.float32),
            ((kept, block, inner), jnp.float32),
        ],
        down,
        up,
        gram_in_low,
        gram_out_low,
    )
    acts = swap(acts, "pipe")
    exact, columns = run(
        next_rows_kernel(first, middle, last, inner, chunk),
        [
            ((tok_rows, chunk), jnp.float32),
            ((tok_rows, (2 * (last - middle) - 1) * inner + LANES), jnp.bfloat16),
        ],
        rows,
        acts,
        all_in,
        all_out,
        specs={
            2: pl.BlockSpec(
                ((last - middle) * chunk, inner), lambda step: (middle // (last - middle), 0)
            )
        },
    )
    sums = exchanged(columns, n_pipe)

    turned = run(
        turning_kernel(middle, last, width, inner, n_pipe),
        [((tok_rows, 2 * (last - middle) * inner + LANES), jnp.bfloat16)],
        sums,
        grad_high,
        gram_high,
    )[0]
    turned = swap(turned, "pipe")

    def packed_shape(group, parts):
        return (parts, 2 * group * chunk * inner // (n_dp * LANES), LANES)

    dp = lax.axis_index("dp")
    core, chip = dp % 2, dp // 2
    chips = jnp.arange(n_dp // 2)
    xs = n_dp // 4
    away = (chips // 2 - chip // 2 + xs) % xs * 2 + (chips % 2 + chip % 2) % 2
    place = jnp.concatenate([away, core[None]]).astype(jnp.int32)

    grads_high, upstream, packed, columns = run(
        grads_kernel(
            middle, last, first, inner, chunk, n_dp, (last - middle) * inner + LANES, False
        ),
        [
            ((last - middle, tok_rows, chunk), jnp.bfloat16),
            ((tok_rows, chunk), jnp.float32),
            (packed_shape(last - middle, n_dp), jnp.bfloat16),
            ((tok_rows, count * inner), jnp.bfloat16),
        ],
        place,
        exact,
        turned,
        turned,
        seed,
        all_in,
        all_out,
        smem=True,
    )
    packed = packed.reshape(-1, LANES)
    packed = lax.psum_scatter(packed, "dp", scatter_dimension=0, tiled=True)
    grad_low = exchanged(columns, n_pipe)

    packs = run(
        backward_kernel(first, middle, width, inner, n_pipe),
        [((tok_rows, count * inner + LANES), jnp.bfloat16)],
        grad_low,
        hidden,
        scale,
        cross,
        gram_in_low,
    )[0]
    packs = swap(packs, "pipe")
    grads, _, mine, other = run(
        grads_kernel(first, middle, first, inner, chunk, n_dp, 0, True),
        [
            ((n_pipe, tok_rows, chunk), jnp.bfloat16),
            ((tok_rows, chunk), jnp.float32),
            (packed_shape(count, n_dp // 2), jnp.bfloat16),
            (packed_shape(count, n_dp // 2), jnp.bfloat16),
        ],
        place,
        rows,
        packs,
        acts,
        upstream,
        all_in,
        all_out,
        grads_high,
        smem=True,
    )

    def unpacked(arrived, group):
        share = group * chunk // n_dp
        rows_out = arrived[0].shape[-2] - share * inner // LANES
        sum_in, sum_out = run(
            unpack_kernel(inner, share, len(arrived)),
            [((share, inner), jnp.bfloat16), ((rows_out, LANES), jnp.bfloat16)],
            *arrived,
            vmem=VMEM_ALMOST_ALL,
        )
        return sum_in, sum_out.reshape(group, -1, LANES)

    blocks = added(mine, other_core(other, n_dp), mine.shape[0])
    arrived_low = between_chips(blocks, n_dp)
    input_grads = swap(grads, "pipe")
    input_grads, arrived_low = lax.optimization_barrier((input_grads, arrived_low))
    ins, outs = zip(unpacked(arrived_low, count), unpacked([packed], last - middle))
    grad_out = swap(jnp.concatenate(outs, axis=0), "pipe")
    grad_in = move_in(*ins, n_pipe, n_dp)
    is_high = (me >= middle).astype(jnp.int32).reshape(1)

    shape_in, shape_out = (share_in, inner), (share_out, width)
    *updated, pieces = run(
        adam_kernel(share_out, chunk // LANES, share_in),
        [(shape_in, jnp.float32)] * 3
        + [(shape_out, jnp.float32)] * 3
        + [((n_dp, 2, share_out, share_in), jnp.bfloat16)],
        is_high,
        *grad_in,
        grad_out,
        master_in[0],
        moment_in[0],
        second_in[0],
        master_out[0],
        moment_out[0],
        second_out[0],
        smem=True,
        vmem=VMEM_ALMOST_ALL,
    )
    new_in, new_moment_in, new_second_in, new_out, new_moment_out, new_second_out = updated
    input_grads = columns_in_place(input_grads)[None]
    roll_in, roll_out = run(
        rollout_kernel(share_out, share_in),
        [(shape_out, jnp.bfloat16), (shape_in, jnp.bfloat16)],
        swap(pieces, "dp"),
    )
    return (
        input_grads,
        new_in[None],
        new_moment_in[None],
        new_second_in[None],
        new_out[None],
        new_moment_out[None],
        new_second_out[None],
        roll_in[None],
        roll_out[None],
    )


def solution(mesh):
    in_specs = (P("dp", None), P("dp", None)) + (P("pipe", "dp", None),) * 6
    out_specs = (P("pipe", "dp", None),) * 9
    return jax.shard_map(
        on_device, mesh=mesh, in_specs=in_specs, out_specs=out_specs, check_vma=False
    )
```
